32 devices in a mesh: group: 8 (over z, core), dev: 4 (over y, x).
Axes of the slice: x: 2, y: 2, z: 4, core: 2. Of those that a mesh axis runs over, the one named last changes fastest.
Arguments:
- density: float32 [512, 3, 152], P(('group', 'dev')), may hold values from -6 to 6
- kernel_hat: bfloat16 [316, 2, 2304], replicated, may hold values from -6 to 6
- send_list: int32 [32, 4, 4], P(('group', 'dev')), may hold values from 0 to 15
- halo_list: int32 [32, 2, 4], P(('group', 'dev')), may hold values from 0 to 15
- inter_src: int32 [512, 32], P(('group', 'dev')), may hold values from 0 to 39, as said below
- inter_off: int32 [512, 32], P(('group', 'dev')), may hold values from 0 to 315
Outputs:
- potential: float32 [512, 3, 152], P(('group', 'dev'))
The draws below stay inside these ranges and needn't reach their ends.
Inputs may be any that keep to these rules, and one draw needn't show every extreme that they name: `inter_src`: never names an entry of an adjacent subtree that does not exist (the previous one of the first subtree, the next one of the last).
All inputs are finite; a program needn't handle non-finite values.
Results may differ from the reference program's by a relative error of at most 0.0029.
Values may be sent and summed in bfloat16 or wider, within the bound.
No kernel may reach another device: no remote copies, remote signals or barrier semaphores. Data moves between devices by JAX's collectives and lax.ppermute only.
A program may use at most 128 MiB of HBM per device.

```python
import jax
import jax.numpy as jnp
import numpy as np
from jax import lax

ORDER = 6
GRID = 16
COMP = 3
OFFSETS = 316
NB = 16
LIST = 32
SURF = 152
FREQ = 2304
CAP = 4
HB = 4
GROUPS = 8
PEERS = 4
BOXES = 512
SLOTS = 40


def draw_inter_src(key, part):
    key = jax.random.fold_in(key, 11)
    keys = jax.random.split(key, 7)
    devices = GROUPS * PEERS
    shape = (devices, NB, LIST)
    region = jax.random.randint(keys[0], shape, 0, 4)
    local_slot = jax.random.randint(keys[1], shape, 0, NB)
    peer_ids = jax.random.randint(keys[2], shape, 0, PEERS)
    counts = jax.random.randint(keys[3], (devices, PEERS), CAP // 2, CAP + 1)
    counts = counts.at[:, 0].set(CAP)
    peer_count = jnp.take_along_axis(counts, peer_ids.reshape(devices, NB * LIST), axis=1).reshape(shape)
    peer_slot = jax.random.randint(keys[4], shape, 0, 65536) % jnp.maximum(peer_count, 1)
    halo_side = jax.random.randint(keys[5], shape, 0, 2)
    group_ids = (jnp.arange(devices, dtype=jnp.int32) // PEERS)[:, None, None]
    halo_side = jnp.where(group_ids == 0, 1, jnp.where(group_ids == GROUPS - 1, 0, halo_side))
    halo_slot = NB + PEERS * CAP + halo_side * HB + jax.random.randint(keys[6], shape, 0, HB)
    chosen = jnp.where(region == 0, local_slot, jnp.where(region == 3, halo_slot, NB + peer_ids * CAP + peer_slot))
    chosen = chosen.at[0, 0, 0].set(SLOTS - 1)
    chosen = chosen.at[0, 0, 1].set(0)
    return chosen.reshape(devices * NB, LIST).astype(jnp.int32)


def touch_ends(entries, key, low, top_value):
    shape = entries.shape
    place = [jax.random.randint(jax.random.fold_in(key, axis), (), 0, shape[axis]) for axis in range(len(shape))]
    entries = entries.at[tuple(place)].set(low)
    longest = shape.index(max(shape))
    place[longest] = (place[longest] + 1) % shape[longest]
    return entries.at[tuple(place)].set(top_value)


def level_of(stream_key, dims, pieces, low, largest):
    factor_of, own = 1.0, jax.random.fold_in(stream_key, 6)
    for axis_at, blocks in pieces:
        steps = jnp.exp(jax.random.uniform(jax.random.fold_in(own, axis_at), (blocks,), jnp.float32, low / len(pieces), largest / len(pieces)))
        factor_of = factor_of * jnp.repeat(steps, dims[axis_at] // blocks).reshape([-1 if axis == axis_at else 1 for axis in range(len(dims))])
    return factor_of


def normal_values(stream_key, extent, width, reach, shards=(), held_as=jnp.bfloat16):
    drawn = jax.random.normal(stream_key, extent, jnp.float32) * width
    if len(shards) > 0:
        drawn = level_of(stream_key, extent, shards, -0.22, 0.18) * drawn
    return jnp.clip(drawn, min=-reach, max=reach).astype(held_as)


def setup_inputs(seed: int = 0) -> dict:
    seeds = jax.random.split(jax.random.key(seed), 7)
    density = normal_values(seeds[0], (BOXES, COMP, SURF), 1.0, 6.0, ((0, 32),), jnp.float32)
    kernel_hat = normal_values(seeds[1], (OFFSETS, 2, FREQ), 1.0, 6.0)
    send_list = touch_ends(jax.random.randint(seeds[2], (GROUPS * PEERS, PEERS, CAP), 0, NB), jax.random.fold_in(seeds[2], 1), 0, NB - 1).astype(jnp.int32)
    halo_list = touch_ends(jax.random.randint(seeds[3], (GROUPS * PEERS, 2, HB), 0, NB), jax.random.fold_in(seeds[3], 1), 0, NB - 1).astype(jnp.int32)
    inter_src = draw_inter_src(jax.random.fold_in(seeds[6], 71), 0)
    inter_off = touch_ends(jax.random.randint(seeds[5], (BOXES, LIST), 0, OFFSETS), jax.random.fold_in(seeds[5], 1), 0, OFFSETS - 1).astype(jnp.int32)
    return dict(density=density, kernel_hat=kernel_hat, send_list=send_list, halo_list=halo_list, inter_src=inter_src, inter_off=inter_off)


def surface_points(edge_count):
    points = [(i, j, k) for i in range(edge_count) for j in range(edge_count) for k in range(edge_count)
              if min(i, j, k) == 0 or max(i, j, k) == edge_count - 1]
    return np.array(points, dtype=np.int32)


def reference(density, kernel_hat, send_list, halo_list, inter_src, inter_off):
    points = surface_points(ORDER)
    coord_x = points[:, 0]
    coord_y = points[:, 1]
    coord_z = points[:, 2]
    devices = GROUPS * PEERS
    check_shift = GRID // 2

    def spectrum_block(rows_block):
        count = rows_block.shape[0]
        field = jnp.zeros((count, COMP, GRID, GRID, GRID), jnp.float32)
        field = field.at[:, :, coord_x, coord_y, coord_z].set(rows_block)
        transformed = jnp.fft.rfftn(field, axes=(2, 3, 4)).reshape(count, COMP, FREQ)
        stacked = jnp.stack([jnp.real(transformed), jnp.imag(transformed)], axis=1)
        return stacked.astype(jnp.float32).astype(jnp.bfloat16)

    spectra = lax.map(spectrum_block, density.reshape(devices, NB, COMP, SURF))
    spectra = spectra.reshape(BOXES, 2, COMP, FREQ)

    dev_ids = jnp.arange(devices, dtype=jnp.int32)
    local_ids = dev_ids[:, None] * NB + jnp.arange(NB, dtype=jnp.int32)[None, :]
    group_ids = dev_ids // PEERS
    member = dev_ids % PEERS
    senders = group_ids[:, None] * PEERS + jnp.arange(PEERS, dtype=jnp.int32)[None, :]
    send_lists = send_list.reshape(devices, PEERS, CAP)
    peer_ids = senders[:, :, None] * NB + send_lists[senders, member[:, None], :]
    halo_rows = halo_list.reshape(devices, 2, HB)
    previous = jnp.clip(dev_ids - PEERS, 0, devices - 1).astype(jnp.int32)
    following = jnp.clip(dev_ids + PEERS, 0, devices - 1).astype(jnp.int32)
    prev_ids = previous[:, None] * NB + halo_rows[previous, 1]
    next_ids = following[:, None] * NB + halo_rows[following, 0]
    source_table = jnp.concatenate([local_ids, peer_ids.reshape(devices, PEERS * CAP), prev_ids, next_ids], axis=1).astype(jnp.int32)
    sources = jnp.take_along_axis(source_table, inter_src.reshape(devices, NB * LIST), axis=1)
    sources = sources.reshape(devices, NB, LIST).astype(jnp.int32)
    offsets = inter_off.reshape(devices, NB, LIST)

    def apply_block(operands):
        source_ids, offset_ids = operands
        gathered = spectra[source_ids].astype(jnp.float32)
        kernel_rows = kernel_hat[offset_ids].astype(jnp.float32)
        kernel_re = kernel_rows[:, :, 0][:, :, None, :]
        kernel_im = kernel_rows[:, :, 1][:, :, None, :]
        source_re = gathered[:, :, 0]
        source_im = gathered[:, :, 1]
        real_part = jnp.sum(kernel_re * source_re - kernel_im * source_im, axis=1)
        imag_part = jnp.sum(kernel_re * source_im + kernel_im * source_re, axis=1)
        complex_hat = lax.complex(real_part, imag_part).reshape(NB, COMP, GRID, GRID, GRID // 2 + 1)
        field = jnp.fft.irfftn(complex_hat, s=(GRID, GRID, GRID), axes=(2, 3, 4))
        return field[:, :, coord_x + check_shift, coord_y + check_shift, coord_z + check_shift].astype(jnp.float32)

    result = lax.map(apply_block, (sources, offsets))
    return result.reshape(BOXES, COMP, SURF)
```

```python
import functools
import math

import jax
import jax.numpy as jnp
import ml_dtypes
import numpy as np
from jax import lax
from jax.experimental import pallas as pl
from jax.experimental.pallas import tpu as pltpu
from jax.sharding import PartitionSpec as P

ORDER = 6
GRID = 16
LANES = 128
HALF = GRID // 2 + 1
FREQ = GRID * GRID * HALF
TILES = FREQ // LANES
MAIN = 16
TAIL = TILES - MAIN
PITCH = MAIN + 1
TAIL_PITCH = 7
POINTS_PAD = 160
CHUNK = 256


def surface_points(edge_count):
    points = [
        (i, j, k)
        for i in range(edge_count)
        for j in range(edge_count)
        for k in range(edge_count)
        if min(i, j, k) == 0 or max(i, j, k) == edge_count - 1
    ]
    return np.array(points, dtype=np.int64)


@functools.lru_cache(maxsize=None)
def transform_tables():
    points = surface_points(ORDER)
    kx, ky, kz = (a.reshape(-1) for a in np.meshgrid(np.arange(GRID), np.arange(GRID), np.arange(HALF), indexing="ij"))
    phase = (points[:, :1] * kx + points[:, 1:2] * ky + points[:, 2:] * kz) % GRID
    angle = phase * (2.0 * math.pi / GRID)
    table = np.zeros((POINTS_PAD, 2 * FREQ), np.float64)
    table[: len(points), :FREQ] = np.cos(angle)
    table[: len(points), FREQ:] = -np.sin(angle)
    table = np.where(np.abs(table) < 1e-9, 0.0, table)
    high = table.astype(ml_dtypes.bfloat16)
    low = (table - high.astype(np.float64)).astype(ml_dtypes.bfloat16)
    edge_plane = (kz == 0) | (kz == GRID // 2)
    factor = np.where(edge_plane, 1.0, 2.0) / GRID**3 * np.where((kx + ky + kz) % 2 == 0, 1.0, -1.0)
    factor = np.concatenate([factor, factor]).astype(np.float32)[None, :]
    return np.concatenate([high, low], axis=0), factor


def pack_kernel(density, send_list, halo_list, to_peers, to_prev, to_next):
    comp_count = density.shape[0]
    peers, cap = send_list.shape
    rim = halo_list.shape[1]
    for c in range(comp_count):
        for e in range(cap):
            for q in range(peers):
                to_peers[q, c, pl.ds(e, 1), :] = density[c, pl.ds(send_list[q, e], 1), :]
        for e in range(rim):
            to_prev[c, pl.ds(e, 1), :] = density[c, pl.ds(halo_list[0, e], 1), :]
            to_next[c, pl.ds(e, 1), :] = density[c, pl.ds(halo_list[1, e], 1), :]


def translate_kernel(
    source, offset, density, peers_in, before, after, table, factor, kernel_hat, out,
    rows, hat, main, tail, total, total_tail,
):
    comp_count, box_count, surf = density.shape
    list_count = source.shape[1]
    peers, _, cap, _ = peers_in.shape
    rim = before.shape[1]
    slots = rows.shape[0] // comp_count
    row_count = rows.shape[0]
    f32, bf16 = jnp.float32, jnp.bfloat16

    rows[...] = jnp.zeros_like(rows)
    for c in range(comp_count):
        base = c * slots
        rows[base : base + box_count, :surf] = density[c]
        base += box_count
        for q in range(peers):
            rows[base + q * cap : base + (q + 1) * cap, :surf] = peers_in[q, c]
        base += peers * cap
        rows[base : base + rim, :surf] = before[c]
        rows[base + rim : base + 2 * rim, :surf] = after[c]

    step = 144
    @pl.loop(0, hat.shape[0] // step)
    def _(i):
        at = pl.ds(pl.multiple_of(i * step, 16), step)
        hat[at, :] = kernel_hat[at, :].astype(f32)

    value = rows[...]
    high = value.astype(bf16)
    low = (value - high.astype(f32)).astype(bf16)
    for part in range(2):
        for n in range(FREQ // CHUNK):
            columns = slice(part * FREQ + n * CHUNK, part * FREQ + (n + 1) * CHUNK)
            t_high = table[:POINTS_PAD, columns]
            t_low = table[POINTS_PAD:, columns]
            x = jnp.dot(high, t_high, preferred_element_type=f32)
            x = x + jnp.dot(low, t_high, preferred_element_type=f32)
            x = x + jnp.dot(high, t_low, preferred_element_type=f32)
            x = x.astype(bf16).astype(f32)
            for m in range(CHUNK // LANES):
                j = n * (CHUNK // LANES) + m
                for g in range(row_count // 8):
                    piece = x[g * 8 : (g + 1) * 8, m * LANES : (m + 1) * LANES]
                    if j < MAIN:
                        main[pl.ds((part * row_count + g * 8) * PITCH + j, 8, stride=PITCH), :] = piece
                    else:
                        c, s = divmod(g * 8, slots)
                        tail[j - MAIN, pl.ds(s * TAIL_PITCH + part * comp_count + c, 8, stride=TAIL_PITCH), :] = piece

    plus = lax.broadcasted_iota(jnp.int32, (8, LANES), 0) < comp_count
    halves = MAIN // 8

    @pl.loop(0, box_count)
    def _(t):
        def pair(w, accs):
            s = source[t, w]
            o = offset[t, w] * (2 * TILES)
            k = [
                [hat[pl.ds(o + 16 * h + r, 8, stride=2), :] for h in range(halves)] for r in range(2)
            ]
            accs = list(accs)
            at = 0
            for c in range(comp_count):
                for h in range(halves):
                    s_re = main[pl.ds((c * slots + s) * PITCH + 8 * h, 8), :]
                    s_im = main[pl.ds((row_count + c * slots + s) * PITCH + 8 * h, 8), :]
                    accs[at] = accs[at] + (k[0][h] * s_re - k[1][h] * s_im)
                    accs[at + 1] = accs[at + 1] + (k[0][h] * s_im + k[1][h] * s_re)
                    at += 2
            for j in range(TAIL):
                x = tail[j, pl.ds(s * TAIL_PITCH, 8), :]
                k_re = hat[pl.ds(o + 2 * (MAIN + j), 8, stride=0), :]
                k_im = hat[pl.ds(o + 2 * (MAIN + j) + 1, 8, stride=0), :]
                accs[at] = accs[at] + k_re * x
                accs[at + 1] = accs[at + 1] + k_im * x
                at += 2
            return tuple(accs)

        count = 2 * (comp_count * halves + TAIL)
        zero = jnp.zeros((8, LANES), f32)
        accs = lax.fori_loop(0, list_count, pair, (zero,) * count, unroll=4)
        at = 0
        for c in range(comp_count):
            for h in range(halves):
                for part in range(2):
                    row = (part * comp_count + c) * box_count + t
                    total[pl.ds(row * PITCH + 8 * h, 8), :] = accs[at + part]
                at += 2
        for j in range(TAIL):
            own, cross = accs[at], accs[at + 1]
            up = jnp.concatenate([cross[comp_count:], cross[:comp_count]], axis=0)
            down = jnp.concatenate([cross[-comp_count:], cross[:-comp_count]], axis=0)
            total_tail[j, pl.ds(t * TAIL_PITCH, 8), :] = jnp.where(plus, own - up, own + down)
            at += 2

    result = jnp.zeros((comp_count * box_count, 2 * POINTS_PAD), f32)
    rest = jnp.zeros((comp_count * box_count, POINTS_PAD), f32)
    groups = box_count // 8
    nt = (((1,), (1,)), ((), ()))
    for part in range(2):
        for n in range(FREQ // CHUNK):
            columns = slice(part * FREQ + n * CHUNK, part * FREQ + (n + 1) * CHUNK)
            lanes = []
            for m in range(CHUNK // LANES):
                j = n * (CHUNK // LANES) + m
                pieces = []
                for c in range(comp_count):
                    for g in range(groups):
                        if j < MAIN:
                            row = (part * comp_count + c) * box_count + g * 8
                            pieces.append(total[pl.ds(row * PITCH + j, 8, stride=PITCH), :])
                        else:
                            row = g * 8 * TAIL_PITCH + part * comp_count + c
                            pieces.append(total_tail[j - MAIN, pl.ds(row, 8, stride=TAIL_PITCH), :])
                lanes.append(jnp.concatenate(pieces, axis=0))
            x = jnp.concatenate(lanes, axis=1) * factor[:, columns]
            high = x.astype(bf16)
            low = (x - high.astype(f32)).astype(bf16)
            result += lax.dot_general(high, table[:, columns], nt, preferred_element_type=f32)
            rest += lax.dot_general(low, table[:POINTS_PAD, columns], nt, preferred_element_type=f32)
    result = result[:, :POINTS_PAD] + result[:, POINTS_PAD:] + rest
    for c in range(comp_count):
        out[c] = result[c * box_count : (c + 1) * box_count, :surf]


def on_device(density, kernel_hat, send_list, halo_list, inter_src, inter_off):
    table, factor = transform_tables()
    box_count, comp_count, surf = density.shape
    _, peers, cap = send_list.shape
    rim = halo_list.shape[2]
    f32 = jnp.float32
    vmem = pl.BlockSpec(memory_space=pltpu.VMEM)
    smem = pl.BlockSpec(memory_space=pltpu.SMEM)
    density = density.transpose(1, 0, 2)

    to_peers, to_prev, to_next = pl.pallas_call(
        pack_kernel,
        out_shape=(
            jax.ShapeDtypeStruct((peers, comp_count, cap, surf), f32),
            jax.ShapeDtypeStruct((comp_count, rim, surf), f32),
            jax.ShapeDtypeStruct((comp_count, rim, surf), f32),
        ),
        in_specs=[vmem, smem, smem],
        out_specs=(vmem, vmem, vmem),
        name="pack",
    )(density, send_list[0], halo_list[0])

    groups = lax.axis_size("group")
    forward = [(i, i + 1) for i in range(groups - 1)]
    backward = [(i + 1, i) for i in range(groups - 1)]
    before = lax.ppermute(to_next, "group", forward)
    after = lax.ppermute(to_prev, "group", backward)
    arrived = lax.all_to_all(to_peers, "dev", split_axis=0, concat_axis=0, tiled=True)

    offsets = kernel_hat.shape[0]
    hat = kernel_hat.reshape(offsets, 2, TILES, LANES).transpose(0, 2, 1, 3).reshape(-1, LANES)

    slots = box_count + peers * cap + 2 * rim
    row_count = comp_count * slots
    potential = pl.pallas_call(
        translate_kernel,
        out_shape=jax.ShapeDtypeStruct((comp_count, box_count, surf), f32),
        in_specs=[smem, smem] + [vmem] * 7,
        out_specs=vmem,
        scratch_shapes=[
            pltpu.VMEM((row_count, POINTS_PAD), f32),
            pltpu.VMEM(hat.shape, f32),
            pltpu.VMEM((2 * row_count * PITCH, LANES), f32),
            pltpu.VMEM((TAIL, (slots + 2) * TAIL_PITCH, LANES), f32),
            pltpu.VMEM((2 * comp_count * box_count * PITCH, LANES), f32),
            pltpu.VMEM((TAIL, (box_count + 2) * TAIL_PITCH, LANES), f32),
        ],
        compiler_params=pltpu.CompilerParams(vmem_limit_bytes=40 * 1024 * 1024),
        name="translate",
    )(inter_src, inter_off, density, arrived, before, after, jnp.asarray(table), jnp.asarray(factor), hat)
    return potential.transpose(1, 0, 2)


def solution(mesh):
    in_specs = (
        P(("group", "dev"), None, None),
        P(),
        P(("group", "dev"), None, None),
        P(("group", "dev"), None, None),
        P(("group", "dev"), None),
        P(("group", "dev"), None),
    )
    out_specs = P(("group", "dev"), None, None)
    return jax.shard_map(
        on_device, mesh=mesh, in_specs=in_specs, out_specs=out_specs, check_vma=False
    )
```

```python
import functools
import math

import jax
import jax.numpy as jnp
import ml_dtypes
import numpy as np
from jax import lax
from jax.experimental import pallas as pl
from jax.experimental.pallas import tpu as pltpu
from jax.sharding import PartitionSpec as P

ORDER = 6
GRID = 16
LANES = 128
HALF = GRID // 2 + 1
FREQ = GRID * GRID * HALF
TILES = FREQ // LANES
MAIN = 16
TAIL = TILES - MAIN
PITCH = MAIN + 1
TAIL_PITCH = 7
POINTS_PAD = 160
CHUNK = 256


def surface_points(edge_count):
    points = [
        (i, j, k)
        for i in range(edge_count)
        for j in range(edge_count)
        for k in range(edge_count)
        if min(i, j, k) == 0 or max(i, j, k) == edge_count - 1
    ]
    return np.array(points, dtype=np.int64)


@functools.lru_cache(maxsize=None)
def transform_tables():
    points = surface_points(ORDER)
    kx, ky, kz = (a.reshape(-1) for a in np.meshgrid(np.arange(GRID), np.arange(GRID), np.arange(HALF), indexing="ij"))
    phase = (points[:, :1] * kx + points[:, 1:2] * ky + points[:, 2:] * kz) % GRID
    angle = phase * (2.0 * math.pi / GRID)
    table = np.zeros((POINTS_PAD, 2 * FREQ), np.float64)
    table[: len(points), :FREQ] = np.cos(angle)
    table[: len(points), FREQ:] = -np.sin(angle)
    table = np.where(np.abs(table) < 1e-9, 0.0, table)
    high = table.astype(ml_dtypes.bfloat16)
    low = (table - high.astype(np.float64)).astype(ml_dtypes.bfloat16)
    edge_plane = (kz == 0) | (kz == GRID // 2)
    factor = np.where(edge_plane, 1.0, 2.0) / GRID**3 * np.where((kx + ky + kz) % 2 == 0, 1.0, -1.0)
    factor = np.concatenate([factor, factor]).astype(np.float32)[None, :]
    return np.concatenate([high, low], axis=0), factor


def pack_kernel(density, send_list, halo_list, to_peers, to_sides):
    comp_count = density.shape[0]
    peers, cap = send_list.shape
    rim = halo_list.shape[1]
    for c in range(comp_count):
        for e in range(cap):
            for q in range(peers):
                to_peers[q, c, pl.ds(e, 1), :] = density[c, pl.ds(send_list[q, e], 1), :]
        for e in range(rim):
            for side in range(2):
                to_sides[side, c, pl.ds(e, 1), :] = density[c, pl.ds(halo_list[side, e], 1), :]


def prepare_kernel(kernel_hat, hat, hat_tail):
    parts, count, _ = kernel_hat.shape
    padded = hat_tail.shape[0] // (parts * TAIL)

    def move(first, height):
        for part in range(parts):
            for j in range(TILES):
                x = kernel_hat[part, pl.ds(first, height), j * LANES : (j + 1) * LANES].astype(jnp.float32)
                for g in range(0, height, 8):
                    size = min(8, height - g)
                    piece = x[g : g + size]
                    if j < MAIN:
                        row = (part * padded + first + g) * PITCH + j
                        hat[pl.ds(row, size, stride=PITCH), :] = piece
                    else:
                        row = (part * TAIL + j - MAIN) * padded + first + g
                        hat_tail[pl.ds(row, size), :] = piece

    whole = count // 16

    @pl.loop(0, whole)
    def _(i):
        move(pl.multiple_of(i * 16, 16), 16)

    if count % 16:
        move(whole * 16, count % 16)


def translate_kernel(
    place, source, offset, density, peers_in, halos_in, table, factor, hat, hat_tail, out,
    rows, main, tail, total, total_tail,
):
    comp_count, box_count, surf = density.shape
    list_count = source.shape[1]
    peers, _, _, cap, _ = peers_in.shape
    rim = halos_in.shape[3]
    padded = hat_tail.shape[0] // (2 * TAIL)
    member, previous, following = place[0], place[1], place[2]
    slots = rows.shape[0] // comp_count
    row_count = rows.shape[0]
    f32, bf16 = jnp.float32, jnp.bfloat16

    rows[...] = jnp.zeros_like(rows)
    for c in range(comp_count):
        base = c * slots
        rows[base : base + box_count, :surf] = density[c]
        base += box_count
        for q in range(peers):
            rows[base + q * cap : base + (q + 1) * cap, :surf] = peers_in[q, member, c]
        base += peers * cap
        rows[base : base + rim, :surf] = halos_in[previous, 1, c]
        rows[base + rim : base + 2 * rim, :surf] = halos_in[following, 0, c]

    value = rows[...]
    high = value.astype(bf16)
    low = (value - high.astype(f32)).astype(bf16)
    for part in range(2):
        for n in range(FREQ // CHUNK):
            columns = slice(part * FREQ + n * CHUNK, part * FREQ + (n + 1) * CHUNK)
            t_high = table[:POINTS_PAD, columns]
            t_low = table[POINTS_PAD:, columns]
            x = jnp.dot(high, t_high, preferred_element_type=f32)
            x = x + jnp.dot(low, t_high, preferred_element_type=f32)
            x = x + jnp.dot(high, t_low, preferred_element_type=f32)
            x = x.astype(bf16).astype(f32)
            for m in range(CHUNK // LANES):
                j = n * (CHUNK // LANES) + m
                for g in range(row_count // 8):
                    piece = x[g * 8 : (g + 1) * 8, m * LANES : (m + 1) * LANES]
                    if j < MAIN:
                        main[pl.ds((part * row_count + g * 8) * PITCH + j, 8, stride=PITCH), :] = piece
                    else:
                        c, s = divmod(g * 8, slots)
                        tail[j - MAIN, pl.ds(s * TAIL_PITCH + part * comp_count + c, 8, stride=TAIL_PITCH), :] = piece

    plus = lax.broadcasted_iota(jnp.int32, (8, LANES), 0) < comp_count
    halves = MAIN // 8

    @pl.loop(0, box_count)
    def _(t):
        def pair(w, accs):
            s = source[t, w]
            o = offset[t, w]
            k = [
                [hat[pl.ds((r * padded + o) * PITCH + 8 * h, 8), :] for h in range(halves)] for r in range(2)
            ]
            accs = list(accs)
            at = 0
            for c in range(comp_count):
                for h in range(halves):
                    s_re = main[pl.ds((c * slots + s) * PITCH + 8 * h, 8), :]
                    s_im = main[pl.ds((row_count + c * slots + s) * PITCH + 8 * h, 8), :]
                    accs[at] = accs[at] + (k[0][h] * s_re - k[1][h] * s_im)
                    accs[at + 1] = accs[at + 1] + (k[0][h] * s_im + k[1][h] * s_re)
                    at += 2
            for j in range(TAIL):
                x = tail[j, pl.ds(s * TAIL_PITCH, 8), :]
                k_re = hat_tail[pl.ds(j * padded + o, 8, stride=0), :]
                k_im = hat_tail[pl.ds((TAIL + j) * padded + o, 8, stride=0), :]
                accs[at] = accs[at] + k_re * x
                accs[at + 1] = accs[at + 1] + k_im * x
                at += 2
            return tuple(accs)

        count = 2 * (comp_count * halves + TAIL)
        zero = jnp.zeros((8, LANES), f32)
        accs = lax.fori_loop(0, list_count, pair, (zero,) * count, unroll=4)
        at = 0
        for c in range(comp_count):
            for h in range(halves):
                for part in range(2):
                    row = (part * comp_count + c) * box_count + t
                    total[pl.ds(row * PITCH + 8 * h, 8), :] = accs[at + part]
                at += 2
        for j in range(TAIL):
            own, cross = accs[at], accs[at + 1]
            up = jnp.concatenate([cross[comp_count:], cross[:comp_count]], axis=0)
            down = jnp.concatenate([cross[-comp_count:], cross[:-comp_count]], axis=0)
            total_tail[j, pl.ds(t * TAIL_PITCH, 8), :] = jnp.where(plus, own - up, own + down)
            at += 2

    result = jnp.zeros((comp_count * box_count, 2 * POINTS_PAD), f32)
    rest = jnp.zeros((comp_count * box_count, POINTS_PAD), f32)
    groups = box_count // 8
    nt = (((1,), (1,)), ((), ()))
    for part in range(2):
        for n in range(FREQ // CHUNK):
            columns = slice(part * FREQ + n * CHUNK, part * FREQ + (n + 1) * CHUNK)
            lanes = []
            for m in range(CHUNK // LANES):
                j = n * (CHUNK // LANES) + m
                pieces = []
                for c in range(comp_count):
                    for g in range(groups):
                        if j < MAIN:
                            row = (part * comp_count + c) * box_count + g * 8
                            pieces.append(total[pl.ds(row * PITCH + j, 8, stride=PITCH), :])
                        else:
                            row = g * 8 * TAIL_PITCH + part * comp_count + c
                            pieces.append(total_tail[j - MAIN, pl.ds(row, 8, stride=TAIL_PITCH), :])
                lanes.append(jnp.concatenate(pieces, axis=0))
            x = jnp.concatenate(lanes, axis=1) * factor[:, columns]
            high = x.astype(bf16)
            low = (x - high.astype(f32)).astype(bf16)
            result += lax.dot_general(high, table[:, columns], nt, preferred_element_type=f32)
            rest += lax.dot_general(low, table[:POINTS_PAD, columns], nt, preferred_element_type=f32)
    result = result[:, :POINTS_PAD] + result[:, POINTS_PAD:] + rest
    for c in range(comp_count):
        out[c] = result[c * box_count : (c + 1) * box_count, :surf]


def on_device(density, kernel_hat, send_list, halo_list, inter_src, inter_off):
    table, factor = transform_tables()
    box_count, comp_count, surf = density.shape
    _, peers, cap = send_list.shape
    rim = halo_list.shape[2]
    f32 = jnp.float32
    vmem = pl.BlockSpec(memory_space=pltpu.VMEM)
    smem = pl.BlockSpec(memory_space=pltpu.SMEM)
    density = density.transpose(1, 0, 2)

    to_peers, to_sides = pl.pallas_call(
        pack_kernel,
        out_shape=(
            jax.ShapeDtypeStruct((peers, comp_count, cap, surf), f32),
            jax.ShapeDtypeStruct((2, comp_count, rim, surf), f32),
        ),
        in_specs=[vmem, smem, smem],
        out_specs=(vmem, vmem),
        name="pack",
    )(density, send_list[0], halo_list[0])
    from_peers = lax.all_gather(to_peers, "dev")
    from_sides = lax.all_gather(to_sides, "group")

    offsets = kernel_hat.shape[0]
    padded = -(-offsets // 8) * 8
    hat_rows = (2 * padded * PITCH, 2 * TAIL * padded)
    hat, hat_tail = pl.pallas_call(
        prepare_kernel,
        out_shape=tuple(jax.ShapeDtypeStruct((n, LANES), f32) for n in hat_rows),
        in_specs=[vmem],
        out_specs=(vmem, vmem),
        compiler_params=pltpu.CompilerParams(vmem_limit_bytes=16 * 1024 * 1024),
        cost_estimate=pl.CostEstimate(flops=kernel_hat.size, bytes_accessed=6 * kernel_hat.size, transcendentals=0),
        name="prepare",
    )(kernel_hat.transpose(1, 0, 2))

    group, groups = lax.axis_index("group"), lax.axis_size("group")
    place = jnp.stack([
        lax.axis_index("dev"), jnp.maximum(group - 1, 0), jnp.minimum(group + 1, groups - 1)
    ]).astype(jnp.int32)

    slots = box_count + peers * cap + 2 * rim
    row_count = comp_count * slots
    potential = pl.pallas_call(
        translate_kernel,
        out_shape=jax.ShapeDtypeStruct((comp_count, box_count, surf), f32),
        in_specs=[smem, smem, smem] + [vmem] * 7,
        out_specs=vmem,
        scratch_shapes=[
            pltpu.VMEM((row_count, POINTS_PAD), f32),
            pltpu.VMEM((2 * row_count * PITCH, LANES), f32),
            pltpu.VMEM((TAIL, (slots + 2) * TAIL_PITCH, LANES), f32),
            pltpu.VMEM((2 * comp_count * box_count * PITCH, LANES), f32),
            pltpu.VMEM((TAIL, (box_count + 2) * TAIL_PITCH, LANES), f32),
        ],
        compiler_params=pltpu.CompilerParams(vmem_limit_bytes=24 * 1024 * 1024),
        name="translate",
    )(
        place, inter_src, inter_off, density, from_peers, from_sides,
        jnp.asarray(table), jnp.asarray(factor), hat, hat_tail,
    )
    return potential.transpose(1, 0, 2)


def solution(mesh):
    in_specs = (
        P(("group", "dev"), None, None),
        P(),
        P(("group", "dev"), None, None),
        P(("group", "dev"), None, None),
        P(("group", "dev"), None),
        P(("group", "dev"), None),
    )
    out_specs = P(("group", "dev"), None, None)
    return jax.shard_map(
        on_device, mesh=mesh, in_specs=in_specs, out_specs=out_specs, check_vma=False
    )
```

```python
import functools
import math

import jax
import jax.numpy as jnp
import ml_dtypes
import numpy as np
from jax import lax
from jax.experimental import pallas as pl
from jax.experimental.pallas import tpu as pltpu
from jax.sharding import PartitionSpec as P

ORDER = 6
GRID = 16
LANES = 128
HALF = GRID // 2 + 1
FREQ = GRID * GRID * HALF
TILES = FREQ // LANES
MAIN = 16
TAIL = TILES - MAIN
PITCH = MAIN + 1
TAIL_PITCH = 7
POINTS_PAD = 160
CHUNK = 256


def surface_points(edge_count):
    points = [
        (i, j, k)
        for i in range(edge_count)
        for j in range(edge_count)
        for k in range(edge_count)
        if min(i, j, k) == 0 or max(i, j, k) == edge_count - 1
    ]
    return np.array(points, dtype=np.int64)


@functools.lru_cache(maxsize=None)
def transform_tables():
    points = surface_points(ORDER)
    kx, ky, kz = (a.reshape(-1) for a in np.meshgrid(np.arange(GRID), np.arange(GRID), np.arange(HALF), indexing="ij"))
    phase = (points[:, :1] * kx + points[:, 1:2] * ky + points[:, 2:] * kz) % GRID
    angle = phase * (2.0 * math.pi / GRID)
    table = np.zeros((POINTS_PAD, 2 * FREQ), np.float64)
    table[: len(points), :FREQ] = np.cos(angle)
    table[: len(points), FREQ:] = -np.sin(angle)
    table = np.where(np.abs(table) < 1e-9, 0.0, table)
    high = table.astype(ml_dtypes.bfloat16)
    low = (table - high.astype(np.float64)).astype(ml_dtypes.bfloat16)
    edge_plane = (kz == 0) | (kz == GRID // 2)
    factor = np.where(edge_plane, 1.0, 2.0) / GRID**3 * np.where((kx + ky + kz) % 2 == 0, 1.0, -1.0)
    factor = np.concatenate([factor, factor]).astype(np.float32)[None, :]
    return np.concatenate([high, low], axis=0), factor


def pack_kernel(place, density, send_list, halo_list, *outs):
    peers, cap = send_list.shape
    rim = halo_list.shape[1]
    for c in range(density.shape[0]):
        for k in range(peers):
            for e in range(cap):
                outs[k][c, e : e + 1, :] = density[c, pl.ds(send_list[place[k], e], 1), :]
        for side in range(2):
            for e in range(rim):
                outs[peers + side][c, e : e + 1, :] = density[c, pl.ds(halo_list[side, e], 1), :]


def prepare_kernel(kernel_hat, hat, hat_tail):
    parts, count, _ = kernel_hat.shape
    padded = hat_tail.shape[0] // (parts * TAIL)

    def move(first, height):
        for part in range(parts):
            for j in range(TILES):
                x = kernel_hat[part, pl.ds(first, height), j * LANES : (j + 1) * LANES].astype(jnp.float32)
                for g in range(0, height, 8):
                    size = min(8, height - g)
                    piece = x[g : g + size]
                    if j < MAIN:
                        row = (part * padded + first + g) * PITCH + j
                        hat[pl.ds(row, size, stride=PITCH), :] = piece
                    else:
                        row = (part * TAIL + j - MAIN) * padded + first + g
                        hat_tail[pl.ds(row, size), :] = piece

    whole = count // 16

    @pl.loop(0, whole)
    def _(i):
        move(pl.multiple_of(i * 16, 16), 16)

    if count % 16:
        move(whole * 16, count % 16)


def forward_kernel(place, density, *refs):
    *pieces, before, after, table, main, tail, rows = refs
    comp_count, box_count, surf = density.shape
    cap = pieces[0].shape[1]
    rim = before.shape[1]
    row_count = rows.shape[0]
    slots = row_count // comp_count
    f32, bf16 = jnp.float32, jnp.bfloat16

    rows[...] = jnp.zeros_like(rows)
    for c in range(comp_count):
        base = c * slots
        rows[base : base + box_count, :surf] = density[c]
        base += box_count
        for k, piece in enumerate(pieces):
            for e in range(cap):
                rows[pl.ds(base + place[k] * cap + e, 1), :surf] = piece[c, e : e + 1]
        base += len(pieces) * cap
        rows[base : base + rim, :surf] = before[c]
        rows[base + rim : base + 2 * rim, :surf] = after[c]

    value = rows[...]
    high = value.astype(bf16)
    low = (value - high.astype(f32)).astype(bf16)
    for part in range(2):
        for n in range(FREQ // CHUNK):
            columns = slice(part * FREQ + n * CHUNK, part * FREQ + (n + 1) * CHUNK)
            t_high = table[:POINTS_PAD, columns]
            t_low = table[POINTS_PAD:, columns]
            x = jnp.dot(high, t_high, preferred_element_type=f32)
            x = x + jnp.dot(low, t_high, preferred_element_type=f32)
            x = x + jnp.dot(high, t_low, preferred_element_type=f32)
            x = x.astype(bf16).astype(f32)
            for m in range(CHUNK // LANES):
                j = n * (CHUNK // LANES) + m
                for g in range(row_count // 8):
                    piece = x[g * 8 : (g + 1) * 8, m * LANES : (m + 1) * LANES]
                    if j < MAIN:
                        main[pl.ds((part * row_count + g * 8) * PITCH + j, 8, stride=PITCH), :] = piece
                    else:
                        c, s = divmod(g * 8, slots)
                        tail[j - MAIN, pl.ds(s * TAIL_PITCH + part * comp_count + c, 8, stride=TAIL_PITCH), :] = piece


def interact_kernel(source, offset, hat, hat_tail, main, tail, total, total_tail):
    box_count, list_count = source.shape
    padded = hat_tail.shape[0] // (2 * TAIL)
    row_count = main.shape[0] // (2 * PITCH)
    slots = tail.shape[1] // TAIL_PITCH - 2
    comp_count = row_count // slots
    f32 = jnp.float32
    plus = lax.broadcasted_iota(jnp.int32, (8, LANES), 0) < comp_count
    halves = MAIN // 8

    @pl.loop(0, box_count)
    def _(t):
        def pair(w, accs):
            s = source[t, w]
            o = offset[t, w]
            k = [
                [hat[pl.ds((r * padded + o) * PITCH + 8 * h, 8), :] for h in range(halves)] for r in range(2)
            ]
            accs = list(accs)
            at = 0
            for c in range(comp_count):
                for h in range(halves):
                    s_re = main[pl.ds((c * slots + s) * PITCH + 8 * h, 8), :]
                    s_im = main[pl.ds((row_count + c * slots + s) * PITCH + 8 * h, 8), :]
                    accs[at] = accs[at] + (k[0][h] * s_re - k[1][h] * s_im)
                    accs[at + 1] = accs[at + 1] + (k[0][h] * s_im + k[1][h] * s_re)
                    at += 2
            for j in range(TAIL):
                x = tail[j, pl.ds(s * TAIL_PITCH, 8), :]
                k_re = hat_tail[pl.ds(j * padded + o, 8, stride=0), :]
                k_im = hat_tail[pl.ds((TAIL + j) * padded + o, 8, stride=0), :]
                accs[at] = accs[at] + k_re * x
                accs[at + 1] = accs[at + 1] + k_im * x
                at += 2
            return tuple(accs)

        count = 2 * (comp_count * halves + TAIL)
        zero = jnp.zeros((8, LANES), f32)
        accs = lax.fori_loop(0, list_count, pair, (zero,) * count, unroll=4)
        at = 0
        for c in range(comp_count):
            for h in range(halves):
                for part in range(2):
                    row = (part * comp_count + c) * box_count + t
                    total[pl.ds(row * PITCH + 8 * h, 8), :] = accs[at + part]
                at += 2
        for j in range(TAIL):
            own, cross = accs[at], accs[at + 1]
            up = jnp.concatenate([cross[comp_count:], cross[:comp_count]], axis=0)
            down = jnp.concatenate([cross[-comp_count:], cross[:-comp_count]], axis=0)
            total_tail[j, pl.ds(t * TAIL_PITCH, 8), :] = jnp.where(plus, own - up, own + down)
            at += 2


def inverse_kernel(total, total_tail, table, factor, out):
    comp_count, box_count, surf = out.shape
    f32, bf16 = jnp.float32, jnp.bfloat16
    result = jnp.zeros((comp_count * box_count, 2 * POINTS_PAD), f32)
    rest = jnp.zeros((comp_count * box_count, POINTS_PAD), f32)
    groups = box_count // 8
    nt = (((1,), (1,)), ((), ()))
    for part in range(2):
        for n in range(FREQ // CHUNK):
            columns = slice(part * FREQ + n * CHUNK, part * FREQ + (n + 1) * CHUNK)
            lanes = []
            for m in range(CHUNK // LANES):
                j = n * (CHUNK // LANES) + m
                pieces = []
                for c in range(comp_count):
                    for g in range(groups):
                        if j < MAIN:
                            row = (part * comp_count + c) * box_count + g * 8
                            pieces.append(total[pl.ds(row * PITCH + j, 8, stride=PITCH), :])
                        else:
                            row = g * 8 * TAIL_PITCH + part * comp_count + c
                            pieces.append(total_tail[j - MAIN, pl.ds(row, 8, stride=TAIL_PITCH), :])
                lanes.append(jnp.concatenate(pieces, axis=0))
            x = jnp.concatenate(lanes, axis=1) * factor[:, columns]
            high = x.astype(bf16)
            low = (x - high.astype(f32)).astype(bf16)
            result += lax.dot_general(high, table[:, columns], nt, preferred_element_type=f32)
            rest += lax.dot_general(low, table[:POINTS_PAD, columns], nt, preferred_element_type=f32)
    result = result[:, :POINTS_PAD] + result[:, POINTS_PAD:] + rest
    for c in range(comp_count):
        out[c] = result[c * box_count : (c + 1) * box_count, :surf]


def on_device(density, kernel_hat, send_list, halo_list, inter_src, inter_off):
    table, factor = transform_tables()
    box_count, comp_count, surf = density.shape
    _, peers, cap = send_list.shape
    rim = halo_list.shape[2]
    f32 = jnp.float32
    vmem = pl.BlockSpec(memory_space=pltpu.VMEM)
    smem = pl.BlockSpec(memory_space=pltpu.SMEM)
    density = density.transpose(1, 0, 2)

    member = lax.axis_index("dev")
    place = jnp.bitwise_xor(member, jnp.arange(peers, dtype=jnp.int32)).astype(jnp.int32)
    boxes = jax.ShapeDtypeStruct((comp_count, cap, surf), f32)
    side = jax.ShapeDtypeStruct((comp_count, rim, surf), f32)
    *to_peers, to_prev, to_next = pl.pallas_call(
        pack_kernel,
        out_shape=(boxes,) * peers + (side,) * 2,
        in_specs=[smem, vmem, smem, smem],
        out_specs=(vmem,) * (peers + 2),
        name="pack",
    )(place, density, send_list[0], halo_list[0])
    pieces = [to_peers[0]]
    for k in range(1, peers):
        pieces.append(lax.ppermute(to_peers[k], "dev", [(i, i ^ k) for i in range(peers)]))
    groups = lax.axis_size("group")
    before = lax.ppermute(to_next, "group", [(i, i + 1) for i in range(groups - 1)])
    after = lax.ppermute(to_prev, "group", [(i + 1, i) for i in range(groups - 1)])

    offsets = kernel_hat.shape[0]
    padded = -(-offsets // 8) * 8
    hat, hat_tail = pl.pallas_call(
        prepare_kernel,
        out_shape=(
            jax.ShapeDtypeStruct((2 * padded * PITCH, LANES), f32),
            jax.ShapeDtypeStruct((2 * TAIL * padded, LANES), f32),
        ),
        in_specs=[vmem],
        out_specs=(vmem, vmem),
        compiler_params=pltpu.CompilerParams(vmem_limit_bytes=16 * 1024 * 1024),
        cost_estimate=pl.CostEstimate(flops=kernel_hat.size, bytes_accessed=6 * kernel_hat.size, transcendentals=0),
        name="prepare",
    )(kernel_hat.transpose(1, 0, 2))

    slots = box_count + peers * cap + 2 * rim
    row_count = comp_count * slots
    params = pltpu.CompilerParams(vmem_limit_bytes=24 * 1024 * 1024)
    table = jnp.asarray(table)
    main, tail = pl.pallas_call(
        forward_kernel,
        out_shape=(
            jax.ShapeDtypeStruct((2 * row_count * PITCH, LANES), f32),
            jax.ShapeDtypeStruct((TAIL, (slots + 2) * TAIL_PITCH, LANES), f32),
        ),
        in_specs=[smem] + [vmem] * (peers + 4),
        out_specs=(vmem, vmem),
        scratch_shapes=[pltpu.VMEM((row_count, POINTS_PAD), f32)],
        compiler_params=params,
        name="forward",
    )(place, density, *pieces, before, after, table)
    total, total_tail = pl.pallas_call(
        interact_kernel,
        out_shape=(
            jax.ShapeDtypeStruct((2 * comp_count * box_count * PITCH, LANES), f32),
            jax.ShapeDtypeStruct((TAIL, (box_count + 2) * TAIL_PITCH, LANES), f32),
        ),
        in_specs=[smem, smem] + [vmem] * 4,
        out_specs=(vmem, vmem),
        compiler_params=params,
        name="interact",
    )(inter_src, inter_off, hat, hat_tail, main, tail)
    potential = pl.pallas_call(
        inverse_kernel,
        out_shape=jax.ShapeDtypeStruct((comp_count, box_count, surf), f32),
        in_specs=[vmem] * 4,
        out_specs=vmem,
        compiler_params=params,
        name="inverse",
    )(total, total_tail, table, jnp.asarray(factor))
    return potential.transpose(1, 0, 2)


def solution(mesh):
    in_specs = (
        P(("group", "dev"), None, None),
        P(),
        P(("group", "dev"), None, None),
        P(("group", "dev"), None, None),
        P(("group", "dev"), None),
        P(("group", "dev"), None),
    )
    out_specs = P(("group", "dev"), None, None)
    return jax.shard_map(
        on_device, mesh=mesh, in_specs=in_specs, out_specs=out_specs, check_vma=False
    )
```

```python
import functools
import math

import jax
import jax.numpy as jnp
import ml_dtypes
import numpy as np
from jax import lax
from jax.experimental import pallas as pl
from jax.experimental.pallas import tpu as pltpu
from jax.sharding import PartitionSpec as P

ORDER = 6
GRID = 16
LANES = 128
HALF = GRID // 2 + 1
FREQ = GRID * GRID * HALF
TILES = FREQ // LANES
MAIN = 16
TAIL = TILES - MAIN
PITCH = MAIN
TAIL_PITCH = 7
POINTS_PAD = 160
CHUNK = 256


def surface_points(edge_count):
    points = [
        (i, j, k)
        for i in range(edge_count)
        for j in range(edge_count)
        for k in range(edge_count)
        if min(i, j, k) == 0 or max(i, j, k) == edge_count - 1
    ]
    return np.array(points, dtype=np.int64)


@functools.lru_cache(maxsize=None)
def transform_tables():
    points = surface_points(ORDER)
    kx, ky, kz = (a.reshape(-1) for a in np.meshgrid(np.arange(GRID), np.arange(GRID), np.arange(HALF), indexing="ij"))
    phase = (points[:, :1] * kx + points[:, 1:2] * ky + points[:, 2:] * kz) % GRID
    angle = phase * (2.0 * math.pi / GRID)
    table = np.zeros((POINTS_PAD, 2 * FREQ), np.float64)
    table[: len(points), :FREQ] = np.cos(angle)
    table[: len(points), FREQ:] = -np.sin(angle)
    table = np.where(np.abs(table) < 1e-9, 0.0, table)
    high = table.astype(ml_dtypes.bfloat16)
    low = (table - high.astype(np.float64)).astype(ml_dtypes.bfloat16)
    edge_plane = (kz == 0) | (kz == GRID // 2)
    factor = np.where(edge_plane, 1.0, 2.0) / GRID**3 * np.where((kx + ky + kz) % 2 == 0, 1.0, -1.0)
    factor = np.concatenate([factor, factor]).astype(np.float32)[None, :]
    return np.concatenate([high, low], axis=0), factor


def pack_kernel(density, send_list, halo_list, to_pair, to_other):
    peers, cap = send_list.shape
    rim = halo_list.shape[1]
    member = lax.axis_index("dev")
    parity = lax.rem(lax.axis_index("group"), 2)
    mine, partner = parity * peers, (1 - parity) * peers + member
    for c in range(density.shape[0]):
        for q in range(peers):
            for e in range(cap):
                to_pair[mine + q, c, e : e + 1, :] = density[c, pl.ds(send_list[q, e], 1), :]
        for e in range(rim):
            to_pair[partner, c, e : e + 1, :] = density[c, pl.ds(halo_list[1 - parity, e], 1), :]
            to_other[c, e : e + 1, :] = density[c, pl.ds(halo_list[parity, e], 1), :]


def prepare_kernel(kernel_hat, hat, hat_tail):
    parts, count, _ = kernel_hat.shape
    padded = hat_tail.shape[0] // (parts * TAIL)

    def move(first, height):
        for part in range(parts):
            for j in range(TILES):
                x = kernel_hat[part, pl.ds(first, height), j * LANES : (j + 1) * LANES].astype(jnp.float32)
                for g in range(0, height, 8):
                    size = min(8, height - g)
                    piece = x[g : g + size]
                    if j < MAIN:
                        row = (part * padded + first + g) * PITCH + j
                        hat[pl.ds(row, size, stride=PITCH), :] = piece
                    else:
                        row = (part * TAIL + j - MAIN) * padded + first + g
                        hat_tail[pl.ds(row, size), :] = piece

    whole = count // 16

    @pl.loop(0, whole)
    def _(i):
        move(pl.multiple_of(i * 16, 16), 16)

    if count % 16:
        move(whole * 16, count % 16)


def forward_kernel(density, send_list, from_pair, from_other, table, main, tail, rows):
    comp_count, box_count, surf = density.shape
    peers, cap = send_list.shape
    rim = from_other.shape[1]
    row_count = rows.shape[0]
    slots = row_count // comp_count
    f32, bf16 = jnp.float32, jnp.bfloat16

    member = lax.axis_index("dev")
    parity = lax.rem(lax.axis_index("group"), 2)
    mine, partner = parity * peers, (1 - parity) * peers + member
    rows[...] = jnp.zeros_like(rows)
    for c in range(comp_count):
        base = c * slots
        rows[base : base + box_count, :surf] = density[c]
        base += box_count
        for q in range(peers):
            rows[base : base + cap, :surf] = from_pair[mine + q, c, :cap]
            base += cap
        for e in range(rim):
            rows[pl.ds(base + (1 - parity) * rim + e, 1), :surf] = from_pair[partner, c, e : e + 1]
            rows[pl.ds(base + parity * rim + e, 1), :surf] = from_other[c, e : e + 1]

    value = rows[...]
    high = value.astype(bf16)
    low = (value - high.astype(f32)).astype(bf16)
    for part in range(2):
        for n in range(FREQ // CHUNK):
            columns = slice(part * FREQ + n * CHUNK, part * FREQ + (n + 1) * CHUNK)
            t_high = table[:POINTS_PAD, columns]
            t_low = table[POINTS_PAD:, columns]
            x = jnp.dot(high, t_high, preferred_element_type=f32)
            x = x + jnp.dot(low, t_high, preferred_element_type=f32)
            x = x + jnp.dot(high, t_low, preferred_element_type=f32)
            x = x.astype(bf16).astype(f32)
            for m in range(CHUNK // LANES):
                j = n * (CHUNK // LANES) + m
                for g in range(row_count // 8):
                    piece = x[g * 8 : (g + 1) * 8, m * LANES : (m + 1) * LANES]
                    if j < MAIN:
                        main[pl.ds((part * row_count + g * 8) * PITCH + j, 8, stride=PITCH), :] = piece
                    else:
                        c, s = divmod(g * 8, slots)
                        tail[j - MAIN, pl.ds(s * TAIL_PITCH + part * comp_count + c, 8, stride=TAIL_PITCH), :] = piece


def interact_kernel(source, offset, hat, hat_tail, main, tail, total, total_tail):
    box_count, list_count = source.shape
    padded = hat_tail.shape[0] // (2 * TAIL)
    row_count = main.shape[0] // (2 * PITCH)
    slots = tail.shape[1] // TAIL_PITCH - 2
    comp_count = row_count // slots
    f32 = jnp.float32
    plus = lax.broadcasted_iota(jnp.int32, (8, LANES), 0) < comp_count
    halves = MAIN // 8

    @pl.loop(0, box_count)
    def _(t):
        def pair(w, accs):
            s = source[t, w]
            o = offset[t, w]
            k = [
                [hat[pl.ds((r * padded + o) * PITCH + 8 * h, 8), :] for h in range(halves)] for r in range(2)
            ]
            accs = list(accs)
            at = 0
            for c in range(comp_count):
                for h in range(halves):
                    s_re = main[pl.ds((c * slots + s) * PITCH + 8 * h, 8), :]
                    s_im = main[pl.ds((row_count + c * slots + s) * PITCH + 8 * h, 8), :]
                    accs[at] = accs[at] + (k[0][h] * s_re - k[1][h] * s_im)
                    accs[at + 1] = accs[at + 1] + (k[0][h] * s_im + k[1][h] * s_re)
                    at += 2
            for j in range(TAIL):
                x = tail[j, pl.ds(s * TAIL_PITCH, 8), :]
                k_re = hat_tail[pl.ds(j * padded + o, 8, stride=0), :]
                k_im = hat_tail[pl.ds((TAIL + j) * padded + o, 8, stride=0), :]
                accs[at] = accs[at] + k_re * x
                accs[at + 1] = accs[at + 1] + k_im * x
                at += 2
            return tuple(accs)

        count = 2 * (comp_count * halves + TAIL)
        zero = jnp.zeros((8, LANES), f32)
        accs = lax.fori_loop(0, list_count, pair, (zero,) * count, unroll=4)
        at = 0
        for c in range(comp_count):
            for h in range(halves):
                for part in range(2):
                    row = (part * comp_count + c) * box_count + t
                    total[pl.ds(row * PITCH + 8 * h, 8), :] = accs[at + part]
                at += 2
        for j in range(TAIL):
            own, cross = accs[at], accs[at + 1]
            up = jnp.concatenate([cross[comp_count:], cross[:comp_count]], axis=0)
            down = jnp.concatenate([cross[-comp_count:], cross[:-comp_count]], axis=0)
            total_tail[j, pl.ds(t * TAIL_PITCH, 8), :] = jnp.where(plus, own - up, own + down)
            at += 2


def inverse_kernel(total, total_tail, table, factor, out):
    comp_count, box_count, surf = out.shape
    f32, bf16 = jnp.float32, jnp.bfloat16
    result = jnp.zeros((comp_count * box_count, 2 * POINTS_PAD), f32)
    rest = jnp.zeros((comp_count * box_count, POINTS_PAD), f32)
    groups = box_count // 8
    nt = (((1,), (1,)), ((), ()))
    for part in range(2):
        for n in range(FREQ // CHUNK):
            columns = slice(part * FREQ + n * CHUNK, part * FREQ + (n + 1) * CHUNK)
            lanes = []
            for m in range(CHUNK // LANES):
                j = n * (CHUNK // LANES) + m
                pieces = []
                for c in range(comp_count):
                    for g in range(groups):
                        if j < MAIN:
                            row = (part * comp_count + c) * box_count + g * 8
                            pieces.append(total[pl.ds(row * PITCH + j, 8, stride=PITCH), :])
                        else:
                            row = g * 8 * TAIL_PITCH + part * comp_count + c
                            pieces.append(total_tail[j - MAIN, pl.ds(row, 8, stride=TAIL_PITCH), :])
                lanes.append(jnp.concatenate(pieces, axis=0))
            x = jnp.concatenate(lanes, axis=1) * factor[:, columns]
            high = x.astype(bf16)
            low = (x - high.astype(f32)).astype(bf16)
            result += lax.dot_general(high, table[:, columns], nt, preferred_element_type=f32)
            rest += lax.dot_general(low, table[:POINTS_PAD, columns], nt, preferred_element_type=f32)
    result = result[:, :POINTS_PAD] + result[:, POINTS_PAD:] + rest
    for c in range(comp_count):
        out[c] = result[c * box_count : (c + 1) * box_count, :surf]


def on_device(density, kernel_hat, send_list, halo_list, inter_src, inter_off):
    table, factor = transform_tables()
    box_count, comp_count, surf = density.shape
    _, peers, cap = send_list.shape
    rim = halo_list.shape[2]
    f32 = jnp.float32
    vmem = pl.BlockSpec(memory_space=pltpu.VMEM)
    smem = pl.BlockSpec(memory_space=pltpu.SMEM)
    density = density.transpose(1, 0, 2)

    groups = lax.axis_size("group")
    high = max(cap, rim)
    to_pair, to_other = pl.pallas_call(
        pack_kernel,
        out_shape=(
            jax.ShapeDtypeStruct((2 * peers, comp_count, high, surf), f32),
            jax.ShapeDtypeStruct((comp_count, rim, surf), f32),
        ),
        in_specs=[vmem, smem, smem],
        out_specs=(vmem, vmem),
        name="pack",
    )(density, send_list[0], halo_list[0])
    pairs = [list(range(i, i + 2 * peers)) for i in range(0, groups * peers, 2 * peers)]
    from_pair = lax.all_to_all(to_pair, ("group", "dev"), 0, 0, axis_index_groups=pairs, tiled=True)
    swaps = [(i, i + 1) for i in range(1, groups - 1, 2)]
    from_other = lax.ppermute(to_other, "group", swaps + [(j, i) for i, j in swaps])

    offsets = kernel_hat.shape[0]
    padded = -(-offsets // 8) * 8
    hat, hat_tail = pl.pallas_call(
        prepare_kernel,
        out_shape=(
            jax.ShapeDtypeStruct((2 * padded * PITCH, LANES), f32),
            jax.ShapeDtypeStruct((2 * TAIL * padded, LANES), f32),
        ),
        in_specs=[vmem],
        out_specs=(vmem, vmem),
        compiler_params=pltpu.CompilerParams(vmem_limit_bytes=16 * 1024 * 1024),
        cost_estimate=pl.CostEstimate(flops=kernel_hat.size, bytes_accessed=6 * kernel_hat.size, transcendentals=0),
        name="prepare",
    )(kernel_hat.transpose(1, 0, 2))

    slots = box_count + peers * cap + 2 * rim
    row_count = comp_count * slots
    params = pltpu.CompilerParams(vmem_limit_bytes=24 * 1024 * 1024)
    table = jnp.asarray(table)
    main, tail = pl.pallas_call(
        forward_kernel,
        out_shape=(
            jax.ShapeDtypeStruct((2 * row_count * PITCH, LANES), f32),
            jax.ShapeDtypeStruct((TAIL, (slots + 2) * TAIL_PITCH, LANES), f32),
        ),
        in_specs=[vmem, smem, vmem, vmem, vmem],
        out_specs=(vmem, vmem),
        scratch_shapes=[pltpu.VMEM((row_count, POINTS_PAD), f32)],
        compiler_params=params,
        name="forward",
    )(density, send_list[0], from_pair, from_other, table)
    total, total_tail = pl.pallas_call(
        interact_kernel,
        out_shape=(
            jax.ShapeDtypeStruct((2 * comp_count * box_count * PITCH, LANES), f32),
            jax.ShapeDtypeStruct((TAIL, (box_count + 2) * TAIL_PITCH, LANES), f32),
        ),
        in_specs=[smem, smem] + [vmem] * 4,
        out_specs=(vmem, vmem),
        compiler_params=params,
        name="interact",
    )(inter_src, inter_off, hat, hat_tail, main, tail)
    potential = pl.pallas_call(
        inverse_kernel,
        out_shape=jax.ShapeDtypeStruct((comp_count, box_count, surf), f32),
        in_specs=[vmem] * 4,
        out_specs=vmem,
        compiler_params=params,
        name="inverse",
    )(total, total_tail, table, jnp.asarray(factor))
    return potential.transpose(1, 0, 2)


def solution(mesh):
    in_specs = (
        P(("group", "dev"), None, None),
        P(),
        P(("group", "dev"), None, None),
        P(("group", "dev"), None, None),
        P(("group", "dev"), None),
        P(("group", "dev"), None),
    )
    out_specs = P(("group", "dev"), None, None)
    return jax.shard_map(
        on_device, mesh=mesh, in_specs=in_specs, out_specs=out_specs, check_vma=False
    )
```

```python
import functools
import math

import jax
import jax.numpy as jnp
import ml_dtypes
import numpy as np
from jax import lax
from jax.experimental import pallas as pl
from jax.experimental.pallas import tpu as pltpu
from jax.sharding import PartitionSpec as P

ORDER = 6
GRID = 16
LANES = 128
HALF = GRID // 2 + 1
FREQ = GRID * GRID * HALF
TILES = FREQ // LANES
MAIN = 16
TAIL = TILES - MAIN
PITCH = MAIN + 1
TAIL_PITCH = 7
POINTS_PAD = 160
CHUNK = 256
PIECE = 512


def surface_points(edge_count):
    points = [
        (i, j, k)
        for i in range(edge_count)
        for j in range(edge_count)
        for k in range(edge_count)
        if min(i, j, k) == 0 or max(i, j, k) == edge_count - 1
    ]
    return np.array(points, dtype=np.int64)


@functools.lru_cache(maxsize=None)
def transform_tables():
    points = surface_points(ORDER)
    kx, ky, kz = (a.reshape(-1) for a in np.meshgrid(np.arange(GRID), np.arange(GRID), np.arange(HALF), indexing="ij"))
    phase = (points[:, :1] * kx + points[:, 1:2] * ky + points[:, 2:] * kz) % GRID
    angle = phase * (2.0 * math.pi / GRID)
    table = np.zeros((POINTS_PAD, 2 * FREQ), np.float64)
    table[: len(points), :FREQ] = np.cos(angle)
    table[: len(points), FREQ:] = -np.sin(angle)
    table = np.where(np.abs(table) < 1e-9, 0.0, table)
    high = table.astype(ml_dtypes.bfloat16)
    low = (table - high.astype(np.float64)).astype(ml_dtypes.bfloat16)
    edge_plane = (kz == 0) | (kz == GRID // 2)
    factor = np.where(edge_plane, 1.0, 2.0) / GRID**3 * np.where((kx + ky + kz) % 2 == 0, 1.0, -1.0)
    factor = np.concatenate([factor, factor]).astype(np.float32)[None, :]
    return np.concatenate([high, low], axis=0), factor


def pack_kernel(density, send_list, halo_list, to_pair, to_other):
    peers, cap = send_list.shape
    rim = halo_list.shape[1]
    member = lax.axis_index("dev")
    parity = lax.rem(lax.axis_index("group"), 2)
    mine, partner = parity * peers, (1 - parity) * peers + member
    for c in range(density.shape[0]):
        for q in range(peers):
            for e in range(cap):
                to_pair[mine + q, c, e : e + 1, :] = density[c, pl.ds(send_list[q, e], 1), :]
        for e in range(rim):
            to_pair[partner, c, e : e + 1, :] = density[c, pl.ds(halo_list[1 - parity, e], 1), :]
            to_other[c, e : e + 1, :] = density[c, pl.ds(halo_list[parity, e], 1), :]


def translate_kernel(
    source, offset, send_list, density, from_pair, from_other, factor, table_hbm, kernel_hbm, out,
    table, raw, hat, hat_tail, rows, main, tail, total, total_tail, table_sem, raw_sem,
):
    comp_count, box_count, surf = density.shape
    list_count = source.shape[1]
    peers, cap = send_list.shape
    rim = from_other.shape[1]
    row_count = rows.shape[0]
    slots = row_count // comp_count
    offsets, padded = kernel_hbm.shape[0], raw.shape[1]
    f32, bf16 = jnp.float32, jnp.bfloat16

    def table_copy(n):
        columns = pl.ds(n * PIECE, PIECE)
        return pltpu.make_async_copy(table_hbm.at[:, columns], table.at[:, columns], table_sem.at[n])

    def raw_copy(j):
        return pltpu.make_async_copy(
            kernel_hbm.at[:, :, pl.ds(j * LANES, LANES)], raw.at[j, pl.ds(0, offsets)], raw_sem.at[j]
        )

    for n in range(2 * FREQ // PIECE):
        table_copy(n).start()
    for j in range(TILES):
        raw_copy(j).start()

    member = lax.axis_index("dev")
    parity = lax.rem(lax.axis_index("group"), 2)
    mine, partner = parity * peers, (1 - parity) * peers + member
    rows[...] = jnp.zeros_like(rows)
    for c in range(comp_count):
        base = c * slots
        rows[base : base + box_count, :surf] = density[c]
        base += box_count
        for q in range(peers):
            rows[base : base + cap, :surf] = from_pair[mine + q, c, :cap]
            base += cap
        for e in range(rim):
            rows[pl.ds(base + (1 - parity) * rim + e, 1), :surf] = from_pair[partner, c, e : e + 1]
            rows[pl.ds(base + parity * rim + e, 1), :surf] = from_other[c, e : e + 1]

    value = rows[...]
    high = value.astype(bf16)
    low = (value - high.astype(f32)).astype(bf16)
    both = jnp.concatenate([high, low], axis=0)
    for n in range(2 * FREQ // CHUNK):
        if n * CHUNK % PIECE == 0:
            table_copy(n * CHUNK // PIECE).wait()
        columns = slice(n * CHUNK, (n + 1) * CHUNK)
        x = jnp.dot(both, table[:POINTS_PAD, columns], preferred_element_type=f32)
        x = x[:row_count] + x[row_count:]
        x = x + jnp.dot(high, table[POINTS_PAD:, columns], preferred_element_type=f32)
        x = x.astype(bf16).astype(f32)
        for m in range(CHUNK // LANES):
            part, j = divmod(n * (CHUNK // LANES) + m, TILES)
            for g in range(row_count // 8):
                piece = x[g * 8 : (g + 1) * 8, m * LANES : (m + 1) * LANES]
                if j < MAIN:
                    main[pl.ds((part * row_count + g * 8) * PITCH + j, 8, stride=PITCH), :] = piece
                else:
                    c, s = divmod(g * 8, slots)
                    tail[j - MAIN, pl.ds(s * TAIL_PITCH + part * comp_count + c, 8, stride=TAIL_PITCH), :] = piece

    for j in range(TILES):
        raw_copy(j).wait()
    flat = raw.reshape(TILES * padded * 2, LANES)

    @pl.loop(0, padded * 2 // 16)
    def _(i):
        for j in range(TILES):
            x = flat[pl.ds(pl.multiple_of(j * padded * 2 + i * 16, 16), 16), :].astype(f32)
            for g in range(2):
                row = i * 16 + g * 8
                if j < MAIN:
                    hat[pl.ds(row * PITCH + j, 8, stride=PITCH), :] = x[g * 8 : g * 8 + 8]
                else:
                    hat_tail[pl.ds((j - MAIN) * padded * 2 + row, 8), :] = x[g * 8 : g * 8 + 8]

    plus = lax.broadcasted_iota(jnp.int32, (8, LANES), 0) < comp_count
    halves = MAIN // 8

    @pl.loop(0, box_count)
    def _(t):
        def pair(w, accs):
            s = source[t, w]
            o = offset[t, w]
            k = [
                [hat[pl.ds((2 * o + r) * PITCH + 8 * h, 8), :] for h in range(halves)] for r in range(2)
            ]
            accs = list(accs)
            at = 0
            for c in range(comp_count):
                for h in range(halves):
                    s_re = main[pl.ds((c * slots + s) * PITCH + 8 * h, 8), :]
                    s_im = main[pl.ds((row_count + c * slots + s) * PITCH + 8 * h, 8), :]
                    accs[at] = accs[at] + (k[0][h] * s_re - k[1][h] * s_im)
                    accs[at + 1] = accs[at + 1] + (k[0][h] * s_im + k[1][h] * s_re)
                    at += 2
            for j in range(TAIL):
                x = tail[j, pl.ds(s * TAIL_PITCH, 8), :]
                k_re = hat_tail[pl.ds(2 * (j * padded + o), 8, stride=0), :]
                k_im = hat_tail[pl.ds(2 * (j * padded + o) + 1, 8, stride=0), :]
                accs[at] = accs[at] + k_re * x
                accs[at + 1] = accs[at + 1] + k_im * x
                at += 2
            return tuple(accs)

        count = 2 * (comp_count * halves + TAIL)
        zero = jnp.zeros((8, LANES), f32)
        accs = lax.fori_loop(0, list_count, pair, (zero,) * count, unroll=True)
        at = 0
        for c in range(comp_count):
            for h in range(halves):
                for part in range(2):
                    row = (part * comp_count + c) * box_count + t
                    total[pl.ds(row * PITCH + 8 * h, 8), :] = accs[at + part]
                at += 2
        for j in range(TAIL):
            own, cross = accs[at], accs[at + 1]
            up = jnp.concatenate([cross[comp_count:], cross[:comp_count]], axis=0)
            down = jnp.concatenate([cross[-comp_count:], cross[:-comp_count]], axis=0)
            total_tail[j, pl.ds(t * TAIL_PITCH, 8), :] = jnp.where(plus, own - up, own + down)
            at += 2

    groups = box_count // 8
    count = comp_count * box_count
    nt = (((1,), (1,)), ((), ()))
    result = jnp.zeros((2 * POINTS_PAD, 2 * count), f32)
    for n in range(2 * FREQ // PIECE):
        lanes = []
        for m in range(PIECE // LANES):
            part, j = divmod(n * (PIECE // LANES) + m, TILES)
            pieces = []
            for c in range(comp_count):
                for g in range(groups):
                    if j < MAIN:
                        row = (part * comp_count + c) * box_count + g * 8
                        pieces.append(total[pl.ds(row * PITCH + j, 8, stride=PITCH), :])
                    else:
                        row = g * 8 * TAIL_PITCH + part * comp_count + c
                        pieces.append(total_tail[j - MAIN, pl.ds(row, 8, stride=TAIL_PITCH), :])
            lanes.append(jnp.concatenate(pieces, axis=0))
        columns = slice(n * PIECE, (n + 1) * PIECE)
        x = jnp.concatenate(lanes, axis=1) * factor[:, columns]
        high = x.astype(bf16)
        low = (x - high.astype(f32)).astype(bf16)
        both = jnp.concatenate([high, low], axis=0)
        result += lax.dot_general(table[:, columns], both, nt, preferred_element_type=f32)
    result = result[:POINTS_PAD, :count] + result[:POINTS_PAD, count:] + result[POINTS_PAD:, :count]
    result = result.T
    for c in range(comp_count):
        out[c] = result[c * box_count : (c + 1) * box_count, :surf]


def on_device(density, kernel_hat, send_list, halo_list, inter_src, inter_off):
    table, factor = transform_tables()
    box_count, comp_count, surf = density.shape
    _, peers, cap = send_list.shape
    rim = halo_list.shape[2]
    f32 = jnp.float32
    vmem = pl.BlockSpec(memory_space=pltpu.VMEM)
    smem = pl.BlockSpec(memory_space=pltpu.SMEM)
    density = density.transpose(1, 0, 2)

    groups = lax.axis_size("group")
    high = max(cap, rim)
    to_pair, to_other = pl.pallas_call(
        pack_kernel,
        out_shape=(
            jax.ShapeDtypeStruct((2 * peers, comp_count, high, surf), f32),
            jax.ShapeDtypeStruct((comp_count, rim, surf), f32),
        ),
        in_specs=[vmem, smem, smem],
        out_specs=(vmem, vmem),
        name="pack",
    )(density, send_list[0], halo_list[0])
    pairs = [list(range(i, i + 2 * peers)) for i in range(0, groups * peers, 2 * peers)]
    from_pair = lax.all_to_all(to_pair, ("group", "dev"), 0, 0, axis_index_groups=pairs, tiled=True)
    swaps = [(i, i + 1) for i in range(1, groups - 1, 2)]
    from_other = lax.ppermute(to_other, "group", swaps + [(j, i) for i, j in swaps])

    padded = -(-kernel_hat.shape[0] // 8) * 8
    slots = box_count + peers * cap + 2 * rim
    row_count = comp_count * slots
    hbm = pl.BlockSpec(memory_space=pl.ANY)
    potential = pl.pallas_call(
        translate_kernel,
        out_shape=jax.ShapeDtypeStruct((comp_count, box_count, surf), f32),
        in_specs=[smem] * 3 + [vmem] * 4 + [hbm] * 2,
        out_specs=vmem,
        scratch_shapes=[
            pltpu.VMEM(table.shape, jnp.bfloat16),
            pltpu.VMEM((TILES, padded, 2, LANES), jnp.bfloat16),
            pltpu.VMEM((2 * padded * PITCH, LANES), f32),
            pltpu.VMEM((TAIL * padded * 2 + 8, LANES), f32),
            pltpu.VMEM((row_count, POINTS_PAD), f32),
            pltpu.VMEM((2 * row_count * PITCH, LANES), f32),
            pltpu.VMEM((TAIL, (slots + 2) * TAIL_PITCH, LANES), f32),
            pltpu.VMEM((2 * comp_count * box_count * PITCH, LANES), f32),
            pltpu.VMEM((TAIL, (box_count + 2) * TAIL_PITCH, LANES), f32),
            pltpu.SemaphoreType.DMA((2 * FREQ // PIECE,)),
            pltpu.SemaphoreType.DMA((TILES,)),
        ],
        compiler_params=pltpu.CompilerParams(vmem_limit_bytes=60 * 1024 * 1024),
        name="translate",
    )(
        inter_src, inter_off, send_list[0], density, from_pair, from_other,
        jnp.asarray(factor), jnp.asarray(table), kernel_hat,
    )
    return potential.transpose(1, 0, 2)


def solution(mesh):
    in_specs = (
        P(("group", "dev"), None, None),
        P(),
        P(("group", "dev"), None, None),
        P(("group", "dev"), None, None),
        P(("group", "dev"), None),
        P(("group", "dev"), None),
    )
    out_specs = P(("group", "dev"), None, None)
    return jax.shard_map(
        on_device, mesh=mesh, in_specs=in_specs, out_specs=out_specs, check_vma=False
    )
```

```python
import functools
import math

import jax
import jax.numpy as jnp
import ml_dtypes
import numpy as np
from jax import lax
from jax.experimental import pallas as pl
from jax.experimental.pallas import tpu as pltpu
from jax.sharding import PartitionSpec as P

ORDER = 6
GRID = 16
LANES = 128
HALF = GRID // 2 + 1
FREQ = GRID * GRID * HALF
TILES = FREQ // LANES
MAIN = 16
TAIL = TILES - MAIN
PITCH = MAIN + 1
TAIL_PITCH = 7
POINTS_PAD = 160
CHUNK = 256
PIECE = 512


def surface_points(edge_count):
    points = [
        (i, j, k)
        for i in range(edge_count)
        for j in range(edge_count)
        for k in range(edge_count)
        if min(i, j, k) == 0 or max(i, j, k) == edge_count - 1
    ]
    return np.array(points, dtype=np.int64)


@functools.lru_cache(maxsize=None)
def transform_tables():
    points = surface_points(ORDER)
    kx, ky, kz = (a.reshape(-1) for a in np.meshgrid(np.arange(GRID), np.arange(GRID), np.arange(HALF), indexing="ij"))
    phase = (points[:, :1] * kx + points[:, 1:2] * ky + points[:, 2:] * kz) % GRID
    angle = phase * (2.0 * math.pi / GRID)
    table = np.zeros((POINTS_PAD, 2 * FREQ), np.float64)
    table[: len(points), :FREQ] = np.cos(angle)
    table[: len(points), FREQ:] = -np.sin(angle)
    table = np.where(np.abs(table) < 1e-9, 0.0, table)
    high = table.astype(ml_dtypes.bfloat16)
    low = (table - high.astype(np.float64)).astype(ml_dtypes.bfloat16)
    edge_plane = (kz == 0) | (kz == GRID // 2)
    factor = np.where(edge_plane, 1.0, 2.0) / GRID**3 * np.where((kx + ky + kz) % 2 == 0, 1.0, -1.0)
    factor = np.concatenate([factor, factor]).astype(np.float32)[None, :]
    return np.concatenate([high, low], axis=0), factor


def pack_kernel(density, send_list, halo_list, *outs):
    peers, cap = send_list.shape
    rim = halo_list.shape[1]
    member = lax.axis_index("dev")
    parity = lax.rem(lax.axis_index("group"), 2)
    to_near, *to_far, to_first, to_second = outs
    for c in range(density.shape[0]):
        for e in range(cap):
            for part, k in enumerate((1, 3)):
                to_near[part, c, e : e + 1, :] = density[c, pl.ds(send_list[member ^ k, e], 1), :]
            for k, out in zip((2, *range(4, peers)), to_far):
                out[c, e : e + 1, :] = density[c, pl.ds(send_list[member ^ k, e], 1), :]
        for e in range(rim):
            to_first[c, e : e + 1, :] = density[c, pl.ds(halo_list[1 - parity, e], 1), :]
            to_second[c, e : e + 1, :] = density[c, pl.ds(halo_list[parity, e], 1), :]


def prepare_kernel(kernel_hat, hat, hat_tail):
    parts, count, _ = kernel_hat.shape
    padded = hat_tail.shape[0] // (parts * TAIL)

    def move(first, height):
        for part in range(parts):
            for j in range(TILES):
                x = kernel_hat[part, pl.ds(first, height), j * LANES : (j + 1) * LANES].astype(jnp.float32)
                for g in range(0, height, 8):
                    size = min(8, height - g)
                    piece = x[g : g + size]
                    if j < MAIN:
                        row = (part * padded + first + g) * PITCH + j
                        hat[pl.ds(row, size, stride=PITCH), :] = piece
                    else:
                        row = (part * TAIL + j - MAIN) * padded + first + g
                        hat_tail[pl.ds(row, size), :] = piece

    whole = count // 16

    @pl.loop(0, whole)
    def _(i):
        move(pl.multiple_of(i * 16, 16), 16)

    if count % 16:
        move(whole * 16, count % 16)


def forward_kernel(send_list, density, from_near, relayed, *refs):
    *from_far, from_first, from_second, table, main, tail, rows = refs
    comp_count, box_count, surf = density.shape
    peers, cap = send_list.shape
    rim = from_first.shape[1]
    row_count = rows.shape[0]
    slots = row_count // comp_count
    f32, bf16 = jnp.float32, jnp.bfloat16

    member = lax.axis_index("dev")
    parity = lax.rem(lax.axis_index("group"), 2)
    rows[...] = jnp.zeros_like(rows)
    pieces = {1: from_near.at[0], 3: relayed.at[1]}
    pieces.update(zip((2, *range(4, peers)), from_far))
    for c in range(comp_count):
        base = c * slots
        rows[base : base + box_count, :surf] = density[c]
        base += box_count
        for e in range(cap):
            rows[pl.ds(base + member * cap + e, 1), :surf] = density[c, pl.ds(send_list[member, e], 1), :]
            for k, piece in pieces.items():
                rows[pl.ds(base + (member ^ k) * cap + e, 1), :surf] = piece[c, e : e + 1]
        base += peers * cap
        for e in range(rim):
            rows[pl.ds(base + (1 - parity) * rim + e, 1), :surf] = from_first[c, e : e + 1]
            rows[pl.ds(base + parity * rim + e, 1), :surf] = from_second[c, e : e + 1]

    value = rows[...]
    high = value.astype(bf16)
    low = (value - high.astype(f32)).astype(bf16)
    both = jnp.concatenate([high, low], axis=0)
    for n in range(2 * FREQ // CHUNK):
        columns = slice(n * CHUNK, (n + 1) * CHUNK)
        x = jnp.dot(both, table[:POINTS_PAD, columns], preferred_element_type=f32)
        x = x[:row_count] + x[row_count:]
        x = x + jnp.dot(high, table[POINTS_PAD:, columns], preferred_element_type=f32)
        x = x.astype(bf16).astype(f32)
        for m in range(CHUNK // LANES):
            part, j = divmod(n * (CHUNK // LANES) + m, TILES)
            for g in range(row_count // 8):
                piece = x[g * 8 : (g + 1) * 8, m * LANES : (m + 1) * LANES]
                if j < MAIN:
                    main[pl.ds((part * row_count + g * 8) * PITCH + j, 8, stride=PITCH), :] = piece
                else:
                    c, s = divmod(g * 8, slots)
                    tail[j - MAIN, pl.ds(s * TAIL_PITCH + part * comp_count + c, 8, stride=TAIL_PITCH), :] = piece


def interact_kernel(source, offset, hat, hat_tail, main, tail, total, total_tail):
    box_count, list_count = source.shape
    padded = hat_tail.shape[0] // (2 * TAIL)
    row_count = main.shape[0] // (2 * PITCH)
    slots = tail.shape[1] // TAIL_PITCH - 2
    comp_count = row_count // slots
    f32 = jnp.float32
    plus = lax.broadcasted_iota(jnp.int32, (8, LANES), 0) < comp_count
    halves = MAIN // 8

    @pl.loop(0, box_count)
    def _(t):
        def pair(w, accs):
            s = source[t, w]
            o = offset[t, w]
            k = [
                [hat[pl.ds((r * padded + o) * PITCH + 8 * h, 8), :] for h in range(halves)] for r in range(2)
            ]
            accs = list(accs)
            at = 0
            for c in range(comp_count):
                for h in range(halves):
                    s_re = main[pl.ds((c * slots + s) * PITCH + 8 * h, 8), :]
                    s_im = main[pl.ds((row_count + c * slots + s) * PITCH + 8 * h, 8), :]
                    accs[at] = accs[at] + (k[0][h] * s_re - k[1][h] * s_im)
                    accs[at + 1] = accs[at + 1] + (k[0][h] * s_im + k[1][h] * s_re)
                    at += 2
            for j in range(TAIL):
                x = tail[j, pl.ds(s * TAIL_PITCH, 8), :]
                k_re = hat_tail[pl.ds(j * padded + o, 8, stride=0), :]
                k_im = hat_tail[pl.ds((TAIL + j) * padded + o, 8, stride=0), :]
                accs[at] = accs[at] + k_re * x
                accs[at + 1] = accs[at + 1] + k_im * x
                at += 2
            return tuple(accs)

        count = 2 * (comp_count * halves + TAIL)
        zero = jnp.zeros((8, LANES), f32)
        accs = lax.fori_loop(0, list_count, pair, (zero,) * count, unroll=True)
        at = 0
        for c in range(comp_count):
            for h in range(halves):
                for part in range(2):
                    row = (part * comp_count + c) * box_count + t
                    total[pl.ds(row * PITCH + 8 * h, 8), :] = accs[at + part]
                at += 2
        for j in range(TAIL):
            own, cross = accs[at], accs[at + 1]
            up = jnp.concatenate([cross[comp_count:], cross[:comp_count]], axis=0)
            down = jnp.concatenate([cross[-comp_count:], cross[:-comp_count]], axis=0)
            total_tail[j, pl.ds(t * TAIL_PITCH, 8), :] = jnp.where(plus, own - up, own + down)
            at += 2


def inverse_kernel(total, total_tail, table, factor, out):
    comp_count, box_count, surf = out.shape
    f32, bf16 = jnp.float32, jnp.bfloat16
    groups = box_count // 8
    count = comp_count * box_count
    nt = (((1,), (1,)), ((), ()))
    result = jnp.zeros((2 * POINTS_PAD, 2 * count), f32)
    for n in range(2 * FREQ // PIECE):
        lanes = []
        for m in range(PIECE // LANES):
            part, j = divmod(n * (PIECE // LANES) + m, TILES)
            pieces = []
            for c in range(comp_count):
                for g in range(groups):
                    if j < MAIN:
                        row = (part * comp_count + c) * box_count + g * 8
                        pieces.append(total[pl.ds(row * PITCH + j, 8, stride=PITCH), :])
                    else:
                        row = g * 8 * TAIL_PITCH + part * comp_count + c
                        pieces.append(total_tail[j - MAIN, pl.ds(row, 8, stride=TAIL_PITCH), :])
            lanes.append(jnp.concatenate(pieces, axis=0))
        columns = slice(n * PIECE, (n + 1) * PIECE)
        x = jnp.concatenate(lanes, axis=1) * factor[:, columns]
        high = x.astype(bf16)
        low = (x - high.astype(f32)).astype(bf16)
        both = jnp.concatenate([high, low], axis=0)
        result += lax.dot_general(table[:, columns], both, nt, preferred_element_type=f32)
    result = result[:POINTS_PAD, :count] + result[:POINTS_PAD, count:] + result[POINTS_PAD:, :count]
    result = result.T
    for c in range(comp_count):
        out[c] = result[c * box_count : (c + 1) * box_count, :surf]


def on_device(density, kernel_hat, send_list, halo_list, inter_src, inter_off):
    table, factor = transform_tables()
    box_count, comp_count, surf = density.shape
    _, peers, cap = send_list.shape
    rim = halo_list.shape[2]
    f32 = jnp.float32
    vmem = pl.BlockSpec(memory_space=pltpu.VMEM)
    smem = pl.BlockSpec(memory_space=pltpu.SMEM)
    density = density.transpose(1, 0, 2)

    boxes = jax.ShapeDtypeStruct((comp_count, cap, surf), f32)
    side = jax.ShapeDtypeStruct((comp_count, rim, surf), f32)
    to_near, *to_far, to_first, to_second = pl.pallas_call(
        pack_kernel,
        out_shape=(jax.ShapeDtypeStruct((2, *boxes.shape), f32),) + (boxes,) * (peers - 3) + (side,) * 2,
        in_specs=[vmem, smem, smem],
        out_specs=(vmem,) * peers,
        name="pack",
    )(density, send_list[0], halo_list[0])

    def swap(x, k):
        return lax.ppermute(x, "dev", [(i, i ^ k) for i in range(peers)])

    def swap_groups(x, start):
        pairs = [(i, i + 1) for i in range(start, lax.axis_size("group") - 1, 2)]
        return lax.ppermute(x, "group", pairs + [(j, i) for i, j in pairs])

    from_near = swap(to_near, 1)
    from_far = [swap(x, k) for x, k in zip(to_far, (2, *range(4, peers)))]
    from_first = swap_groups(to_first, 0)
    from_second = swap_groups(to_second, 1)
    by_part, near = lax.optimization_barrier((kernel_hat.transpose(1, 0, 2), from_near))
    relayed = swap(near, 2)

    offsets = kernel_hat.shape[0]
    padded = -(-offsets // 8) * 8
    hat, hat_tail = pl.pallas_call(
        prepare_kernel,
        out_shape=(
            jax.ShapeDtypeStruct((2 * padded * PITCH, LANES), f32),
            jax.ShapeDtypeStruct((2 * TAIL * padded, LANES), f32),
        ),
        in_specs=[vmem],
        out_specs=(vmem, vmem),
        compiler_params=pltpu.CompilerParams(vmem_limit_bytes=16 * 1024 * 1024),
        cost_estimate=pl.CostEstimate(flops=kernel_hat.size, bytes_accessed=6 * kernel_hat.size, transcendentals=0),
        name="prepare",
    )(by_part)

    slots = box_count + peers * cap + 2 * rim
    row_count = comp_count * slots
    params = pltpu.CompilerParams(vmem_limit_bytes=24 * 1024 * 1024)
    table = jnp.asarray(table)
    arrays = (send_list[0], density, from_near, relayed, *from_far, from_first, from_second, table)
    main, tail = pl.pallas_call(
        forward_kernel,
        out_shape=(
            jax.ShapeDtypeStruct((2 * row_count * PITCH, LANES), f32),
            jax.ShapeDtypeStruct((TAIL, (slots + 2) * TAIL_PITCH, LANES), f32),
        ),
        in_specs=[smem] + [vmem] * (len(arrays) - 1),
        out_specs=(vmem, vmem),
        scratch_shapes=[pltpu.VMEM((row_count, POINTS_PAD), f32)],
        compiler_params=params,
        name="forward",
    )(*arrays)
    total, total_tail = pl.pallas_call(
        interact_kernel,
        out_shape=(
            jax.ShapeDtypeStruct((2 * comp_count * box_count * PITCH, LANES), f32),
            jax.ShapeDtypeStruct((TAIL, (box_count + 2) * TAIL_PITCH, LANES), f32),
        ),
        in_specs=[smem, smem] + [vmem] * 4,
        out_specs=(vmem, vmem),
        compiler_params=params,
        name="interact",
    )(inter_src, inter_off, hat, hat_tail, main, tail)
    potential = pl.pallas_call(
        inverse_kernel,
        out_shape=jax.ShapeDtypeStruct((comp_count, box_count, surf), f32),
        in_specs=[vmem] * 4,
        out_specs=vmem,
        compiler_params=params,
        name="inverse",
    )(total, total_tail, table, jnp.asarray(factor))
    return potential.transpose(1, 0, 2)


def solution(mesh):
    in_specs = (
        P(("group", "dev"), None, None),
        P(),
        P(("group", "dev"), None, None),
        P(("group", "dev"), None, None),
        P(("group", "dev"), None),
        P(("group", "dev"), None),
    )
    out_specs = P(("group", "dev"), None, None)
    return jax.shard_map(
        on_device, mesh=mesh, in_specs=in_specs, out_specs=out_specs, check_vma=False
    )
```

```python
import functools
import math

import jax
import jax.numpy as jnp
import ml_dtypes
import numpy as np
from jax import lax
from jax.experimental import pallas as pl
from jax.experimental.pallas import tpu as pltpu
from jax.sharding import PartitionSpec as P

ORDER = 6
GRID = 16
LANES = 128
HALF = GRID // 2 + 1
FREQ = GRID * GRID * HALF
TILES = FREQ // LANES
MAIN = 16
TAIL = TILES - MAIN
PITCH = MAIN + 1
TAIL_PITCH = 7
HAT_ROWS = 2 * TILES + 1
POINTS_PAD = 160
CHUNK = 256
PIECE = 512


def surface_points(edge_count):
    points = [
        (i, j, k)
        for i in range(edge_count)
        for j in range(edge_count)
        for k in range(edge_count)
        if min(i, j, k) == 0 or max(i, j, k) == edge_count - 1
    ]
    return np.array(points, dtype=np.int64)


@functools.lru_cache(maxsize=None)
def transform_tables():
    points = surface_points(ORDER)
    kx, ky, kz = (a.reshape(-1) for a in np.meshgrid(np.arange(GRID), np.arange(GRID), np.arange(HALF), indexing="ij"))
    phase = (points[:, :1] * kx + points[:, 1:2] * ky + points[:, 2:] * kz) % GRID
    angle = phase * (2.0 * math.pi / GRID)
    table = np.zeros((POINTS_PAD, 2 * FREQ), np.float64)
    table[: len(points), :FREQ] = np.cos(angle)
    table[: len(points), FREQ:] = -np.sin(angle)
    table = np.where(np.abs(table) < 1e-9, 0.0, table)
    high = table.astype(ml_dtypes.bfloat16)
    low = (table - high.astype(np.float64)).astype(ml_dtypes.bfloat16)
    edge_plane = (kz == 0) | (kz == GRID // 2)
    factor = np.where(edge_plane, 1.0, 2.0) / GRID**3 * np.where((kx + ky + kz) % 2 == 0, 1.0, -1.0)
    factor = np.concatenate([factor, factor]).astype(np.float32)[None, :]
    return np.concatenate([high, low], axis=0), factor


def source_rows(comp_count):
    return (2 * comp_count * MAIN + TAIL * 8) | 1


def source_row(comp_count, which, tile):
    if tile < MAIN:
        return which * MAIN + tile
    return 2 * comp_count * MAIN + (tile - MAIN) * 8 + which


def pack_kernel(density, send_list, halo_list, *outs):
    peers, cap = send_list.shape
    rim = halo_list.shape[1]
    member = lax.axis_index("dev")
    parity = lax.rem(lax.axis_index("group"), 2)
    to_near, *to_far, to_first, to_second = outs
    for c in range(density.shape[0]):
        for e in range(cap):
            for part, k in enumerate((1, 3)):
                to_near[part, c, e : e + 1, :] = density[c, pl.ds(send_list[member ^ k, e], 1), :]
            for k, out in zip((2, *range(4, peers)), to_far):
                out[c, e : e + 1, :] = density[c, pl.ds(send_list[member ^ k, e], 1), :]
        for e in range(rim):
            to_first[c, e : e + 1, :] = density[c, pl.ds(halo_list[1 - parity, e], 1), :]
            to_second[c, e : e + 1, :] = density[c, pl.ds(halo_list[parity, e], 1), :]


def prepare_kernel(kernel_hat, hat):
    parts, count, _ = kernel_hat.shape

    def move(first, height):
        for part in range(parts):
            for j in range(TILES):
                x = kernel_hat[part, pl.ds(first, height), j * LANES : (j + 1) * LANES].astype(jnp.float32)
                for g in range(0, height, 8):
                    size = min(8, height - g)
                    piece = x[g : g + size]
                    row = (first + g) * HAT_ROWS + part * TILES + j
                    hat[pl.ds(row, size, stride=HAT_ROWS), :] = piece

    whole = count // 16

    @pl.loop(0, whole)
    def _(i):
        move(pl.multiple_of(i * 16, 16), 16)

    if count % 16:
        move(whole * 16, count % 16)


def forward_kernel(send_list, density, from_near, relayed, *refs):
    *from_far, from_first, from_second, table, main, rows = refs
    comp_count, box_count, surf = density.shape
    peers, cap = send_list.shape
    rim = from_first.shape[1]
    row_count = rows.shape[0]
    slots = row_count // comp_count
    pitch = source_rows(comp_count)
    f32, bf16 = jnp.float32, jnp.bfloat16

    member = lax.axis_index("dev")
    parity = lax.rem(lax.axis_index("group"), 2)
    rows[...] = jnp.zeros_like(rows)
    pieces = {1: from_near.at[0], 3: relayed.at[1]}
    pieces.update(zip((2, *range(4, peers)), from_far))
    for c in range(comp_count):
        base = c * slots
        rows[base : base + box_count, :surf] = density[c]
        base += box_count
        for e in range(cap):
            rows[pl.ds(base + member * cap + e, 1), :surf] = density[c, pl.ds(send_list[member, e], 1), :]
            for k, piece in pieces.items():
                rows[pl.ds(base + (member ^ k) * cap + e, 1), :surf] = piece[c, e : e + 1]
        base += peers * cap
        for e in range(rim):
            rows[pl.ds(base + (1 - parity) * rim + e, 1), :surf] = from_first[c, e : e + 1]
            rows[pl.ds(base + parity * rim + e, 1), :surf] = from_second[c, e : e + 1]

    value = rows[...]
    high = value.astype(bf16)
    low = (value - high.astype(f32)).astype(bf16)
    both = jnp.concatenate([high, low], axis=0)
    for n in range(2 * FREQ // CHUNK):
        columns = slice(n * CHUNK, (n + 1) * CHUNK)
        x = jnp.dot(both, table[:POINTS_PAD, columns], preferred_element_type=f32)
        x = x[:row_count] + x[row_count:]
        x = x + jnp.dot(high, table[POINTS_PAD:, columns], preferred_element_type=f32)
        x = x.astype(bf16).astype(f32)
        for m in range(CHUNK // LANES):
            part, j = divmod(n * (CHUNK // LANES) + m, TILES)
            for g in range(row_count // 8):
                piece = x[g * 8 : (g + 1) * 8, m * LANES : (m + 1) * LANES]
                c, s = divmod(g * 8, slots)
                row = source_row(comp_count, part * comp_count + c, j)
                main[pl.ds(s * pitch + row, 8, stride=pitch), :] = piece


def interact_kernel(comp_count, source, offset, hat, main, total, total_tail):
    box_count, list_count = source.shape
    pitch = source_rows(comp_count)
    f32 = jnp.float32
    plus = lax.broadcasted_iota(jnp.int32, (8, LANES), 0) < comp_count
    halves = MAIN // 8

    @pl.loop(0, box_count)
    def _(t):
        def pair(w, accs):
            s = source[t, w] * pitch
            o = offset[t, w] * HAT_ROWS
            k = [[hat[pl.ds(o + (r * TILES + 8 * h), 8), :] for h in range(halves)] for r in range(2)]
            accs = list(accs)
            at = 0
            for c in range(comp_count):
                for h in range(halves):
                    s_re = main[pl.ds(s + (source_row(comp_count, c, 8 * h)), 8), :]
                    s_im = main[pl.ds(s + (source_row(comp_count, comp_count + c, 8 * h)), 8), :]
                    accs[at] = accs[at] + (k[0][h] * s_re - k[1][h] * s_im)
                    accs[at + 1] = accs[at + 1] + (k[0][h] * s_im + k[1][h] * s_re)
                    at += 2
            for j in range(MAIN, TILES):
                x = main[pl.ds(s + source_row(comp_count, 0, j), 8), :]
                k_re = hat[pl.ds(o + j, 8, stride=0), :]
                k_im = hat[pl.ds(o + TILES + j, 8, stride=0), :]
                accs[at] = accs[at] + k_re * x
                accs[at + 1] = accs[at + 1] + k_im * x
                at += 2
            return tuple(accs)

        count = 2 * (comp_count * halves + TAIL)
        zero = jnp.zeros((8, LANES), f32)
        accs = lax.fori_loop(0, list_count, pair, (zero,) * count, unroll=4)
        at = 0
        for c in range(comp_count):
            for h in range(halves):
                for part in range(2):
                    row = (part * comp_count + c) * box_count + t
                    total[pl.ds(row * PITCH + 8 * h, 8), :] = accs[at + part]
                at += 2
        for j in range(TAIL):
            own, cross = accs[at], accs[at + 1]
            up = jnp.concatenate([cross[comp_count:], cross[:comp_count]], axis=0)
            down = jnp.concatenate([cross[-comp_count:], cross[:-comp_count]], axis=0)
            total_tail[j, pl.ds(t * TAIL_PITCH, 8), :] = jnp.where(plus, own - up, own + down)
            at += 2


def inverse_kernel(total, total_tail, table, factor, out):
    comp_count, box_count, surf = out.shape
    f32, bf16 = jnp.float32, jnp.bfloat16
    groups = box_count // 8
    count = comp_count * box_count
    nt = (((1,), (1,)), ((), ()))
    result = jnp.zeros((2 * POINTS_PAD, 2 * count), f32)
    for n in range(2 * FREQ // PIECE):
        lanes = []
        for m in range(PIECE // LANES):
            part, j = divmod(n * (PIECE // LANES) + m, TILES)
            pieces = []
            for c in range(comp_count):
                for g in range(groups):
                    if j < MAIN:
                        row = (part * comp_count + c) * box_count + g * 8
                        pieces.append(total[pl.ds(row * PITCH + j, 8, stride=PITCH), :])
                    else:
                        row = g * 8 * TAIL_PITCH + part * comp_count + c
                        pieces.append(total_tail[j - MAIN, pl.ds(row, 8, stride=TAIL_PITCH), :])
            lanes.append(jnp.concatenate(pieces, axis=0))
        columns = slice(n * PIECE, (n + 1) * PIECE)
        x = jnp.concatenate(lanes, axis=1) * factor[:, columns]
        high = x.astype(bf16)
        low = (x - high.astype(f32)).astype(bf16)
        both = jnp.concatenate([high, low], axis=0)
        result += lax.dot_general(table[:, columns], both, nt, preferred_element_type=f32)
    result = result[:POINTS_PAD, :count] + result[:POINTS_PAD, count:] + result[POINTS_PAD:, :count]
    result = result.T
    for c in range(comp_count):
        out[c] = result[c * box_count : (c + 1) * box_count, :surf]


def on_device(density, kernel_hat, send_list, halo_list, inter_src, inter_off):
    table, factor = transform_tables()
    box_count, comp_count, surf = density.shape
    _, peers, cap = send_list.shape
    rim = halo_list.shape[2]
    f32 = jnp.float32
    vmem = pl.BlockSpec(memory_space=pltpu.VMEM)
    smem = pl.BlockSpec(memory_space=pltpu.SMEM)
    density = density.transpose(1, 0, 2)

    boxes = jax.ShapeDtypeStruct((comp_count, cap, surf), f32)
    side = jax.ShapeDtypeStruct((comp_count, rim, surf), f32)
    to_near, *to_far, to_first, to_second = pl.pallas_call(
        pack_kernel,
        out_shape=(jax.ShapeDtypeStruct((2, *boxes.shape), f32),) + (boxes,) * (peers - 3) + (side,) * 2,
        in_specs=[vmem, smem, smem],
        out_specs=(vmem,) * peers,
        name="pack",
    )(density, send_list[0], halo_list[0])

    def swap(x, k):
        return lax.ppermute(x, "dev", [(i, i ^ k) for i in range(peers)])

    def swap_groups(x, start):
        pairs = [(i, i + 1) for i in range(start, lax.axis_size("group") - 1, 2)]
        return lax.ppermute(x, "group", pairs + [(j, i) for i, j in pairs])

    from_near = swap(to_near, 1)
    from_far = [swap(x, k) for x, k in zip(to_far, (2, *range(4, peers)))]
    from_first = swap_groups(to_first, 0)
    from_second = swap_groups(to_second, 1)
    by_part, near = lax.optimization_barrier((kernel_hat.transpose(1, 0, 2), from_near))
    relayed = swap(near, 2)

    offsets = kernel_hat.shape[0]
    hat = pl.pallas_call(
        prepare_kernel,
        out_shape=jax.ShapeDtypeStruct((offsets * HAT_ROWS + 8, LANES), f32),
        in_specs=[vmem],
        out_specs=vmem,
        compiler_params=pltpu.CompilerParams(vmem_limit_bytes=16 * 1024 * 1024),
        cost_estimate=pl.CostEstimate(flops=kernel_hat.size, bytes_accessed=6 * kernel_hat.size, transcendentals=0),
        name="prepare",
    )(by_part)

    slots = box_count + peers * cap + 2 * rim
    row_count = comp_count * slots
    params = pltpu.CompilerParams(vmem_limit_bytes=24 * 1024 * 1024)
    table = jnp.asarray(table)
    arrays = (send_list[0], density, from_near, relayed, *from_far, from_first, from_second, table)
    main = pl.pallas_call(
        forward_kernel,
        out_shape=jax.ShapeDtypeStruct((slots * source_rows(comp_count) + 8, LANES), f32),
        in_specs=[smem] + [vmem] * (len(arrays) - 1),
        out_specs=vmem,
        scratch_shapes=[pltpu.VMEM((row_count, POINTS_PAD), f32)],
        compiler_params=params,
        name="forward",
    )(*arrays)
    total, total_tail = pl.pallas_call(
        functools.partial(interact_kernel, comp_count),
        out_shape=(
            jax.ShapeDtypeStruct((2 * comp_count * box_count * PITCH, LANES), f32),
            jax.ShapeDtypeStruct((TAIL, (box_count + 2) * TAIL_PITCH, LANES), f32),
        ),
        in_specs=[smem, smem] + [vmem] * 2,
        out_specs=(vmem, vmem),
        compiler_params=params,
        name="interact",
    )(inter_src, inter_off, hat, main)
    potential = pl.pallas_call(
        inverse_kernel,
        out_shape=jax.ShapeDtypeStruct((comp_count, box_count, surf), f32),
        in_specs=[vmem] * 4,
        out_specs=vmem,
        compiler_params=params,
        name="inverse",
    )(total, total_tail, table, jnp.asarray(factor))
    return potential.transpose(1, 0, 2)


def solution(mesh):
    in_specs = (
        P(("group", "dev"), None, None),
        P(),
        P(("group", "dev"), None, None),
        P(("group", "dev"), None, None),
        P(("group", "dev"), None),
        P(("group", "dev"), None),
    )
    out_specs = P(("group", "dev"), None, None)
    return jax.shard_map(
        on_device, mesh=mesh, in_specs=in_specs, out_specs=out_specs, check_vma=False
    )
```

```python
import functools
import math

import jax
import jax.numpy as jnp
import ml_dtypes
import numpy as np
from jax import lax
from jax.experimental import pallas as pl
from jax.experimental.pallas import tpu as pltpu
from jax.sharding import PartitionSpec as P

ORDER = 6
GRID = 16
LANES = 128
HALF = GRID // 2 + 1
FREQ = GRID * GRID * HALF
TILES = FREQ // LANES
MAIN = 16
TAIL = TILES - MAIN
PITCH = MAIN + 1
TAIL_PITCH = 7
HAT_ROWS = 2 * TILES
POINTS_PAD = 160
CHUNK = 256
PIECE = 512


def surface_points(edge_count):
    points = [
        (i, j, k)
        for i in range(edge_count)
        for j in range(edge_count)
        for k in range(edge_count)
        if min(i, j, k) == 0 or max(i, j, k) == edge_count - 1
    ]
    return np.array(points, dtype=np.int64)


@functools.lru_cache(maxsize=None)
def transform_tables():
    points = surface_points(ORDER)
    kx, ky, kz = (a.reshape(-1) for a in np.meshgrid(np.arange(GRID), np.arange(GRID), np.arange(HALF), indexing="ij"))
    phase = (points[:, :1] * kx + points[:, 1:2] * ky + points[:, 2:] * kz) % GRID
    angle = phase * (2.0 * math.pi / GRID)
    table = np.zeros((POINTS_PAD, 2 * FREQ), np.float64)
    table[: len(points), :FREQ] = np.cos(angle)
    table[: len(points), FREQ:] = -np.sin(angle)
    table = np.where(np.abs(table) < 1e-9, 0.0, table)
    high = table.astype(ml_dtypes.bfloat16)
    low = (table - high.astype(np.float64)).astype(ml_dtypes.bfloat16)
    edge_plane = (kz == 0) | (kz == GRID // 2)
    factor = np.where(edge_plane, 1.0, 2.0) / GRID**3 * np.where((kx + ky + kz) % 2 == 0, 1.0, -1.0)
    factor = np.concatenate([factor, factor]).astype(np.float32)[None, :]
    return np.concatenate([high, low], axis=0), factor


def source_rows(comp_count):
    return (2 * comp_count * MAIN + TAIL * 8) | 1


def source_row(comp_count, which, tile):
    if tile < MAIN:
        return which * MAIN + tile
    return 2 * comp_count * MAIN + (tile - MAIN) * 8 + which


def pack_kernel(density, send_list, halo_list, *outs):
    peers, cap = send_list.shape
    rim = halo_list.shape[1]
    member = lax.axis_index("dev")
    parity = lax.rem(lax.axis_index("group"), 2)
    to_near, *to_far, to_first, to_second = outs
    for c in range(density.shape[0]):
        for e in range(cap):
            for part, k in enumerate((1, 3)):
                to_near[part, c, e : e + 1, :] = density[c, pl.ds(send_list[member ^ k, e], 1), :]
            for k, out in zip((2, *range(4, peers)), to_far):
                out[c, e : e + 1, :] = density[c, pl.ds(send_list[member ^ k, e], 1), :]
        for e in range(rim):
            to_first[c, e : e + 1, :] = density[c, pl.ds(halo_list[1 - parity, e], 1), :]
            to_second[c, e : e + 1, :] = density[c, pl.ds(halo_list[parity, e], 1), :]


def prepare_kernel(kernel_hat, hat):
    count = kernel_hat.shape[0]
    step = 8

    def move(first, height):
        for j in range(TILES):
            hat[pl.ds(first, height), j] = kernel_hat[pl.ds(first, height), :, j * LANES : (j + 1) * LANES].astype(jnp.float32)

    @pl.loop(0, count // step)
    def _(i):
        move(i * step, step)

    if count % step:
        move(count - count % step, count % step)


def forward_kernel(send_list, density, from_near, relayed, *refs):
    *from_far, from_first, from_second, table, main, rows = refs
    comp_count, box_count, surf = density.shape
    peers, cap = send_list.shape
    rim = from_first.shape[1]
    row_count = rows.shape[0]
    slots = row_count // comp_count
    pitch = source_rows(comp_count)
    f32, bf16 = jnp.float32, jnp.bfloat16

    member = lax.axis_index("dev")
    parity = lax.rem(lax.axis_index("group"), 2)
    rows[...] = jnp.zeros_like(rows)
    pieces = {1: from_near.at[0], 3: relayed.at[1]}
    pieces.update(zip((2, *range(4, peers)), from_far))
    for c in range(comp_count):
        base = c * slots
        rows[base : base + box_count, :surf] = density[c]
        base += box_count
        for e in range(cap):
            rows[pl.ds(base + member * cap + e, 1), :surf] = density[c, pl.ds(send_list[member, e], 1), :]
            for k, piece in pieces.items():
                rows[pl.ds(base + (member ^ k) * cap + e, 1), :surf] = piece[c, e : e + 1]
        base += peers * cap
        for e in range(rim):
            rows[pl.ds(base + (1 - parity) * rim + e, 1), :surf] = from_first[c, e : e + 1]
            rows[pl.ds(base + parity * rim + e, 1), :surf] = from_second[c, e : e + 1]

    value = rows[...]
    high = value.astype(bf16)
    low = (value - high.astype(f32)).astype(bf16)
    both = jnp.concatenate([high, low], axis=0)
    for n in range(2 * FREQ // CHUNK):
        columns = slice(n * CHUNK, (n + 1) * CHUNK)
        x = jnp.dot(both, table[:POINTS_PAD, columns], preferred_element_type=f32)
        x = x[:row_count] + x[row_count:]
        x = x + jnp.dot(high, table[POINTS_PAD:, columns], preferred_element_type=f32)
        x = x.astype(bf16).astype(f32)
        for m in range(CHUNK // LANES):
            part, j = divmod(n * (CHUNK // LANES) + m, TILES)
            for g in range(row_count // 8):
                piece = x[g * 8 : (g + 1) * 8, m * LANES : (m + 1) * LANES]
                c, s = divmod(g * 8, slots)
                row = source_row(comp_count, part * comp_count + c, j)
                main[pl.ds(s * pitch + row, 8, stride=pitch), :] = piece


def interact_kernel(comp_count, source, offset, hat, main, total, total_tail):
    box_count, list_count = source.shape
    pitch = source_rows(comp_count)
    f32 = jnp.float32
    plus = lax.broadcasted_iota(jnp.int32, (8, LANES), 0) < comp_count
    halves = MAIN // 8

    flat = hat.reshape(-1, LANES)
    zero = jnp.zeros((8, LANES), f32)

    @pl.loop(0, box_count)
    def _(t):
        for h in range(halves):
            def pair(w, accs):
                s = source[t, w] * pitch
                o = offset[t, w] * HAT_ROWS
                k_re = flat[pl.ds(o + 16 * h, 8, stride=2), :]
                k_im = flat[pl.ds(o + (16 * h + 1), 8, stride=2), :]
                done = []
                for c in range(comp_count):
                    s_re = main[pl.ds(s + (source_row(comp_count, c, 8 * h)), 8), :]
                    s_im = main[pl.ds(s + (source_row(comp_count, comp_count + c, 8 * h)), 8), :]
                    done.append(accs[2 * c] + (k_re * s_re - k_im * s_im))
                    done.append(accs[2 * c + 1] + (k_re * s_im + k_im * s_re))
                return tuple(done)

            accs = lax.fori_loop(0, list_count, pair, (zero,) * (2 * comp_count), unroll=8)
            for c in range(comp_count):
                for part in range(2):
                    row = (part * comp_count + c) * box_count + t
                    total[pl.ds(row * PITCH + 8 * h, 8), :] = accs[2 * c + part]

        def pair_tail(w, accs):
            s = source[t, w] * pitch
            o = offset[t, w] * HAT_ROWS
            done = []
            for j in range(MAIN, TILES):
                x = main[pl.ds(s + source_row(comp_count, 0, j), 8), :]
                done.append(accs[len(done)] + flat[pl.ds(o + 2 * j, 8, stride=0), :] * x)
                done.append(accs[len(done)] + flat[pl.ds(o + (2 * j + 1), 8, stride=0), :] * x)
            return tuple(done)

        accs = lax.fori_loop(0, list_count, pair_tail, (zero,) * (2 * TAIL), unroll=8)
        for j in range(TAIL):
            own, cross = accs[2 * j], accs[2 * j + 1]
            up = jnp.concatenate([cross[comp_count:], cross[:comp_count]], axis=0)
            down = jnp.concatenate([cross[-comp_count:], cross[:-comp_count]], axis=0)
            total_tail[j, pl.ds(t * TAIL_PITCH, 8), :] = jnp.where(plus, own - up, own + down)


def inverse_kernel(total, total_tail, table, factor, out):
    comp_count, box_count, surf = out.shape
    f32, bf16 = jnp.float32, jnp.bfloat16
    groups = box_count // 8
    count = comp_count * box_count
    nt = (((1,), (1,)), ((), ()))
    result = jnp.zeros((2 * POINTS_PAD, 2 * count), f32)
    for n in range(2 * FREQ // PIECE):
        lanes = []
        for m in range(PIECE // LANES):
            part, j = divmod(n * (PIECE // LANES) + m, TILES)
            pieces = []
            for c in range(comp_count):
                for g in range(groups):
                    if j < MAIN:
                        row = (part * comp_count + c) * box_count + g * 8
                        pieces.append(total[pl.ds(row * PITCH + j, 8, stride=PITCH), :])
                    else:
                        row = g * 8 * TAIL_PITCH + part * comp_count + c
                        pieces.append(total_tail[j - MAIN, pl.ds(row, 8, stride=TAIL_PITCH), :])
            lanes.append(jnp.concatenate(pieces, axis=0))
        columns = slice(n * PIECE, (n + 1) * PIECE)
        x = jnp.concatenate(lanes, axis=1) * factor[:, columns]
        high = x.astype(bf16)
        low = (x - high.astype(f32)).astype(bf16)
        both = jnp.concatenate([high, low], axis=0)
        result += lax.dot_general(table[:, columns], both, nt, preferred_element_type=f32)
    result = result[:POINTS_PAD, :count] + result[:POINTS_PAD, count:] + result[POINTS_PAD:, :count]
    result = result.T
    for c in range(comp_count):
        out[c] = result[c * box_count : (c + 1) * box_count, :surf]


def on_device(density, kernel_hat, send_list, halo_list, inter_src, inter_off):
    table, factor = transform_tables()
    box_count, comp_count, surf = density.shape
    _, peers, cap = send_list.shape
    rim = halo_list.shape[2]
    f32 = jnp.float32
    vmem = pl.BlockSpec(memory_space=pltpu.VMEM)
    smem = pl.BlockSpec(memory_space=pltpu.SMEM)
    density = density.transpose(1, 0, 2)

    boxes = jax.ShapeDtypeStruct((comp_count, cap, surf), f32)
    side = jax.ShapeDtypeStruct((comp_count, rim, surf), f32)
    to_near, *to_far, to_first, to_second = pl.pallas_call(
        pack_kernel,
        out_shape=(jax.ShapeDtypeStruct((2, *boxes.shape), f32),) + (boxes,) * (peers - 3) + (side,) * 2,
        in_specs=[vmem, smem, smem],
        out_specs=(vmem,) * peers,
        name="pack",
    )(density, send_list[0], halo_list[0])

    def swap(x, k):
        return lax.ppermute(x, "dev", [(i, i ^ k) for i in range(peers)])

    def swap_groups(x, start):
        pairs = [(i, i + 1) for i in range(start, lax.axis_size("group") - 1, 2)]
        return lax.ppermute(x, "group", pairs + [(j, i) for i, j in pairs])

    from_near = swap(to_near, 1)
    from_far = [swap(x, k) for x, k in zip(to_far, (2, *range(4, peers)))]
    from_first = swap_groups(to_first, 0)
    from_second = swap_groups(to_second, 1)
    offsets = kernel_hat.shape[0]
    hat = pl.pallas_call(
        prepare_kernel,
        out_shape=jax.ShapeDtypeStruct((offsets, TILES, 2, LANES), f32),
        in_specs=[vmem],
        out_specs=vmem,
        compiler_params=pltpu.CompilerParams(vmem_limit_bytes=16 * 1024 * 1024),
        cost_estimate=pl.CostEstimate(flops=kernel_hat.size, bytes_accessed=6 * kernel_hat.size, transcendentals=0),
        name="prepare",
    )(kernel_hat)
    hat, near = lax.optimization_barrier((hat, from_near))
    relayed = swap(near, 2)

    slots = box_count + peers * cap + 2 * rim
    row_count = comp_count * slots
    params = pltpu.CompilerParams(vmem_limit_bytes=24 * 1024 * 1024)
    table = jnp.asarray(table)
    arrays = (send_list[0], density, from_near, relayed, *from_far, from_first, from_second, table)
    main = pl.pallas_call(
        forward_kernel,
        out_shape=jax.ShapeDtypeStruct((slots * source_rows(comp_count) + 8, LANES), f32),
        in_specs=[smem] + [vmem] * (len(arrays) - 1),
        out_specs=vmem,
        scratch_shapes=[pltpu.VMEM((row_count, POINTS_PAD), f32)],
        compiler_params=params,
        name="forward",
    )(*arrays)
    total, total_tail = pl.pallas_call(
        functools.partial(interact_kernel, comp_count),
        out_shape=(
            jax.ShapeDtypeStruct((2 * comp_count * box_count * PITCH, LANES), f32),
            jax.ShapeDtypeStruct((TAIL, (box_count + 2) * TAIL_PITCH, LANES), f32),
        ),
        in_specs=[smem, smem] + [vmem] * 2,
        out_specs=(vmem, vmem),
        compiler_params=params,
        name="interact",
    )(inter_src, inter_off, hat, main)
    potential = pl.pallas_call(
        inverse_kernel,
        out_shape=jax.ShapeDtypeStruct((comp_count, box_count, surf), f32),
        in_specs=[vmem] * 4,
        out_specs=vmem,
        compiler_params=params,
        name="inverse",
    )(total, total_tail, table, jnp.asarray(factor))
    return potential.transpose(1, 0, 2)


def solution(mesh):
    in_specs = (
        P(("group", "dev"), None, None),
        P(),
        P(("group", "dev"), None, None),
        P(("group", "dev"), None, None),
        P(("group", "dev"), None),
        P(("group", "dev"), None),
    )
    out_specs = P(("group", "dev"), None, None)
    return jax.shard_map(
        on_device, mesh=mesh, in_specs=in_specs, out_specs=out_specs, check_vma=False
    )
```

```python
import functools
import math

import jax
import jax.numpy as jnp
import ml_dtypes
import numpy as np
from jax import lax
from jax.experimental import pallas as pl
from jax.experimental.pallas import tpu as pltpu
from jax.sharding import PartitionSpec as P

ORDER = 6
GRID = 16
LANES = 128
HALF = GRID // 2 + 1
FREQ = GRID * GRID * HALF
TILES = FREQ // LANES
MAIN = 16
TAIL = TILES - MAIN
PITCH = MAIN + 1
TAIL_PITCH = 7
HAT_ROWS = 2 * TILES + 1
POINTS_PAD = 160
CHUNK = 256
PIECE = 512
UNROLL = 8


def surface_points(edge_count):
    points = [
        (i, j, k)
        for i in range(edge_count)
        for j in range(edge_count)
        for k in range(edge_count)
        if min(i, j, k) == 0 or max(i, j, k) == edge_count - 1
    ]
    return np.array(points, dtype=np.int64)


@functools.lru_cache(maxsize=None)
def transform_tables():
    points = surface_points(ORDER)
    kx, ky, kz = (a.reshape(-1) for a in np.meshgrid(np.arange(GRID), np.arange(GRID), np.arange(HALF), indexing="ij"))
    phase = (points[:, :1] * kx + points[:, 1:2] * ky + points[:, 2:] * kz) % GRID
    angle = phase * (2.0 * math.pi / GRID)
    table = np.zeros((POINTS_PAD, 2 * FREQ), np.float64)
    table[: len(points), :FREQ] = np.cos(angle)
    table[: len(points), FREQ:] = -np.sin(angle)
    table = np.where(np.abs(table) < 1e-9, 0.0, table)
    high = table.astype(ml_dtypes.bfloat16)
    low = (table - high.astype(np.float64)).astype(ml_dtypes.bfloat16)
    edge_plane = (kz == 0) | (kz == GRID // 2)
    factor = np.where(edge_plane, 1.0, 2.0) / GRID**3 * np.where((kx + ky + kz) % 2 == 0, 1.0, -1.0)
    factor = np.concatenate([factor, factor]).astype(np.float32)[None, :]
    return np.concatenate([high, low], axis=0), factor


def source_rows(comp_count):
    return (2 * comp_count * MAIN + TAIL * 8) | 1


def source_row(comp_count, which, tile):
    if tile < MAIN:
        return which * MAIN + tile
    return 2 * comp_count * MAIN + (tile - MAIN) * 8 + which


def pack_kernel(density, send_list, halo_list, *outs):
    peers, cap = send_list.shape
    rim = halo_list.shape[1]
    member = lax.axis_index("dev")
    parity = lax.rem(lax.axis_index("group"), 2)
    to_near, *to_far, to_first, to_second = outs
    for c in range(density.shape[0]):
        for e in range(cap):
            for part, k in enumerate((1, 3)):
                to_near[part, c, e : e + 1, :] = density[c, pl.ds(send_list[member ^ k, e], 1), :]
            for k, out in zip((2, *range(4, peers)), to_far):
                out[c, e : e + 1, :] = density[c, pl.ds(send_list[member ^ k, e], 1), :]
        for e in range(rim):
            to_first[c, e : e + 1, :] = density[c, pl.ds(halo_list[1 - parity, e], 1), :]
            to_second[c, e : e + 1, :] = density[c, pl.ds(halo_list[parity, e], 1), :]


def prepare_kernel(kernel_hat, hat):
    parts, count, _ = kernel_hat.shape

    def move(first, height):
        for part in range(parts):
            for j in range(TILES):
                x = kernel_hat[part, pl.ds(first, height), j * LANES : (j + 1) * LANES].astype(jnp.float32)
                for g in range(0, height, 8):
                    size = min(8, height - g)
                    piece = x[g : g + size]
                    row = (first + g) * HAT_ROWS + part * TILES + j
                    hat[pl.ds(row, size, stride=HAT_ROWS), :] = piece

    whole = count // 16

    @pl.loop(0, whole)
    def _(i):
        move(pl.multiple_of(i * 16, 16), 16)

    if count % 16:
        move(whole * 16, count % 16)


def forward_kernel(send_list, density, from_near, relayed, *refs):
    *from_far, from_first, from_second, table, main, rows = refs
    comp_count, box_count, surf = density.shape
    peers, cap = send_list.shape
    rim = from_first.shape[1]
    row_count = rows.shape[0]
    slots = row_count // comp_count
    pitch = source_rows(comp_count)
    f32, bf16 = jnp.float32, jnp.bfloat16

    member = lax.axis_index("dev")
    parity = lax.rem(lax.axis_index("group"), 2)
    rows[...] = jnp.zeros_like(rows)
    pieces = {1: from_near.at[0], 3: relayed.at[1]}
    pieces.update(zip((2, *range(4, peers)), from_far))
    for c in range(comp_count):
        base = c * slots
        rows[base : base + box_count, :surf] = density[c]
        base += box_count
        for e in range(cap):
            rows[pl.ds(base + member * cap + e, 1), :surf] = density[c, pl.ds(send_list[member, e], 1), :]
            for k, piece in pieces.items():
                rows[pl.ds(base + (member ^ k) * cap + e, 1), :surf] = piece[c, e : e + 1]
        base += peers * cap
        for e in range(rim):
            rows[pl.ds(base + (1 - parity) * rim + e, 1), :surf] = from_first[c, e : e + 1]
            rows[pl.ds(base + parity * rim + e, 1), :surf] = from_second[c, e : e + 1]

    value = rows[...]
    high = value.astype(bf16)
    low = (value - high.astype(f32)).astype(bf16)
    both = jnp.concatenate([high, low], axis=0)
    for n in range(2 * FREQ // CHUNK):
        columns = slice(n * CHUNK, (n + 1) * CHUNK)
        x = jnp.dot(both, table[:POINTS_PAD, columns], preferred_element_type=f32)
        x = x[:row_count] + x[row_count:]
        x = x + jnp.dot(high, table[POINTS_PAD:, columns], preferred_element_type=f32)
        x = x.astype(bf16).astype(f32)
        for m in range(CHUNK // LANES):
            part, j = divmod(n * (CHUNK // LANES) + m, TILES)
            for g in range(row_count // 8):
                piece = x[g * 8 : (g + 1) * 8, m * LANES : (m + 1) * LANES]
                c, s = divmod(g * 8, slots)
                row = source_row(comp_count, part * comp_count + c, j)
                main[pl.ds(s * pitch + row, 8, stride=pitch), :] = piece


def interact_kernel(comp_count, source, offset, hat, main, total, total_tail):
    box_count, list_count = source.shape
    pitch = source_rows(comp_count)
    f32 = jnp.float32
    plus = lax.broadcasted_iota(jnp.int32, (8, LANES), 0) < comp_count
    halves = MAIN // 8

    @pl.loop(0, box_count)
    def _(t):
        def rows_of(first):
            return tuple(
                (source[t, first + u] * pitch, offset[t, first + u] * HAT_ROWS) for u in range(UNROLL)
            )

        def pair(s, o, accs):
            k = [[hat[pl.ds(o + (r * TILES + 8 * h), 8), :] for h in range(halves)] for r in range(2)]
            accs = list(accs)
            at = 0
            for c in range(comp_count):
                for h in range(halves):
                    s_re = main[pl.ds(s + (source_row(comp_count, c, 8 * h)), 8), :]
                    s_im = main[pl.ds(s + (source_row(comp_count, comp_count + c, 8 * h)), 8), :]
                    accs[at] = accs[at] + (k[0][h] * s_re - k[1][h] * s_im)
                    accs[at + 1] = accs[at + 1] + (k[0][h] * s_im + k[1][h] * s_re)
                    at += 2
            for j in range(MAIN, TILES):
                x = main[pl.ds(s + source_row(comp_count, 0, j), 8), :]
                k_re = hat[pl.ds(o + j, 8, stride=0), :]
                k_im = hat[pl.ds(o + TILES + j, 8, stride=0), :]
                accs[at] = accs[at] + k_re * x
                accs[at + 1] = accs[at + 1] + k_im * x
                at += 2
            return tuple(accs)

        count = 2 * (comp_count * halves + TAIL)
        zero = jnp.zeros((8, LANES), f32)

        def block(i, carry):
            accs, here = carry
            ahead = rows_of(lax.rem((i + 1) * UNROLL, list_count))
            for s, o in here:
                accs = pair(s, o, accs)
            return accs, ahead

        accs, _ = lax.fori_loop(0, list_count // UNROLL, block, ((zero,) * count, rows_of(0)))
        at = 0
        for c in range(comp_count):
            for h in range(halves):
                for part in range(2):
                    row = (part * comp_count + c) * box_count + t
                    total[pl.ds(row * PITCH + 8 * h, 8), :] = accs[at + part]
                at += 2
        for j in range(TAIL):
            own, cross = accs[at], accs[at + 1]
            up = jnp.concatenate([cross[comp_count:], cross[:comp_count]], axis=0)
            down = jnp.concatenate([cross[-comp_count:], cross[:-comp_count]], axis=0)
            total_tail[j, pl.ds(t * TAIL_PITCH, 8), :] = jnp.where(plus, own - up, own + down)
            at += 2


def inverse_kernel(total, total_tail, table, factor, out):
    comp_count, box_count, surf = out.shape
    f32, bf16 = jnp.float32, jnp.bfloat16
    groups = box_count // 8
    count = comp_count * box_count
    nt = (((1,), (1,)), ((), ()))
    result = jnp.zeros((2 * POINTS_PAD, 2 * count), f32)
    for n in range(2 * FREQ // PIECE):
        lanes = []
        for m in range(PIECE // LANES):
            part, j = divmod(n * (PIECE // LANES) + m, TILES)
            pieces = []
            for c in range(comp_count):
                for g in range(groups):
                    if j < MAIN:
                        row = (part * comp_count + c) * box_count + g * 8
                        pieces.append(total[pl.ds(row * PITCH + j, 8, stride=PITCH), :])
                    else:
                        row = g * 8 * TAIL_PITCH + part * comp_count + c
                        pieces.append(total_tail[j - MAIN, pl.ds(row, 8, stride=TAIL_PITCH), :])
            lanes.append(jnp.concatenate(pieces, axis=0))
        columns = slice(n * PIECE, (n + 1) * PIECE)
        x = jnp.concatenate(lanes, axis=1) * factor[:, columns]
        high = x.astype(bf16)
        low = (x - high.astype(f32)).astype(bf16)
        both = jnp.concatenate([high, low], axis=0)
        result += lax.dot_general(table[:, columns], both, nt, preferred_element_type=f32)
    result = result[:POINTS_PAD, :count] + result[:POINTS_PAD, count:] + result[POINTS_PAD:, :count]
    result = result.T
    for c in range(comp_count):
        out[c] = result[c * box_count : (c + 1) * box_count, :surf]


def on_device(density, kernel_hat, send_list, halo_list, inter_src, inter_off):
    table, factor = transform_tables()
    box_count, comp_count, surf = density.shape
    _, peers, cap = send_list.shape
    rim = halo_list.shape[2]
    f32 = jnp.float32
    vmem = pl.BlockSpec(memory_space=pltpu.VMEM)
    smem = pl.BlockSpec(memory_space=pltpu.SMEM)
    density = density.transpose(1, 0, 2)

    boxes = jax.ShapeDtypeStruct((comp_count, cap, surf), f32)
    side = jax.ShapeDtypeStruct((comp_count, rim, surf), f32)
    to_near, *to_far, to_first, to_second = pl.pallas_call(
        pack_kernel,
        out_shape=(jax.ShapeDtypeStruct((2, *boxes.shape), f32),) + (boxes,) * (peers - 3) + (side,) * 2,
        in_specs=[vmem, smem, smem],
        out_specs=(vmem,) * peers,
        compiler_params=pltpu.CompilerParams(vmem_limit_bytes=4 * 1024 * 1024),
        name="pack",
    )(density, send_list[0], halo_list[0])

    def swap(x, k):
        return lax.ppermute(x, "dev", [(i, i ^ k) for i in range(peers)])

    def swap_groups(x, start):
        pairs = [(i, i + 1) for i in range(start, lax.axis_size("group") - 1, 2)]
        return lax.ppermute(x, "group", pairs + [(j, i) for i, j in pairs])

    from_near = swap(to_near, 1)
    from_far = [swap(x, k) for x, k in zip(to_far, (2, *range(4, peers)))]
    from_first = swap_groups(to_first, 0)
    from_second = swap_groups(to_second, 1)
    by_part, near = lax.optimization_barrier((kernel_hat.transpose(1, 0, 2), from_near))
    relayed = swap(near, 2)

    offsets = kernel_hat.shape[0]
    hat = pl.pallas_call(
        prepare_kernel,
        out_shape=jax.ShapeDtypeStruct((offsets * HAT_ROWS + 8, LANES), f32),
        in_specs=[vmem],
        out_specs=vmem,
        compiler_params=pltpu.CompilerParams(vmem_limit_bytes=16 * 1024 * 1024),
        cost_estimate=pl.CostEstimate(flops=kernel_hat.size, bytes_accessed=6 * kernel_hat.size, transcendentals=0),
        name="prepare",
    )(by_part)

    slots = box_count + peers * cap + 2 * rim
    row_count = comp_count * slots
    params = pltpu.CompilerParams(vmem_limit_bytes=24 * 1024 * 1024)
    table = jnp.asarray(table)
    arrays = (send_list[0], density, from_near, relayed, *from_far, from_first, from_second, table)
    main = pl.pallas_call(
        forward_kernel,
        out_shape=jax.ShapeDtypeStruct((slots * source_rows(comp_count) + 8, LANES), f32),
        in_specs=[smem] + [vmem] * (len(arrays) - 1),
        out_specs=vmem,
        scratch_shapes=[pltpu.VMEM((row_count, POINTS_PAD), f32)],
        compiler_params=params,
        name="forward",
    )(*arrays)
    total, total_tail = pl.pallas_call(
        functools.partial(interact_kernel, comp_count),
        out_shape=(
            jax.ShapeDtypeStruct((2 * comp_count * box_count * PITCH, LANES), f32),
            jax.ShapeDtypeStruct((TAIL, (box_count + 2) * TAIL_PITCH, LANES), f32),
        ),
        in_specs=[smem, smem] + [vmem] * 2,
        out_specs=(vmem, vmem),
        compiler_params=params,
        name="interact",
    )(inter_src, inter_off, hat, main)
    potential = pl.pallas_call(
        inverse_kernel,
        out_shape=jax.ShapeDtypeStruct((comp_count, box_count, surf), f32),
        in_specs=[vmem] * 4,
        out_specs=vmem,
        compiler_params=params,
        name="inverse",
    )(total, total_tail, table, jnp.asarray(factor))
    return potential.transpose(1, 0, 2)


def solution(mesh):
    in_specs = (
        P(("group", "dev"), None, None),
        P(),
        P(("group", "dev"), None, None),
        P(("group", "dev"), None, None),
        P(("group", "dev"), None),
        P(("group", "dev"), None),
    )
    out_specs = P(("group", "dev"), None, None)
    return jax.shard_map(
        on_device, mesh=mesh, in_specs=in_specs, out_specs=out_specs, check_vma=False
    )
```

```python
import functools
import math

import jax
import jax.numpy as jnp
import ml_dtypes
import numpy as np
from jax import lax
from jax.experimental import pallas as pl
from jax.experimental.pallas import tpu as pltpu
from jax.sharding import PartitionSpec as P

ORDER = 6
GRID = 16
LANES = 128
HALF = GRID // 2 + 1
FREQ = GRID * GRID * HALF
TILES = FREQ // LANES
MAIN = 16
TAIL = TILES - MAIN
PITCH = MAIN + 1
TAIL_PITCH = 7
HAT_ROWS = 2 * TILES + 1
POINTS_PAD = 160
CHUNK = 256
PIECE = 512


def surface_points(edge_count):
    points = [
        (i, j, k)
        for i in range(edge_count)
        for j in range(edge_count)
        for k in range(edge_count)
        if min(i, j, k) == 0 or max(i, j, k) == edge_count - 1
    ]
    return np.array(points, dtype=np.int64)


@functools.lru_cache(maxsize=None)
def transform_tables():
    points = surface_points(ORDER)
    kx, ky, kz = (a.reshape(-1) for a in np.meshgrid(np.arange(GRID), np.arange(GRID), np.arange(HALF), indexing="ij"))
    phase = (points[:, :1] * kx + points[:, 1:2] * ky + points[:, 2:] * kz) % GRID
    angle = phase * (2.0 * math.pi / GRID)
    table = np.zeros((POINTS_PAD, 2 * FREQ), np.float64)
    table[: len(points), :FREQ] = np.cos(angle)
    table[: len(points), FREQ:] = -np.sin(angle)
    table = np.where(np.abs(table) < 1e-9, 0.0, table)
    high = table.astype(ml_dtypes.bfloat16)
    low = (table - high.astype(np.float64)).astype(ml_dtypes.bfloat16)
    edge_plane = (kz == 0) | (kz == GRID // 2)
    factor = np.where(edge_plane, 1.0, 2.0) / GRID**3 * np.where((kx + ky + kz) % 2 == 0, 1.0, -1.0)
    factor = np.concatenate([factor, factor]).astype(np.float32)[None, :]
    return np.concatenate([high, low], axis=0), factor


def source_rows(comp_count):
    return (2 * comp_count * MAIN + TAIL * 8) | 1


def source_row(comp_count, which, tile):
    if tile < MAIN:
        return which * MAIN + tile
    return 2 * comp_count * MAIN + (tile - MAIN) * 8 + which


def pack_kernel(density, send_list, halo_list, *outs):
    peers, cap = send_list.shape
    rim = halo_list.shape[1]
    member = lax.axis_index("dev")
    parity = lax.rem(lax.axis_index("group"), 2)
    to_near, *to_far, to_first, to_second = outs
    for c in range(density.shape[0]):
        for e in range(cap):
            for part, k in enumerate((1, 3)):
                to_near[part, c, e : e + 1, :] = density[c, pl.ds(send_list[member ^ k, e], 1), :]
            for k, out in zip((2, *range(4, peers)), to_far):
                out[c, e : e + 1, :] = density[c, pl.ds(send_list[member ^ k, e], 1), :]
        for e in range(rim):
            to_first[c, e : e + 1, :] = density[c, pl.ds(halo_list[1 - parity, e], 1), :]
            to_second[c, e : e + 1, :] = density[c, pl.ds(halo_list[parity, e], 1), :]


def prepare_kernel(kernel_hat, hat):
    parts, count, _ = kernel_hat.shape

    def move(first, height):
        for part in range(parts):
            for j in range(TILES):
                x = kernel_hat[part, pl.ds(first, height), j * LANES : (j + 1) * LANES].astype(jnp.float32)
                for g in range(0, height, 8):
                    size = min(8, height - g)
                    piece = x[g : g + size]
                    row = (first + g) * HAT_ROWS + part * TILES + j
                    hat[pl.ds(row, size, stride=HAT_ROWS), :] = piece

    whole = count // 16

    @pl.loop(0, whole)
    def _(i):
        move(pl.multiple_of(i * 16, 16), 16)

    if count % 16:
        move(whole * 16, count % 16)


def forward_kernel(send_list, density, from_near, relayed, *refs):
    *from_far, from_first, from_second, table, main, rows = refs
    comp_count, box_count, surf = density.shape
    peers, cap = send_list.shape
    rim = from_first.shape[1]
    row_count = rows.shape[0]
    slots = row_count // comp_count
    pitch = source_rows(comp_count)
    f32, bf16 = jnp.float32, jnp.bfloat16

    member = lax.axis_index("dev")
    parity = lax.rem(lax.axis_index("group"), 2)
    rows[...] = jnp.zeros_like(rows)
    pieces = {1: from_near.at[0], 3: relayed.at[1]}
    pieces.update(zip((2, *range(4, peers)), from_far))
    for c in range(comp_count):
        base = c * slots
        rows[base : base + box_count, :surf] = density[c]
        base += box_count
        for e in range(cap):
            rows[pl.ds(base + member * cap + e, 1), :surf] = density[c, pl.ds(send_list[member, e], 1), :]
            for k, piece in pieces.items():
                rows[pl.ds(base + (member ^ k) * cap + e, 1), :surf] = piece[c, e : e + 1]
        base += peers * cap
        for e in range(rim):
            rows[pl.ds(base + (1 - parity) * rim + e, 1), :surf] = from_first[c, e : e + 1]
            rows[pl.ds(base + parity * rim + e, 1), :surf] = from_second[c, e : e + 1]

    value = rows[...]
    high = value.astype(bf16)
    low = (value - high.astype(f32)).astype(bf16)
    both = jnp.concatenate([high, low], axis=0)
    for n in range(2 * FREQ // CHUNK):
        columns = slice(n * CHUNK, (n + 1) * CHUNK)
        x = jnp.dot(both, table[:POINTS_PAD, columns], preferred_element_type=f32)
        x = x[:row_count] + x[row_count:]
        x = x + jnp.dot(high, table[POINTS_PAD:, columns], preferred_element_type=f32)
        x = x.astype(bf16).astype(f32)
        for m in range(CHUNK // LANES):
            part, j = divmod(n * (CHUNK // LANES) + m, TILES)
            for g in range(row_count // 8):
                piece = x[g * 8 : (g + 1) * 8, m * LANES : (m + 1) * LANES]
                c, s = divmod(g * 8, slots)
                row = source_row(comp_count, part * comp_count + c, j)
                main[pl.ds(s * pitch + row, 8, stride=pitch), :] = piece


def interact_kernel(comp_count, source, offset, hat, main, total, total_tail):
    box_count, list_count = source.shape
    pitch = source_rows(comp_count)
    f32 = jnp.float32
    plus = lax.broadcasted_iota(jnp.int32, (8, LANES), 0) < comp_count
    halves = MAIN // 8

    @pl.loop(0, box_count)
    def _(t):
        def pair(s, o, accs):
            k = [[hat[pl.ds(o + (r * TILES + 8 * h), 8), :] for h in range(halves)] for r in range(2)]
            accs = list(accs)
            at = 0
            for c in range(comp_count):
                for h in range(halves):
                    s_re = main[pl.ds(s + (source_row(comp_count, c, 8 * h)), 8), :]
                    s_im = main[pl.ds(s + (source_row(comp_count, comp_count + c, 8 * h)), 8), :]
                    accs[at] = accs[at] + (k[0][h] * s_re - k[1][h] * s_im)
                    accs[at + 1] = accs[at + 1] + (k[0][h] * s_im + k[1][h] * s_re)
                    at += 2
            for j in range(MAIN, TILES):
                x = main[pl.ds(s + source_row(comp_count, 0, j), 8), :]
                k_re = hat[pl.ds(o + j, 8, stride=0), :]
                k_im = hat[pl.ds(o + TILES + j, 8, stride=0), :]
                accs[at] = accs[at] + k_re * x
                accs[at + 1] = accs[at + 1] + k_im * x
                at += 2
            return tuple(accs)

        count = 2 * (comp_count * halves + TAIL)
        zero = jnp.zeros((8, LANES), f32)

        accs, last = (zero,) * count, t
        for w in range(list_count):
            s = source[t, w + jnp.minimum(last, 0)]
            last = offset[t, w + jnp.minimum(s, 0)]
            accs = pair(s * pitch, last * HAT_ROWS, accs)
        at = 0
        for c in range(comp_count):
            for h in range(halves):
                for part in range(2):
                    row = (part * comp_count + c) * box_count + t
                    total[pl.ds(row * PITCH + 8 * h, 8), :] = accs[at + part]
                at += 2
        for j in range(TAIL):
            own, cross = accs[at], accs[at + 1]
            up = jnp.concatenate([cross[comp_count:], cross[:comp_count]], axis=0)
            down = jnp.concatenate([cross[-comp_count:], cross[:-comp_count]], axis=0)
            total_tail[j, pl.ds(t * TAIL_PITCH, 8), :] = jnp.where(plus, own - up, own + down)
            at += 2


def inverse_kernel(total, total_tail, table, factor, out):
    comp_count, box_count, surf = out.shape
    f32, bf16 = jnp.float32, jnp.bfloat16
    groups = box_count // 8
    count = comp_count * box_count
    nt = (((1,), (1,)), ((), ()))
    result = jnp.zeros((2 * POINTS_PAD, 2 * count), f32)
    for n in range(2 * FREQ // PIECE):
        lanes = []
        for m in range(PIECE // LANES):
            part, j = divmod(n * (PIECE // LANES) + m, TILES)
            pieces = []
            for c in range(comp_count):
                for g in range(groups):
                    if j < MAIN:
                        row = (part * comp_count + c) * box_count + g * 8
                        pieces.append(total[pl.ds(row * PITCH + j, 8, stride=PITCH), :])
                    else:
                        row = g * 8 * TAIL_PITCH + part * comp_count + c
                        pieces.append(total_tail[j - MAIN, pl.ds(row, 8, stride=TAIL_PITCH), :])
            lanes.append(jnp.concatenate(pieces, axis=0))
        columns = slice(n * PIECE, (n + 1) * PIECE)
        x = jnp.concatenate(lanes, axis=1) * factor[:, columns]
        high = x.astype(bf16)
        low = (x - high.astype(f32)).astype(bf16)
        both = jnp.concatenate([high, low], axis=0)
        result += lax.dot_general(table[:, columns], both, nt, preferred_element_type=f32)
    result = result[:POINTS_PAD, :count] + result[:POINTS_PAD, count:] + result[POINTS_PAD:, :count]
    result = result.T
    for c in range(comp_count):
        out[c] = result[c * box_count : (c + 1) * box_count, :surf]


def on_device(density, kernel_hat, send_list, halo_list, inter_src, inter_off):
    table, factor = transform_tables()
    box_count, comp_count, surf = density.shape
    _, peers, cap = send_list.shape
    rim = halo_list.shape[2]
    f32 = jnp.float32
    vmem = pl.BlockSpec(memory_space=pltpu.VMEM)
    smem = pl.BlockSpec(memory_space=pltpu.SMEM)
    density = density.transpose(1, 0, 2)

    boxes = jax.ShapeDtypeStruct((comp_count, cap, surf), f32)
    side = jax.ShapeDtypeStruct((comp_count, rim, surf), f32)
    to_near, *to_far, to_first, to_second = pl.pallas_call(
        pack_kernel,
        out_shape=(jax.ShapeDtypeStruct((2, *boxes.shape), f32),) + (boxes,) * (peers - 3) + (side,) * 2,
        in_specs=[vmem, smem, smem],
        out_specs=(vmem,) * peers,
        name="pack",
    )(density, send_list[0], halo_list[0])

    def swap(x, k):
        return lax.ppermute(x, "dev", [(i, i ^ k) for i in range(peers)])

    def swap_groups(x, start):
        pairs = [(i, i + 1) for i in range(start, lax.axis_size("group") - 1, 2)]
        return lax.ppermute(x, "group", pairs + [(j, i) for i, j in pairs])

    from_near = swap(to_near, 1)
    from_far = [swap(x, k) for x, k in zip(to_far, (2, *range(4, peers)))]
    from_first = swap_groups(to_first, 0)
    from_second = swap_groups(to_second, 1)
    by_part, near = lax.optimization_barrier((kernel_hat.transpose(1, 0, 2), from_near))
    relayed = swap(near, 2)

    offsets = kernel_hat.shape[0]
    hat = pl.pallas_call(
        prepare_kernel,
        out_shape=jax.ShapeDtypeStruct((offsets * HAT_ROWS + 8, LANES), f32),
        in_specs=[vmem],
        out_specs=vmem,
        compiler_params=pltpu.CompilerParams(vmem_limit_bytes=16 * 1024 * 1024),
        cost_estimate=pl.CostEstimate(flops=kernel_hat.size, bytes_accessed=6 * kernel_hat.size, transcendentals=0),
        name="prepare",
    )(by_part)

    slots = box_count + peers * cap + 2 * rim
    row_count = comp_count * slots
    params = pltpu.CompilerParams(vmem_limit_bytes=24 * 1024 * 1024)
    table = jnp.asarray(table)
    arrays = (send_list[0], density, from_near, relayed, *from_far, from_first, from_second, table)
    main = pl.pallas_call(
        forward_kernel,
        out_shape=jax.ShapeDtypeStruct((slots * source_rows(comp_count) + 8, LANES), f32),
        in_specs=[smem] + [vmem] * (len(arrays) - 1),
        out_specs=vmem,
        scratch_shapes=[pltpu.VMEM((row_count, POINTS_PAD), f32)],
        compiler_params=params,
        name="forward",
    )(*arrays)
    total, total_tail = pl.pallas_call(
        functools.partial(interact_kernel, comp_count),
        out_shape=(
            jax.ShapeDtypeStruct((2 * comp_count * box_count * PITCH, LANES), f32),
            jax.ShapeDtypeStruct((TAIL, (box_count + 2) * TAIL_PITCH, LANES), f32),
        ),
        in_specs=[smem, smem] + [vmem] * 2,
        out_specs=(vmem, vmem),
        compiler_params=params,
        name="interact",
    )(inter_src, inter_off, hat, main)
    potential = pl.pallas_call(
        inverse_kernel,
        out_shape=jax.ShapeDtypeStruct((comp_count, box_count, surf), f32),
        in_specs=[vmem] * 4,
        out_specs=vmem,
        compiler_params=params,
        name="inverse",
    )(total, total_tail, table, jnp.asarray(factor))
    return potential.transpose(1, 0, 2)


def solution(mesh):
    in_specs = (
        P(("group", "dev"), None, None),
        P(),
        P(("group", "dev"), None, None),
        P(("group", "dev"), None, None),
        P(("group", "dev"), None),
        P(("group", "dev"), None),
    )
    out_specs = P(("group", "dev"), None, None)
    return jax.shard_map(
        on_device, mesh=mesh, in_specs=in_specs, out_specs=out_specs, check_vma=False
    )
```

```python
import functools
import math

import jax
import jax.numpy as jnp
import ml_dtypes
import numpy as np
from jax import lax
from jax.experimental import pallas as pl
from jax.experimental.pallas import tpu as pltpu
from jax.sharding import PartitionSpec as P

ORDER = 6
GRID = 16
LANES = 128
HALF = GRID // 2 + 1
FREQ = GRID * GRID * HALF
TILES = FREQ // LANES
MAIN = 16
TAIL = TILES - MAIN
PITCH = MAIN + 1
TAIL_PITCH = 7
HAT_ROWS = 2 * TILES + 1
POINTS_PAD = 160
CHUNK = 256
PIECE = 512
GROUP = 2


def surface_points(edge_count):
    points = [
        (i, j, k)
        for i in range(edge_count)
        for j in range(edge_count)
        for k in range(edge_count)
        if min(i, j, k) == 0 or max(i, j, k) == edge_count - 1
    ]
    return np.array(points, dtype=np.int64)


@functools.lru_cache(maxsize=None)
def transform_tables():
    points = surface_points(ORDER)
    kx, ky, kz = (a.reshape(-1) for a in np.meshgrid(np.arange(GRID), np.arange(GRID), np.arange(HALF), indexing="ij"))
    phase = (points[:, :1] * kx + points[:, 1:2] * ky + points[:, 2:] * kz) % GRID
    angle = phase * (2.0 * math.pi / GRID)
    table = np.zeros((POINTS_PAD, 2 * FREQ), np.float64)
    table[: len(points), :FREQ] = np.cos(angle)
    table[: len(points), FREQ:] = -np.sin(angle)
    table = np.where(np.abs(table) < 1e-9, 0.0, table)
    high = table.astype(ml_dtypes.bfloat16)
    low = (table - high.astype(np.float64)).astype(ml_dtypes.bfloat16)
    edge_plane = (kz == 0) | (kz == GRID // 2)
    factor = np.where(edge_plane, 1.0, 2.0) / GRID**3 * np.where((kx + ky + kz) % 2 == 0, 1.0, -1.0)
    factor = np.concatenate([factor, factor]).astype(np.float32)[None, :]
    return np.concatenate([high, low], axis=0), factor


def source_rows(comp_count):
    return (2 * comp_count * MAIN + TAIL * 8) | 1


def source_row(comp_count, which, tile):
    if tile < MAIN:
        return which * MAIN + tile
    return 2 * comp_count * MAIN + (tile - MAIN) * 8 + which


def pack_kernel(density, send_list, halo_list, *outs):
    peers, cap = send_list.shape
    rim = halo_list.shape[1]
    member = lax.axis_index("dev")
    parity = lax.rem(lax.axis_index("group"), 2)
    to_near, *to_far, to_first, to_second = outs
    for c in range(density.shape[0]):
        for e in range(cap):
            for part, k in enumerate((1, 3)):
                to_near[part, c, e : e + 1, :] = density[c, pl.ds(send_list[member ^ k, e], 1), :]
            for k, out in zip((2, *range(4, peers)), to_far):
                out[c, e : e + 1, :] = density[c, pl.ds(send_list[member ^ k, e], 1), :]
        for e in range(rim):
            to_first[c, e : e + 1, :] = density[c, pl.ds(halo_list[1 - parity, e], 1), :]
            to_second[c, e : e + 1, :] = density[c, pl.ds(halo_list[parity, e], 1), :]


def prepare_kernel(kernel_hat, hat):
    parts, count, _ = kernel_hat.shape

    def move(first, height):
        for part in range(parts):
            for j in range(TILES):
                x = kernel_hat[part, pl.ds(first, height), j * LANES : (j + 1) * LANES].astype(jnp.float32)
                for g in range(0, height, 8):
                    size = min(8, height - g)
                    piece = x[g : g + size]
                    row = (first + g) * HAT_ROWS + part * TILES + j
                    hat[pl.ds(row, size, stride=HAT_ROWS), :] = piece

    whole = count // 16

    @pl.loop(0, whole)
    def _(i):
        move(pl.multiple_of(i * 16, 16), 16)

    if count % 16:
        move(whole * 16, count % 16)


def forward_kernel(send_list, density, from_near, relayed, *refs):
    *from_far, from_first, from_second, table, main, rows = refs
    comp_count, box_count, surf = density.shape
    peers, cap = send_list.shape
    rim = from_first.shape[1]
    row_count = rows.shape[0]
    slots = row_count // comp_count
    pitch = source_rows(comp_count)
    f32, bf16 = jnp.float32, jnp.bfloat16

    member = lax.axis_index("dev")
    parity = lax.rem(lax.axis_index("group"), 2)
    rows[...] = jnp.zeros_like(rows)
    pieces = {1: from_near.at[0], 3: relayed.at[1]}
    pieces.update(zip((2, *range(4, peers)), from_far))
    for c in range(comp_count):
        base = c * slots
        rows[base : base + box_count, :surf] = density[c]
        base += box_count
        for e in range(cap):
            rows[pl.ds(base + member * cap + e, 1), :surf] = density[c, pl.ds(send_list[member, e], 1), :]
            for k, piece in pieces.items():
                rows[pl.ds(base + (member ^ k) * cap + e, 1), :surf] = piece[c, e : e + 1]
        base += peers * cap
        for e in range(rim):
            rows[pl.ds(base + (1 - parity) * rim + e, 1), :surf] = from_first[c, e : e + 1]
            rows[pl.ds(base + parity * rim + e, 1), :surf] = from_second[c, e : e + 1]

    value = rows[...]
    high = value.astype(bf16)
    low = (value - high.astype(f32)).astype(bf16)
    twice = jnp.concatenate([high, high], axis=1)
    for n in range(2 * FREQ // CHUNK):
        columns = slice(n * CHUNK, (n + 1) * CHUNK)
        x = jnp.dot(twice, table[:, columns], preferred_element_type=f32)
        x = x + jnp.dot(low, table[:POINTS_PAD, columns], preferred_element_type=f32)
        x = x.astype(bf16).astype(f32)
        for m in range(CHUNK // LANES):
            part, j = divmod(n * (CHUNK // LANES) + m, TILES)
            for g in range(row_count // 8):
                piece = x[g * 8 : (g + 1) * 8, m * LANES : (m + 1) * LANES]
                c, s = divmod(g * 8, slots)
                row = source_row(comp_count, part * comp_count + c, j)
                main[pl.ds(s * pitch + row, 8, stride=pitch), :] = piece


def interact_kernel(comp_count, source, offset, hat, main, total, total_tail):
    box_count, list_count = source.shape
    pitch = source_rows(comp_count)
    f32 = jnp.float32
    plus = lax.broadcasted_iota(jnp.int32, (8, LANES), 0) < comp_count
    halves = MAIN // 8

    @pl.loop(0, box_count)
    def _(t):
        def pair(s, o, accs):
            k = [[hat[pl.ds(o + (r * TILES + 8 * h), 8), :] for h in range(halves)] for r in range(2)]
            accs = list(accs)
            at = 0
            for c in range(comp_count):
                for h in range(halves):
                    s_re = main[pl.ds(s + (source_row(comp_count, c, 8 * h)), 8), :]
                    s_im = main[pl.ds(s + (source_row(comp_count, comp_count + c, 8 * h)), 8), :]
                    accs[at] = accs[at] + (k[0][h] * s_re - k[1][h] * s_im)
                    accs[at + 1] = accs[at + 1] + (k[0][h] * s_im + k[1][h] * s_re)
                    at += 2
            for j in range(MAIN, TILES):
                x = main[pl.ds(s + source_row(comp_count, 0, j), 8), :]
                k_re = hat[pl.ds(o + j, 8, stride=0), :]
                k_im = hat[pl.ds(o + TILES + j, 8, stride=0), :]
                accs[at] = accs[at] + k_re * x
                accs[at + 1] = accs[at + 1] + k_im * x
                at += 2
            return tuple(accs)

        count = 2 * (comp_count * halves + TAIL)
        zero = jnp.zeros((8, LANES), f32)

        accs, last = (zero,) * count, t
        for first in range(0, list_count, GROUP):
            ahead = jnp.minimum(last, 0)
            pairs = [(source[t, w + ahead], offset[t, w + ahead]) for w in range(first, first + GROUP)]
            last = pairs[-1][1]
            for s, o in pairs:
                accs = pair(s * pitch, o * HAT_ROWS, accs)
        at = 0
        for c in range(comp_count):
            for h in range(halves):
                for part in range(2):
                    row = (part * comp_count + c) * box_count + t
                    total[pl.ds(row * PITCH + 8 * h, 8), :] = accs[at + part]
                at += 2
        for j in range(TAIL):
            own, cross = accs[at], accs[at + 1]
            up = jnp.concatenate([cross[comp_count:], cross[:comp_count]], axis=0)
            down = jnp.concatenate([cross[-comp_count:], cross[:-comp_count]], axis=0)
            total_tail[j, pl.ds(t * TAIL_PITCH, 8), :] = jnp.where(plus, own - up, own + down)
            at += 2


def inverse_kernel(total, total_tail, table, factor, out):
    comp_count, box_count, surf = out.shape
    f32, bf16 = jnp.float32, jnp.bfloat16
    groups = box_count // 8
    count = comp_count * box_count
    nt = (((1,), (1,)), ((), ()))
    result = jnp.zeros((2 * POINTS_PAD, 2 * count), f32)
    for n in range(2 * FREQ // PIECE):
        lanes = []
        for m in range(PIECE // LANES):
            part, j = divmod(n * (PIECE // LANES) + m, TILES)
            pieces = []
            for c in range(comp_count):
                for g in range(groups):
                    if j < MAIN:
                        row = (part * comp_count + c) * box_count + g * 8
                        pieces.append(total[pl.ds(row * PITCH + j, 8, stride=PITCH), :])
                    else:
                        row = g * 8 * TAIL_PITCH + part * comp_count + c
                        pieces.append(total_tail[j - MAIN, pl.ds(row, 8, stride=TAIL_PITCH), :])
            lanes.append(jnp.concatenate(pieces, axis=0))
        columns = slice(n * PIECE, (n + 1) * PIECE)
        x = jnp.concatenate(lanes, axis=1) * factor[:, columns]
        high = x.astype(bf16)
        low = (x - high.astype(f32)).astype(bf16)
        both = jnp.concatenate([high, low], axis=0)
        result += lax.dot_general(table[:, columns], both, nt, preferred_element_type=f32)
    result = result[:POINTS_PAD, :count] + result[:POINTS_PAD, count:] + result[POINTS_PAD:, :count]
    result = result.T
    for c in range(comp_count):
        out[c] = result[c * box_count : (c + 1) * box_count, :surf]


def on_device(density, kernel_hat, send_list, halo_list, inter_src, inter_off):
    table, factor = transform_tables()
    box_count, comp_count, surf = density.shape
    _, peers, cap = send_list.shape
    rim = halo_list.shape[2]
    f32 = jnp.float32
    vmem = pl.BlockSpec(memory_space=pltpu.VMEM)
    smem = pl.BlockSpec(memory_space=pltpu.SMEM)
    density = density.transpose(1, 0, 2)

    boxes = jax.ShapeDtypeStruct((comp_count, cap, surf), f32)
    side = jax.ShapeDtypeStruct((comp_count, rim, surf), f32)
    to_near, *to_far, to_first, to_second = pl.pallas_call(
        pack_kernel,
        out_shape=(jax.ShapeDtypeStruct((2, *boxes.shape), f32),) + (boxes,) * (peers - 3) + (side,) * 2,
        in_specs=[vmem, smem, smem],
        out_specs=(vmem,) * peers,
        name="pack",
    )(density, send_list[0], halo_list[0])

    def swap(x, k):
        return lax.ppermute(x, "dev", [(i, i ^ k) for i in range(peers)])

    def swap_groups(x, start):
        pairs = [(i, i + 1) for i in range(start, lax.axis_size("group") - 1, 2)]
        return lax.ppermute(x, "group", pairs + [(j, i) for i, j in pairs])

    from_near = swap(to_near, 1)
    from_far = [swap(x, k) for x, k in zip(to_far, (2, *range(4, peers)))]
    from_first = swap_groups(to_first, 0)
    from_second = swap_groups(to_second, 1)
    by_part, near = lax.optimization_barrier((kernel_hat.transpose(1, 0, 2), from_near))
    relayed = swap(near, 2)

    offsets = kernel_hat.shape[0]
    hat = pl.pallas_call(
        prepare_kernel,
        out_shape=jax.ShapeDtypeStruct((offsets * HAT_ROWS + 8, LANES), f32),
        in_specs=[vmem],
        out_specs=vmem,
        compiler_params=pltpu.CompilerParams(vmem_limit_bytes=16 * 1024 * 1024),
        cost_estimate=pl.CostEstimate(flops=kernel_hat.size, bytes_accessed=6 * kernel_hat.size, transcendentals=0),
        name="prepare",
    )(by_part)

    slots = box_count + peers * cap + 2 * rim
    row_count = comp_count * slots
    params = pltpu.CompilerParams(vmem_limit_bytes=24 * 1024 * 1024)
    table = jnp.asarray(table)
    arrays = (send_list[0], density, from_near, relayed, *from_far, from_first, from_second, table)
    main = pl.pallas_call(
        forward_kernel,
        out_shape=jax.ShapeDtypeStruct((slots * source_rows(comp_count) + 8, LANES), f32),
        in_specs=[smem] + [vmem] * (len(arrays) - 1),
        out_specs=vmem,
        scratch_shapes=[pltpu.VMEM((row_count, POINTS_PAD), f32)],
        compiler_params=params,
        name="forward",
    )(*arrays)
    total, total_tail = pl.pallas_call(
        functools.partial(interact_kernel, comp_count),
        out_shape=(
            jax.ShapeDtypeStruct((2 * comp_count * box_count * PITCH, LANES), f32),
            jax.ShapeDtypeStruct((TAIL, (box_count + 2) * TAIL_PITCH, LANES), f32),
        ),
        in_specs=[smem, smem] + [vmem] * 2,
        out_specs=(vmem, vmem),
        compiler_params=params,
        name="interact",
    )(inter_src, inter_off, hat, main)
    potential = pl.pallas_call(
        inverse_kernel,
        out_shape=jax.ShapeDtypeStruct((comp_count, box_count, surf), f32),
        in_specs=[vmem] * 4,
        out_specs=vmem,
        compiler_params=params,
        name="inverse",
    )(total, total_tail, table, jnp.asarray(factor))
    return potential.transpose(1, 0, 2)


def solution(mesh):
    in_specs = (
        P(("group", "dev"), None, None),
        P(),
        P(("group", "dev"), None, None),
        P(("group", "dev"), None, None),
        P(("group", "dev"), None),
        P(("group", "dev"), None),
    )
    out_specs = P(("group", "dev"), None, None)
    return jax.shard_map(
        on_device, mesh=mesh, in_specs=in_specs, out_specs=out_specs, check_vma=False
    )
```

```python
import functools
import math

import jax
import jax.numpy as jnp
import ml_dtypes
import numpy as np
from jax import lax
from jax.experimental import pallas as pl
from jax.experimental.pallas import tpu as pltpu
from jax.sharding import PartitionSpec as P

ORDER = 6
GRID = 16
LANES = 128
HALF = GRID // 2 + 1
FREQ = GRID * GRID * HALF
TILES = FREQ // LANES
MAIN = 16
TAIL = TILES - MAIN
PITCH = MAIN + 1
TAIL_PITCH = 7
HAT_ROWS = 40
POINTS_PAD = 160
CHUNK = 768
PIECE = 512
UNROLL = 8


def surface_points(edge_count):
    points = [
        (i, j, k)
        for i in range(edge_count)
        for j in range(edge_count)
        for k in range(edge_count)
        if min(i, j, k) == 0 or max(i, j, k) == edge_count - 1
    ]
    return np.array(points, dtype=np.int64)


@functools.lru_cache(maxsize=None)
def transform_tables():
    points = surface_points(ORDER)
    kx, ky, kz = (a.reshape(-1) for a in np.meshgrid(np.arange(GRID), np.arange(GRID), np.arange(HALF), indexing="ij"))
    phase = (points[:, :1] * kx + points[:, 1:2] * ky + points[:, 2:] * kz) % GRID
    angle = phase * (2.0 * math.pi / GRID)
    table = np.zeros((POINTS_PAD, 2 * FREQ), np.float64)
    table[: len(points), :FREQ] = np.cos(angle)
    table[: len(points), FREQ:] = -np.sin(angle)
    table = np.where(np.abs(table) < 1e-9, 0.0, table)
    high = table.astype(ml_dtypes.bfloat16)
    low = (table - high.astype(np.float64)).astype(ml_dtypes.bfloat16)
    edge_plane = (kz == 0) | (kz == GRID // 2)
    factor = np.where(edge_plane, 1.0, 2.0) / GRID**3 * np.where((kx + ky + kz) % 2 == 0, 1.0, -1.0)
    factor = np.concatenate([factor, factor]).astype(np.float32)[None, :]
    return np.concatenate([high, low], axis=0), factor


def source_rows(comp_count):
    return ((2 * comp_count * MAIN // 8 + TAIL) | 1) * 8


def kernel_row(part, tile):
    return part * MAIN + tile if tile < MAIN else 2 * MAIN + (tile - MAIN) * 2 + part


def source_row(comp_count, which, tile):
    if tile < MAIN:
        return which * MAIN + tile
    return 2 * comp_count * MAIN + (tile - MAIN) * 8 + which


def pack_kernel(density, send_list, halo_list, *outs):
    peers, cap = send_list.shape
    rim = halo_list.shape[1]
    member = lax.axis_index("dev")
    parity = lax.rem(lax.axis_index("group"), 2)
    to_near, *to_far, to_first, to_second = outs
    for c in range(density.shape[0]):
        for e in range(cap):
            for part, k in enumerate((1, 3)):
                to_near[part, c, e : e + 1, :] = density[c, pl.ds(send_list[member ^ k, e], 1), :]
            for k, out in zip((2, *range(4, peers)), to_far):
                out[c, e : e + 1, :] = density[c, pl.ds(send_list[member ^ k, e], 1), :]
        for e in range(rim):
            to_first[c, e : e + 1, :] = density[c, pl.ds(halo_list[1 - parity, e], 1), :]
            to_second[c, e : e + 1, :] = density[c, pl.ds(halo_list[parity, e], 1), :]


def prepare_kernel(kernel_hat, hat):
    parts, count, _ = kernel_hat.shape
    flat = hat.reshape(count * HAT_ROWS, LANES)

    def move(first, height):
        for part in range(parts):
            for j in range(TILES):
                x = kernel_hat[part, pl.ds(first, height), j * LANES : (j + 1) * LANES].astype(jnp.float32)
                for g in range(0, height, 8):
                    size = min(8, height - g)
                    piece = x[g : g + size]
                    flat[pl.ds((first + g) * HAT_ROWS + kernel_row(part, j), size, stride=HAT_ROWS), :] = piece

    whole = count // 16

    @pl.loop(0, whole)
    def _(i):
        move(pl.multiple_of(i * 16, 16), 16)

    if count % 16:
        move(whole * 16, count % 16)


def forward_kernel(send_list, density, from_near, relayed, *refs):
    *from_far, from_first, from_second, table, main, rows = refs
    comp_count, box_count, surf = density.shape
    peers, cap = send_list.shape
    rim = from_first.shape[1]
    row_count = rows.shape[0]
    slots = row_count // comp_count
    pitch = source_rows(comp_count)
    flat = main.reshape(slots * pitch, LANES)
    f32, bf16 = jnp.float32, jnp.bfloat16

    member = lax.axis_index("dev")
    parity = lax.rem(lax.axis_index("group"), 2)
    rows[...] = jnp.zeros_like(rows)
    pieces = {1: from_near.at[0], 3: relayed.at[1]}
    pieces.update(zip((2, *range(4, peers)), from_far))
    for c in range(comp_count):
        base = c * slots
        rows[base : base + box_count, :surf] = density[c]
        base += box_count
        for e in range(cap):
            rows[pl.ds(base + member * cap + e, 1), :surf] = density[c, pl.ds(send_list[member, e], 1), :]
            for k, piece in pieces.items():
                rows[pl.ds(base + (member ^ k) * cap + e, 1), :surf] = piece[c, e : e + 1]
        base += peers * cap
        for e in range(rim):
            rows[pl.ds(base + (1 - parity) * rim + e, 1), :surf] = from_first[c, e : e + 1]
            rows[pl.ds(base + parity * rim + e, 1), :surf] = from_second[c, e : e + 1]

    value = rows[...]
    high = value.astype(bf16)
    low = (value - high.astype(f32)).astype(bf16)
    both = jnp.concatenate([high, low], axis=0)
    for n in range(2 * FREQ // CHUNK):
        columns = slice(n * CHUNK, (n + 1) * CHUNK)
        x = jnp.dot(both, table[:POINTS_PAD, columns], preferred_element_type=f32)
        x = x[:row_count] + x[row_count:]
        x = x + jnp.dot(high, table[POINTS_PAD:, columns], preferred_element_type=f32)
        x = x.astype(bf16).astype(f32)
        for m in range(CHUNK // LANES):
            part, j = divmod(n * (CHUNK // LANES) + m, TILES)
            for g in range(row_count // 8):
                piece = x[g * 8 : (g + 1) * 8, m * LANES : (m + 1) * LANES]
                c, s = divmod(g * 8, slots)
                row = source_row(comp_count, part * comp_count + c, j)
                flat[pl.ds(s * pitch + row, 8, stride=pitch), :] = piece


def interact_kernel(comp_count, source, offset, hat, main, total, total_tail):
    box_count, list_count = source.shape
    f32 = jnp.float32
    plus = lax.broadcasted_iota(jnp.int32, (8, LANES), 0) < comp_count
    halves = MAIN // 8

    @pl.loop(0, box_count)
    def _(t):
        def rows_of(first):
            return tuple(
                (source[t, first + u], offset[t, first + u]) for u in range(UNROLL)
            )

        def pair(s, o, accs):
            def kernel_tiles(part, tile):
                row = kernel_row(part, tile)
                return hat[o, row : row + 8, :]

            def source_tiles(which, tile):
                row = source_row(comp_count, which, tile)
                return main[s, row : row + 8, :]

            k = [[kernel_tiles(r, 8 * h) for h in range(halves)] for r in range(2)]
            accs = list(accs)
            at = 0
            for c in range(comp_count):
                for h in range(halves):
                    s_re, s_im = source_tiles(c, 8 * h), source_tiles(comp_count + c, 8 * h)
                    accs[at] = accs[at] + (k[0][h] * s_re - k[1][h] * s_im)
                    accs[at + 1] = accs[at + 1] + (k[0][h] * s_im + k[1][h] * s_re)
                    at += 2
            for j in range(MAIN, TILES):
                x = source_tiles(0, j)
                for r in range(2):
                    accs[at + r] = accs[at + r] + hat[o, pl.ds(kernel_row(r, j), 8, stride=0), :] * x
                at += 2
            return tuple(accs)

        count = 2 * (comp_count * halves + TAIL)
        zero = jnp.zeros((8, LANES), f32)

        def block(i, carry):
            accs, here = carry
            ahead = rows_of(lax.rem((i + 1) * UNROLL, list_count))
            for s, o in here:
                accs = pair(s, o, accs)
            return accs, ahead

        accs, _ = lax.fori_loop(0, list_count // UNROLL, block, ((zero,) * count, rows_of(0)))
        at = 0
        for c in range(comp_count):
            for h in range(halves):
                for part in range(2):
                    row = (part * comp_count + c) * box_count + t
                    total[pl.ds(row * PITCH + 8 * h, 8), :] = accs[at + part]
                at += 2
        for j in range(TAIL):
            own, cross = accs[at], accs[at + 1]
            up = jnp.concatenate([cross[comp_count:], cross[:comp_count]], axis=0)
            down = jnp.concatenate([cross[-comp_count:], cross[:-comp_count]], axis=0)
            total_tail[j, pl.ds(t * TAIL_PITCH, 8), :] = jnp.where(plus, own - up, own + down)
            at += 2


def inverse_kernel(total, total_tail, table, factor, out):
    comp_count, box_count, surf = out.shape
    f32, bf16 = jnp.float32, jnp.bfloat16
    groups = box_count // 8
    count = comp_count * box_count
    nt = (((1,), (1,)), ((), ()))
    result = jnp.zeros((2 * POINTS_PAD, 2 * count), f32)
    for n in range(2 * FREQ // PIECE):
        lanes = []
        for m in range(PIECE // LANES):
            part, j = divmod(n * (PIECE // LANES) + m, TILES)
            pieces = []
            for c in range(comp_count):
                for g in range(groups):
                    if j < MAIN:
                        row = (part * comp_count + c) * box_count + g * 8
                        pieces.append(total[pl.ds(row * PITCH + j, 8, stride=PITCH), :])
                    else:
                        row = g * 8 * TAIL_PITCH + part * comp_count + c
                        pieces.append(total_tail[j - MAIN, pl.ds(row, 8, stride=TAIL_PITCH), :])
            lanes.append(jnp.concatenate(pieces, axis=0))
        columns = slice(n * PIECE, (n + 1) * PIECE)
        x = jnp.concatenate(lanes, axis=1) * factor[:, columns]
        high = x.astype(bf16)
        low = (x - high.astype(f32)).astype(bf16)
        both = jnp.concatenate([high, low], axis=0)
        result += lax.dot_general(table[:, columns], both, nt, preferred_element_type=f32)
    result = result[:POINTS_PAD, :count] + result[:POINTS_PAD, count:] + result[POINTS_PAD:, :count]
    result = result.T
    for c in range(comp_count):
        out[c] = result[c * box_count : (c + 1) * box_count, :surf]


def on_device(density, kernel_hat, send_list, halo_list, inter_src, inter_off):
    table, factor = transform_tables()
    box_count, comp_count, surf = density.shape
    _, peers, cap = send_list.shape
    rim = halo_list.shape[2]
    f32 = jnp.float32
    vmem = pl.BlockSpec(memory_space=pltpu.VMEM)
    smem = pl.BlockSpec(memory_space=pltpu.SMEM)
    density = density.transpose(1, 0, 2)

    boxes = jax.ShapeDtypeStruct((comp_count, cap, surf), f32)
    side = jax.ShapeDtypeStruct((comp_count, rim, surf), f32)
    to_near, *to_far, to_first, to_second = pl.pallas_call(
        pack_kernel,
        out_shape=(jax.ShapeDtypeStruct((2, *boxes.shape), f32),) + (boxes,) * (peers - 3) + (side,) * 2,
        in_specs=[vmem, smem, smem],
        out_specs=(vmem,) * peers,
        name="pack",
    )(density, send_list[0], halo_list[0])

    def swap(x, k):
        return lax.ppermute(x, "dev", [(i, i ^ k) for i in range(peers)])

    def swap_groups(x, start):
        pairs = [(i, i + 1) for i in range(start, lax.axis_size("group") - 1, 2)]
        return lax.ppermute(x, "group", pairs + [(j, i) for i, j in pairs])

    from_near = swap(to_near, 1)
    from_far = [swap(x, k) for x, k in zip(to_far, (2, *range(4, peers)))]
    from_first = swap_groups(to_first, 0)
    from_second = swap_groups(to_second, 1)
    by_part, near = lax.optimization_barrier((kernel_hat.transpose(1, 0, 2), from_near))
    relayed = swap(near, 2)

    offsets = kernel_hat.shape[0]
    hat = pl.pallas_call(
        prepare_kernel,
        out_shape=jax.ShapeDtypeStruct((offsets, HAT_ROWS, LANES), f32),
        in_specs=[vmem],
        out_specs=vmem,
        compiler_params=pltpu.CompilerParams(vmem_limit_bytes=16 * 1024 * 1024),
        cost_estimate=pl.CostEstimate(flops=kernel_hat.size, bytes_accessed=6 * kernel_hat.size, transcendentals=0),
        name="prepare",
    )(by_part)

    slots = box_count + peers * cap + 2 * rim
    row_count = comp_count * slots
    params = pltpu.CompilerParams(vmem_limit_bytes=24 * 1024 * 1024)
    table = jnp.asarray(table)
    arrays = (send_list[0], density, from_near, relayed, *from_far, from_first, from_second, table)
    main = pl.pallas_call(
        forward_kernel,
        out_shape=jax.ShapeDtypeStruct((slots, source_rows(comp_count), LANES), f32),
        in_specs=[smem] + [vmem] * (len(arrays) - 1),
        out_specs=vmem,
        scratch_shapes=[pltpu.VMEM((row_count, POINTS_PAD), f32)],
        compiler_params=params,
        name="forward",
    )(*arrays)
    total, total_tail = pl.pallas_call(
        functools.partial(interact_kernel, comp_count),
        out_shape=(
            jax.ShapeDtypeStruct((2 * comp_count * box_count * PITCH, LANES), f32),
            jax.ShapeDtypeStruct((TAIL, (box_count + 2) * TAIL_PITCH, LANES), f32),
        ),
        in_specs=[smem, smem] + [vmem] * 2,
        out_specs=(vmem, vmem),
        compiler_params=params,
        name="interact",
    )(inter_src, inter_off, hat, main)
    potential = pl.pallas_call(
        inverse_kernel,
        out_shape=jax.ShapeDtypeStruct((comp_count, box_count, surf), f32),
        in_specs=[vmem] * 4,
        out_specs=vmem,
        compiler_params=params,
        name="inverse",
    )(total, total_tail, table, jnp.asarray(factor))
    return potential.transpose(1, 0, 2)


def solution(mesh):
    in_specs = (
        P(("group", "dev"), None, None),
        P(),
        P(("group", "dev"), None, None),
        P(("group", "dev"), None, None),
        P(("group", "dev"), None),
        P(("group", "dev"), None),
    )
    out_specs = P(("group", "dev"), None, None)
    return jax.shard_map(
        on_device, mesh=mesh, in_specs=in_specs, out_specs=out_specs, check_vma=False
    )
```

```python
import functools
import math

import jax
import jax.numpy as jnp
import ml_dtypes
import numpy as np
from jax import lax
from jax.experimental import pallas as pl
from jax.experimental.pallas import tpu as pltpu
from jax.sharding import PartitionSpec as P

ORDER = 6
GRID = 16
LANES = 128
HALF = GRID // 2 + 1
FREQ = GRID * GRID * HALF
TILES = FREQ // LANES
MAIN = 16
TAIL = TILES - MAIN
PITCH = MAIN + 1
TAIL_PITCH = 7
HAT_ROWS = 2 * TILES + 1
POINTS_PAD = 160
CHUNK = 256
PIECE = 512
UNROLL = 8


def surface_points(edge_count):
    points = [
        (i, j, k)
        for i in range(edge_count)
        for j in range(edge_count)
        for k in range(edge_count)
        if min(i, j, k) == 0 or max(i, j, k) == edge_count - 1
    ]
    return np.array(points, dtype=np.int64)


@functools.lru_cache(maxsize=None)
def transform_tables():
    points = surface_points(ORDER)
    kx, ky, kz = (a.reshape(-1) for a in np.meshgrid(np.arange(GRID), np.arange(GRID), np.arange(HALF), indexing="ij"))
    phase = (points[:, :1] * kx + points[:, 1:2] * ky + points[:, 2:] * kz) % GRID
    angle = phase * (2.0 * math.pi / GRID)
    table = np.zeros((POINTS_PAD, 2 * FREQ), np.float64)
    table[: len(points), :FREQ] = np.cos(angle)
    table[: len(points), FREQ:] = -np.sin(angle)
    table = np.where(np.abs(table) < 1e-9, 0.0, table)
    high = table.astype(ml_dtypes.bfloat16)
    low = (table - high.astype(np.float64)).astype(ml_dtypes.bfloat16)
    edge_plane = (kz == 0) | (kz == GRID // 2)
    factor = np.where(edge_plane, 1.0, 2.0) / GRID**3 * np.where((kx + ky + kz) % 2 == 0, 1.0, -1.0)
    factor = np.concatenate([factor, factor]).astype(np.float32)[None, :]
    return np.concatenate([high, low], axis=0), factor


def source_rows(comp_count):
    return (2 * comp_count * MAIN + TAIL * 8) | 1


def source_row(comp_count, which, tile):
    if tile < MAIN:
        return which * MAIN + tile
    return 2 * comp_count * MAIN + (tile - MAIN) * 8 + which


def kernel_row(part, tile):
    return part * MAIN + tile if tile < MAIN else 2 * MAIN + (tile - MAIN) * 2 + part


def pack_kernel(density, send_list, halo_list, *outs):
    peers, cap = send_list.shape
    rim = halo_list.shape[1]
    member = lax.axis_index("dev")
    parity = lax.rem(lax.axis_index("group"), 2)
    to_near, *to_far, to_first, to_second = outs
    for c in range(density.shape[0]):
        for e in range(cap):
            for part, k in enumerate((1, 3)):
                to_near[part, c, e : e + 1, :] = density[c, pl.ds(send_list[member ^ k, e], 1), :]
            for k, out in zip((2, *range(4, peers)), to_far):
                out[c, e : e + 1, :] = density[c, pl.ds(send_list[member ^ k, e], 1), :]
        for e in range(rim):
            to_first[c, e : e + 1, :] = density[c, pl.ds(halo_list[1 - parity, e], 1), :]
            to_second[c, e : e + 1, :] = density[c, pl.ds(halo_list[parity, e], 1), :]


def prepare_kernel(kernel_hat, hat):
    parts, count, _ = kernel_hat.shape

    def move(first, height):
        for part in range(parts):
            for j in range(TILES):
                x = kernel_hat[part, pl.ds(first, height), j * LANES : (j + 1) * LANES].astype(jnp.float32)
                for g in range(0, height, 8):
                    size = min(8, height - g)
                    piece = x[g : g + size]
                    row = (first + g) * HAT_ROWS + kernel_row(part, j)
                    hat[pl.ds(row, size, stride=HAT_ROWS), :] = piece

    whole = count // 16

    @pl.loop(0, whole)
    def _(i):
        move(pl.multiple_of(i * 16, 16), 16)

    if count % 16:
        move(whole * 16, count % 16)


def forward_kernel(send_list, density, from_near, relayed, *refs):
    *from_far, from_first, from_second, table, main, rows = refs
    comp_count, box_count, surf = density.shape
    peers, cap = send_list.shape
    rim = from_first.shape[1]
    row_count = rows.shape[0]
    slots = row_count // comp_count
    pitch = source_rows(comp_count)
    f32, bf16 = jnp.float32, jnp.bfloat16

    member = lax.axis_index("dev")
    parity = lax.rem(lax.axis_index("group"), 2)
    rows[...] = jnp.zeros_like(rows)
    pieces = {1: from_near.at[0], 3: relayed.at[1]}
    pieces.update(zip((2, *range(4, peers)), from_far))
    for c in range(comp_count):
        base = c * slots
        rows[base : base + box_count, :surf] = density[c]
        base += box_count
        for e in range(cap):
            rows[pl.ds(base + member * cap + e, 1), :surf] = density[c, pl.ds(send_list[member, e], 1), :]
            for k, piece in pieces.items():
                rows[pl.ds(base + (member ^ k) * cap + e, 1), :surf] = piece[c, e : e + 1]
        base += peers * cap
        for e in range(rim):
            rows[pl.ds(base + (1 - parity) * rim + e, 1), :surf] = from_first[c, e : e + 1]
            rows[pl.ds(base + parity * rim + e, 1), :surf] = from_second[c, e : e + 1]

    value = rows[...]
    high = value.astype(bf16)
    low = (value - high.astype(f32)).astype(bf16)
    both = jnp.concatenate([high, low], axis=0)
    for n in range(2 * FREQ // CHUNK):
        columns = slice(n * CHUNK, (n + 1) * CHUNK)
        x = jnp.dot(both, table[:POINTS_PAD, columns], preferred_element_type=f32)
        x = x[:row_count] + x[row_count:]
        x = x + jnp.dot(high, table[POINTS_PAD:, columns], preferred_element_type=f32)
        x = x.astype(bf16).astype(f32)
        for m in range(CHUNK // LANES):
            part, j = divmod(n * (CHUNK // LANES) + m, TILES)
            for g in range(row_count // 8):
                piece = x[g * 8 : (g + 1) * 8, m * LANES : (m + 1) * LANES]
                c, s = divmod(g * 8, slots)
                row = source_row(comp_count, part * comp_count + c, j)
                main[pl.ds(s * pitch + row, 8, stride=pitch), :] = piece


def interact_kernel(comp_count, source, offset, hat, main, total, total_tail):
    box_count, list_count = source.shape
    pitch = source_rows(comp_count)
    f32 = jnp.float32
    plus = lax.broadcasted_iota(jnp.int32, (8, LANES), 0) < comp_count
    halves = MAIN // 8

    @pl.loop(0, box_count)
    def _(t):
        def rows_of(first):
            return tuple(
                (source[t, first + u] * pitch, offset[t, first + u] * HAT_ROWS) for u in range(UNROLL)
            )

        def pair(s, o, accs):
            k = [[hat[pl.ds(o + kernel_row(r, 8 * h), 8), :] for h in range(halves)] for r in range(2)]
            accs = list(accs)
            at = 0
            for c in range(comp_count):
                for h in range(halves):
                    s_re = main[pl.ds(s + (source_row(comp_count, c, 8 * h)), 8), :]
                    s_im = main[pl.ds(s + (source_row(comp_count, comp_count + c, 8 * h)), 8), :]
                    accs[at] = accs[at] + (k[0][h] * s_re - k[1][h] * s_im)
                    accs[at + 1] = accs[at + 1] + (k[0][h] * s_im + k[1][h] * s_re)
                    at += 2
            k_tail = hat[pl.ds(o + kernel_row(0, MAIN), 8), :]
            for j in range(TAIL):
                x = main[pl.ds(s + source_row(comp_count, 0, MAIN + j), 8), :]
                for r in range(2):
                    row = 2 * j + r
                    accs[at + r] = accs[at + r] + jnp.broadcast_to(k_tail[row : row + 1], (8, LANES)) * x
                at += 2
            return tuple(accs)

        count = 2 * (comp_count * halves + TAIL)
        zero = jnp.zeros((8, LANES), f32)

        def block(i, carry):
            accs, here = carry
            ahead = rows_of(lax.rem((i + 1) * UNROLL, list_count))
            for s, o in here:
                accs = pair(s, o, accs)
            return accs, ahead

        accs, _ = lax.fori_loop(0, list_count // UNROLL, block, ((zero,) * count, rows_of(0)))
        at = 0
        for c in range(comp_count):
            for h in range(halves):
                for part in range(2):
                    row = (part * comp_count + c) * box_count + t
                    total[pl.ds(row * PITCH + 8 * h, 8), :] = accs[at + part]
                at += 2
        for j in range(TAIL):
            own, cross = accs[at], accs[at + 1]
            up = jnp.concatenate([cross[comp_count:], cross[:comp_count]], axis=0)
            down = jnp.concatenate([cross[-comp_count:], cross[:-comp_count]], axis=0)
            total_tail[j, pl.ds(t * TAIL_PITCH, 8), :] = jnp.where(plus, own - up, own + down)
            at += 2


def inverse_kernel(total, total_tail, table, factor, out):
    comp_count, box_count, surf = out.shape
    f32, bf16 = jnp.float32, jnp.bfloat16
    groups = box_count // 8
    count = comp_count * box_count
    nt = (((1,), (1,)), ((), ()))
    result = jnp.zeros((2 * POINTS_PAD, 2 * count), f32)
    for n in range(2 * FREQ // PIECE):
        lanes = []
        for m in range(PIECE // LANES):
            part, j = divmod(n * (PIECE // LANES) + m, TILES)
            pieces = []
            for c in range(comp_count):
                for g in range(groups):
                    if j < MAIN:
                        row = (part * comp_count + c) * box_count + g * 8
                        pieces.append(total[pl.ds(row * PITCH + j, 8, stride=PITCH), :])
                    else:
                        row = g * 8 * TAIL_PITCH + part * comp_count + c
                        pieces.append(total_tail[j - MAIN, pl.ds(row, 8, stride=TAIL_PITCH), :])
            lanes.append(jnp.concatenate(pieces, axis=0))
        columns = slice(n * PIECE, (n + 1) * PIECE)
        x = jnp.concatenate(lanes, axis=1) * factor[:, columns]
        high = x.astype(bf16)
        low = (x - high.astype(f32)).astype(bf16)
        both = jnp.concatenate([high, low], axis=0)
        result += lax.dot_general(table[:, columns], both, nt, preferred_element_type=f32)
    result = result[:POINTS_PAD, :count] + result[:POINTS_PAD, count:] + result[POINTS_PAD:, :count]
    result = result.T
    for c in range(comp_count):
        out[c] = result[c * box_count : (c + 1) * box_count, :surf]


def on_device(density, kernel_hat, send_list, halo_list, inter_src, inter_off):
    table, factor = transform_tables()
    box_count, comp_count, surf = density.shape
    _, peers, cap = send_list.shape
    rim = halo_list.shape[2]
    f32 = jnp.float32
    vmem = pl.BlockSpec(memory_space=pltpu.VMEM)
    smem = pl.BlockSpec(memory_space=pltpu.SMEM)
    density = density.transpose(1, 0, 2)

    boxes = jax.ShapeDtypeStruct((comp_count, cap, surf), f32)
    side = jax.ShapeDtypeStruct((comp_count, rim, surf), f32)
    to_near, *to_far, to_first, to_second = pl.pallas_call(
        pack_kernel,
        out_shape=(jax.ShapeDtypeStruct((2, *boxes.shape), f32),) + (boxes,) * (peers - 3) + (side,) * 2,
        in_specs=[vmem, smem, smem],
        out_specs=(vmem,) * peers,
        name="pack",
    )(density, send_list[0], halo_list[0])

    def swap(x, k):
        return lax.ppermute(x, "dev", [(i, i ^ k) for i in range(peers)])

    def swap_groups(x, start):
        pairs = [(i, i + 1) for i in range(start, lax.axis_size("group") - 1, 2)]
        return lax.ppermute(x, "group", pairs + [(j, i) for i, j in pairs])

    from_near = swap(to_near, 1)
    from_far = [swap(x, k) for x, k in zip(to_far, (2, *range(4, peers)))]
    from_first = swap_groups(to_first, 0)
    from_second = swap_groups(to_second, 1)
    by_part, near = lax.optimization_barrier((kernel_hat.transpose(1, 0, 2), from_near))
    relayed = swap(near, 2)

    offsets = kernel_hat.shape[0]
    hat = pl.pallas_call(
        prepare_kernel,
        out_shape=jax.ShapeDtypeStruct((offsets * HAT_ROWS + 8, LANES), f32),
        in_specs=[vmem],
        out_specs=vmem,
        compiler_params=pltpu.CompilerParams(vmem_limit_bytes=16 * 1024 * 1024),
        cost_estimate=pl.CostEstimate(flops=kernel_hat.size, bytes_accessed=6 * kernel_hat.size, transcendentals=0),
        name="prepare",
    )(by_part)

    slots = box_count + peers * cap + 2 * rim
    row_count = comp_count * slots
    params = pltpu.CompilerParams(vmem_limit_bytes=24 * 1024 * 1024)
    table = jnp.asarray(table)
    arrays = (send_list[0], density, from_near, relayed, *from_far, from_first, from_second, table)
    main = pl.pallas_call(
        forward_kernel,
        out_shape=jax.ShapeDtypeStruct((slots * source_rows(comp_count) + 8, LANES), f32),
        in_specs=[smem] + [vmem] * (len(arrays) - 1),
        out_specs=vmem,
        scratch_shapes=[pltpu.VMEM((row_count, POINTS_PAD), f32)],
        compiler_params=params,
        name="forward",
    )(*arrays)
    total, total_tail = pl.pallas_call(
        functools.partial(interact_kernel, comp_count),
        out_shape=(
            jax.ShapeDtypeStruct((2 * comp_count * box_count * PITCH, LANES), f32),
            jax.ShapeDtypeStruct((TAIL, (box_count + 2) * TAIL_PITCH, LANES), f32),
        ),
        in_specs=[smem, smem] + [vmem] * 2,
        out_specs=(vmem, vmem),
        compiler_params=params,
        name="interact",
    )(inter_src, inter_off, hat, main)
    potential = pl.pallas_call(
        inverse_kernel,
        out_shape=jax.ShapeDtypeStruct((comp_count, box_count, surf), f32),
        in_specs=[vmem] * 4,
        out_specs=vmem,
        compiler_params=params,
        name="inverse",
    )(total, total_tail, table, jnp.asarray(factor))
    return potential.transpose(1, 0, 2)


def solution(mesh):
    in_specs = (
        P(("group", "dev"), None, None),
        P(),
        P(("group", "dev"), None, None),
        P(("group", "dev"), None, None),
        P(("group", "dev"), None),
        P(("group", "dev"), None),
    )
    out_specs = P(("group", "dev"), None, None)
    return jax.shard_map(
        on_device, mesh=mesh, in_specs=in_specs, out_specs=out_specs, check_vma=False
    )
```

```python
import functools
import math

import jax
import jax.numpy as jnp
import ml_dtypes
import numpy as np
from jax import lax
from jax.experimental import pallas as pl
from jax.experimental.pallas import tpu as pltpu
from jax.sharding import PartitionSpec as P

ORDER = 6
GRID = 16
LANES = 128
HALF = GRID // 2 + 1
FREQ = GRID * GRID * HALF
TILES = FREQ // LANES
MAIN = 16
TAIL = TILES - MAIN
PITCH = MAIN + 1
TAIL_PITCH = 7
HAT_ROWS = 3 * MAIN + 2 * TAIL + 1
POINTS_PAD = 160
CHUNK = 256
PIECE = 512
UNROLL = 8


def surface_points(edge_count):
    points = [
        (i, j, k)
        for i in range(edge_count)
        for j in range(edge_count)
        for k in range(edge_count)
        if min(i, j, k) == 0 or max(i, j, k) == edge_count - 1
    ]
    return np.array(points, dtype=np.int64)


@functools.lru_cache(maxsize=None)
def transform_tables():
    points = surface_points(ORDER)
    kx, ky, kz = (a.reshape(-1) for a in np.meshgrid(np.arange(GRID), np.arange(GRID), np.arange(HALF), indexing="ij"))
    phase = (points[:, :1] * kx + points[:, 1:2] * ky + points[:, 2:] * kz) % GRID
    angle = phase * (2.0 * math.pi / GRID)
    table = np.zeros((POINTS_PAD, 2 * FREQ), np.float64)
    table[: len(points), :FREQ] = np.cos(angle)
    table[: len(points), FREQ:] = -np.sin(angle)
    table = np.where(np.abs(table) < 1e-9, 0.0, table)
    high = table.astype(ml_dtypes.bfloat16)
    low = (table - high.astype(np.float64)).astype(ml_dtypes.bfloat16)
    edge_plane = (kz == 0) | (kz == GRID // 2)
    factor = np.where(edge_plane, 1.0, 2.0) / GRID**3 * np.where((kx + ky + kz) % 2 == 0, 1.0, -1.0)
    factor = np.concatenate([factor, factor]).astype(np.float32)[None, :]
    return np.concatenate([high, low], axis=0), factor


def source_rows(comp_count):
    return (3 * comp_count * MAIN + TAIL * 8) | 1


def source_row(comp_count, which, tile):
    if tile < MAIN:
        return which * MAIN + tile
    return 3 * comp_count * MAIN + (tile - MAIN) * 8 + which


def kernel_row(which, tile):
    return which * MAIN + tile if tile < MAIN else 3 * MAIN + (tile - MAIN) * 2 + which


def pack_kernel(density, send_list, halo_list, *outs):
    peers, cap = send_list.shape
    rim = halo_list.shape[1]
    member = lax.axis_index("dev")
    parity = lax.rem(lax.axis_index("group"), 2)
    to_near, *to_far, to_first, to_second = outs
    for c in range(density.shape[0]):
        for e in range(cap):
            for part, k in enumerate((1, 3)):
                to_near[part, c, e : e + 1, :] = density[c, pl.ds(send_list[member ^ k, e], 1), :]
            for k, out in zip((2, *range(4, peers)), to_far):
                out[c, e : e + 1, :] = density[c, pl.ds(send_list[member ^ k, e], 1), :]
        for e in range(rim):
            to_first[c, e : e + 1, :] = density[c, pl.ds(halo_list[1 - parity, e], 1), :]
            to_second[c, e : e + 1, :] = density[c, pl.ds(halo_list[parity, e], 1), :]


def prepare_kernel(kernel_hat, hat):
    parts, count, _ = kernel_hat.shape

    def move(first, height):
        for j in range(TILES):
            re, im = (
                kernel_hat[part, pl.ds(first, height), j * LANES : (j + 1) * LANES].astype(jnp.float32)
                for part in range(parts)
            )
            for which, x in enumerate((re, re + im, im - re) if j < MAIN else (re, im)):
                for g in range(0, height, 8):
                    size = min(8, height - g)
                    row = (first + g) * HAT_ROWS + kernel_row(which, j)
                    hat[pl.ds(row, size, stride=HAT_ROWS), :] = x[g : g + size]

    whole = count // 16

    @pl.loop(0, whole)
    def _(i):
        move(pl.multiple_of(i * 16, 16), 16)

    if count % 16:
        move(whole * 16, count % 16)


def forward_kernel(send_list, density, from_near, relayed, *refs):
    *from_far, from_first, from_second, table, main, rows = refs
    comp_count, box_count, surf = density.shape
    peers, cap = send_list.shape
    rim = from_first.shape[1]
    row_count = rows.shape[0]
    slots = row_count // comp_count
    pitch = source_rows(comp_count)
    f32, bf16 = jnp.float32, jnp.bfloat16

    member = lax.axis_index("dev")
    parity = lax.rem(lax.axis_index("group"), 2)
    rows[...] = jnp.zeros_like(rows)
    pieces = {1: from_near.at[0], 3: relayed.at[1]}
    pieces.update(zip((2, *range(4, peers)), from_far))
    for c in range(comp_count):
        base = c * slots
        rows[base : base + box_count, :surf] = density[c]
        base += box_count
        for e in range(cap):
            rows[pl.ds(base + member * cap + e, 1), :surf] = density[c, pl.ds(send_list[member, e], 1), :]
            for k, piece in pieces.items():
                rows[pl.ds(base + (member ^ k) * cap + e, 1), :surf] = piece[c, e : e + 1]
        base += peers * cap
        for e in range(rim):
            rows[pl.ds(base + (1 - parity) * rim + e, 1), :surf] = from_first[c, e : e + 1]
            rows[pl.ds(base + parity * rim + e, 1), :surf] = from_second[c, e : e + 1]

    value = rows[...]
    high = value.astype(bf16)
    low = (value - high.astype(f32)).astype(bf16)
    both = jnp.concatenate([high, low], axis=0)

    def spectrum(first):
        columns = slice(first, first + CHUNK)
        x = jnp.dot(both, table[:POINTS_PAD, columns], preferred_element_type=f32)
        x = x[:row_count] + x[row_count:]
        x = x + jnp.dot(high, table[POINTS_PAD:, columns], preferred_element_type=f32)
        return x.astype(bf16).astype(f32)

    for n in range(FREQ // CHUNK):
        re, im = spectrum(n * CHUNK), spectrum(FREQ + n * CHUNK)
        for m in range(CHUNK // LANES):
            j = n * (CHUNK // LANES) + m
            for g in range(row_count // 8):
                at = (slice(g * 8, (g + 1) * 8), slice(m * LANES, (m + 1) * LANES))
                c, s = divmod(g * 8, slots)
                pieces = [re[at], im[at]]
                if j < MAIN:
                    pieces.append(pieces[0] + pieces[1])
                for part, piece in enumerate(pieces):
                    row = source_row(comp_count, part * comp_count + c, j)
                    main[pl.ds(s * pitch + row, 8, stride=pitch), :] = piece


def interact_kernel(comp_count, source, offset, hat, main, total, total_tail):
    box_count, list_count = source.shape
    pitch = source_rows(comp_count)
    f32 = jnp.float32
    plus = lax.broadcasted_iota(jnp.int32, (8, LANES), 0) < comp_count
    halves = MAIN // 8

    @pl.loop(0, box_count)
    def _(t):
        def rows_of(first):
            return tuple(
                (source[t, first + u] * pitch, offset[t, first + u] * HAT_ROWS) for u in range(UNROLL)
            )

        def pair(s, o, accs):
            k = [[hat[pl.ds(o + kernel_row(r, 8 * h), 8), :] for h in range(halves)] for r in range(3)]
            accs = list(accs)
            at = 0
            for c in range(comp_count):
                for h in range(halves):
                    s_re, s_im, s_sum = (
                        main[pl.ds(s + source_row(comp_count, r * comp_count + c, 8 * h), 8), :] for r in range(3)
                    )
                    accs[at] = accs[at] + k[0][h] * s_sum
                    accs[at + 1] = accs[at + 1] + k[1][h] * s_im
                    accs[at + 2] = accs[at + 2] + k[2][h] * s_re
                    at += 3
            k_tail = hat[pl.ds(o + kernel_row(0, MAIN), 8), :]
            for j in range(TAIL):
                x = main[pl.ds(s + source_row(comp_count, 0, MAIN + j), 8), :]
                for r in range(2):
                    row = 2 * j + r
                    accs[at + r] = accs[at + r] + jnp.broadcast_to(k_tail[row : row + 1], (8, LANES)) * x
                at += 2
            return tuple(accs)

        count = 3 * comp_count * halves + 2 * TAIL
        zero = jnp.zeros((8, LANES), f32)

        def block(i, carry):
            accs, here = carry
            ahead = rows_of(lax.rem((i + 1) * UNROLL, list_count))
            for s, o in here:
                accs = pair(s, o, accs)
            return accs, ahead

        accs, _ = lax.fori_loop(0, list_count // UNROLL, block, ((zero,) * count, rows_of(0)))
        at = 0
        for c in range(comp_count):
            for h in range(halves):
                for part, value in enumerate((accs[at] - accs[at + 1], accs[at] + accs[at + 2])):
                    row = (part * comp_count + c) * box_count + t
                    total[pl.ds(row * PITCH + 8 * h, 8), :] = value
                at += 3
        for j in range(TAIL):
            own, cross = accs[at], accs[at + 1]
            up = jnp.concatenate([cross[comp_count:], cross[:comp_count]], axis=0)
            down = jnp.concatenate([cross[-comp_count:], cross[:-comp_count]], axis=0)
            total_tail[j, pl.ds(t * TAIL_PITCH, 8), :] = jnp.where(plus, own - up, own + down)
            at += 2


def inverse_kernel(total, total_tail, table, factor, out):
    comp_count, box_count, surf = out.shape
    f32, bf16 = jnp.float32, jnp.bfloat16
    groups = box_count // 8
    count = comp_count * box_count
    nt = (((1,), (1,)), ((), ()))
    result = jnp.zeros((2 * POINTS_PAD, 2 * count), f32)
    for n in range(2 * FREQ // PIECE):
        lanes = []
        for m in range(PIECE // LANES):
            part, j = divmod(n * (PIECE // LANES) + m, TILES)
            pieces = []
            for c in range(comp_count):
                for g in range(groups):
                    if j < MAIN:
                        row = (part * comp_count + c) * box_count + g * 8
                        pieces.append(total[pl.ds(row * PITCH + j, 8, stride=PITCH), :])
                    else:
                        row = g * 8 * TAIL_PITCH + part * comp_count + c
                        pieces.append(total_tail[j - MAIN, pl.ds(row, 8, stride=TAIL_PITCH), :])
            lanes.append(jnp.concatenate(pieces, axis=0))
        columns = slice(n * PIECE, (n + 1) * PIECE)
        x = jnp.concatenate(lanes, axis=1) * factor[:, columns]
        high = x.astype(bf16)
        low = (x - high.astype(f32)).astype(bf16)
        both = jnp.concatenate([high, low], axis=0)
        result += lax.dot_general(table[:, columns], both, nt, preferred_element_type=f32)
    result = result[:POINTS_PAD, :count] + result[:POINTS_PAD, count:] + result[POINTS_PAD:, :count]
    result = result.T
    for c in range(comp_count):
        out[c] = result[c * box_count : (c + 1) * box_count, :surf]


def on_device(density, kernel_hat, send_list, halo_list, inter_src, inter_off):
    table, factor = transform_tables()
    box_count, comp_count, surf = density.shape
    _, peers, cap = send_list.shape
    rim = halo_list.shape[2]
    f32 = jnp.float32
    vmem = pl.BlockSpec(memory_space=pltpu.VMEM)
    smem = pl.BlockSpec(memory_space=pltpu.SMEM)
    density = density.transpose(1, 0, 2)

    boxes = jax.ShapeDtypeStruct((comp_count, cap, surf), f32)
    side = jax.ShapeDtypeStruct((comp_count, rim, surf), f32)
    to_near, *to_far, to_first, to_second = pl.pallas_call(
        pack_kernel,
        out_shape=(jax.ShapeDtypeStruct((2, *boxes.shape), f32),) + (boxes,) * (peers - 3) + (side,) * 2,
        in_specs=[vmem, smem, smem],
        out_specs=(vmem,) * peers,
        name="pack",
    )(density, send_list[0], halo_list[0])

    def swap(x, k):
        return lax.ppermute(x, "dev", [(i, i ^ k) for i in range(peers)])

    def swap_groups(x, start):
        pairs = [(i, i + 1) for i in range(start, lax.axis_size("group") - 1, 2)]
        return lax.ppermute(x, "group", pairs + [(j, i) for i, j in pairs])

    from_near = swap(to_near, 1)
    from_far = [swap(x, k) for x, k in zip(to_far, (2, *range(4, peers)))]
    from_first = swap_groups(to_first, 0)
    from_second = swap_groups(to_second, 1)
    by_part, near = lax.optimization_barrier((kernel_hat.transpose(1, 0, 2), from_near))
    relayed = swap(near, 2)

    offsets = kernel_hat.shape[0]
    hat = pl.pallas_call(
        prepare_kernel,
        out_shape=jax.ShapeDtypeStruct((offsets * HAT_ROWS + 8, LANES), f32),
        in_specs=[vmem],
        out_specs=vmem,
        compiler_params=pltpu.CompilerParams(vmem_limit_bytes=16 * 1024 * 1024),
        cost_estimate=pl.CostEstimate(flops=kernel_hat.size, bytes_accessed=6 * kernel_hat.size, transcendentals=0),
        name="prepare",
    )(by_part)

    slots = box_count + peers * cap + 2 * rim
    row_count = comp_count * slots
    params = pltpu.CompilerParams(vmem_limit_bytes=24 * 1024 * 1024)
    table = jnp.asarray(table)
    arrays = (send_list[0], density, from_near, relayed, *from_far, from_first, from_second, table)
    main = pl.pallas_call(
        forward_kernel,
        out_shape=jax.ShapeDtypeStruct((slots * source_rows(comp_count) + 8, LANES), f32),
        in_specs=[smem] + [vmem] * (len(arrays) - 1),
        out_specs=vmem,
        scratch_shapes=[pltpu.VMEM((row_count, POINTS_PAD), f32)],
        compiler_params=params,
        name="forward",
    )(*arrays)
    total, total_tail = pl.pallas_call(
        functools.partial(interact_kernel, comp_count),
        out_shape=(
            jax.ShapeDtypeStruct((2 * comp_count * box_count * PITCH, LANES), f32),
            jax.ShapeDtypeStruct((TAIL, (box_count + 2) * TAIL_PITCH, LANES), f32),
        ),
        in_specs=[smem, smem] + [vmem] * 2,
        out_specs=(vmem, vmem),
        compiler_params=params,
        name="interact",
    )(inter_src, inter_off, hat, main)
    potential = pl.pallas_call(
        inverse_kernel,
        out_shape=jax.ShapeDtypeStruct((comp_count, box_count, surf), f32),
        in_specs=[vmem] * 4,
        out_specs=vmem,
        compiler_params=params,
        name="inverse",
    )(total, total_tail, table, jnp.asarray(factor))
    return potential.transpose(1, 0, 2)


def solution(mesh):
    in_specs = (
        P(("group", "dev"), None, None),
        P(),
        P(("group", "dev"), None, None),
        P(("group", "dev"), None, None),
        P(("group", "dev"), None),
        P(("group", "dev"), None),
    )
    out_specs = P(("group", "dev"), None, None)
    return jax.shard_map(
        on_device, mesh=mesh, in_specs=in_specs, out_specs=out_specs, check_vma=False
    )
```

```python
import functools
import math

import jax
import jax.numpy as jnp
import ml_dtypes
import numpy as np
from jax import lax
from jax.experimental import pallas as pl
from jax.experimental.pallas import tpu as pltpu
from jax.sharding import PartitionSpec as P

ORDER = 6
GRID = 16
LANES = 128
HALF = GRID // 2 + 1
FREQ = GRID * GRID * HALF
TILES = FREQ // LANES
MAIN = 16
TAIL = TILES - MAIN
PITCH = MAIN + 1
TAIL_PITCH = 7
HAT_ROWS = 3 * MAIN + 2 * TAIL + 1
POINTS_PAD = 160
CHUNK = 256
PIECE = 512
UNROLL = 8


def surface_points(edge_count):
    points = [
        (i, j, k)
        for i in range(edge_count)
        for j in range(edge_count)
        for k in range(edge_count)
        if min(i, j, k) == 0 or max(i, j, k) == edge_count - 1
    ]
    return np.array(points, dtype=np.int64)


@functools.lru_cache(maxsize=None)
def transform_tables():
    points = surface_points(ORDER)
    kx, ky, kz = (a.reshape(-1) for a in np.meshgrid(np.arange(GRID), np.arange(GRID), np.arange(HALF), indexing="ij"))
    phase = (points[:, :1] * kx + points[:, 1:2] * ky + points[:, 2:] * kz) % GRID
    angle = phase * (2.0 * math.pi / GRID)
    table = np.zeros((POINTS_PAD, 2 * FREQ), np.float64)
    table[: len(points), :FREQ] = np.cos(angle)
    table[: len(points), FREQ:] = -np.sin(angle)
    table = np.where(np.abs(table) < 1e-9, 0.0, table)
    high = table.astype(ml_dtypes.bfloat16)
    low = (table - high.astype(np.float64)).astype(ml_dtypes.bfloat16)
    edge_plane = (kz == 0) | (kz == GRID // 2)
    factor = np.where(edge_plane, 1.0, 2.0) / GRID**3 * np.where((kx + ky + kz) % 2 == 0, 1.0, -1.0)
    factor = np.concatenate([factor, factor]).astype(np.float32)[None, :]
    return np.concatenate([high, low], axis=0), factor


def source_rows(comp_count):
    return (3 * comp_count * MAIN + TAIL * 8) | 1


def source_row(comp_count, which, tile):
    if tile < MAIN:
        return which * MAIN + tile
    return 3 * comp_count * MAIN + (tile - MAIN) * 8 + which


def kernel_row(which, tile):
    return which * MAIN + tile if tile < MAIN else 3 * MAIN + (tile - MAIN) * 2 + which


def pack_kernel(density, send_list, halo_list, *outs):
    peers, cap = send_list.shape
    rim = halo_list.shape[1]
    member = lax.axis_index("dev")
    parity = lax.rem(lax.axis_index("group"), 2)
    to_near, *to_far, to_first, to_second = outs
    for c in range(density.shape[0]):
        for e in range(cap):
            for part, k in enumerate((1, 3)):
                to_near[part, c, e : e + 1, :] = density[c, pl.ds(send_list[member ^ k, e], 1), :]
            for k, out in zip((2, *range(4, peers)), to_far):
                out[c, e : e + 1, :] = density[c, pl.ds(send_list[member ^ k, e], 1), :]
        for e in range(rim):
            to_first[c, e : e + 1, :] = density[c, pl.ds(halo_list[1 - parity, e], 1), :]
            to_second[c, e : e + 1, :] = density[c, pl.ds(halo_list[parity, e], 1), :]


def prepare_kernel(kernel_hat, hat):
    parts, count, _ = kernel_hat.shape

    def move(first, height):
        for j in range(TILES):
            re, im = (
                kernel_hat[part, pl.ds(first, height), j * LANES : (j + 1) * LANES].astype(jnp.float32)
                for part in range(parts)
            )
            for which, x in enumerate((re, re + im, im - re) if j < MAIN else (re, im)):
                for g in range(0, height, 8):
                    size = min(8, height - g)
                    row = (first + g) * HAT_ROWS + kernel_row(which, j)
                    hat[pl.ds(row, size, stride=HAT_ROWS), :] = x[g : g + size]

    whole = count // 16

    @pl.loop(0, whole)
    def _(i):
        move(pl.multiple_of(i * 16, 16), 16)

    if count % 16:
        move(whole * 16, count % 16)


def forward_kernel(send_list, density, from_near, relayed, *refs):
    *from_far, from_first, from_second, table, main, rows = refs
    comp_count, box_count, surf = density.shape
    peers, cap = send_list.shape
    rim = from_first.shape[1]
    row_count = rows.shape[0]
    slots = row_count // comp_count
    pitch = source_rows(comp_count)
    f32, bf16 = jnp.float32, jnp.bfloat16

    member = lax.axis_index("dev")
    parity = lax.rem(lax.axis_index("group"), 2)
    rows[...] = jnp.zeros_like(rows)
    pieces = {1: from_near.at[0], 3: relayed.at[1]}
    pieces.update(zip((2, *range(4, peers)), from_far))
    for c in range(comp_count):
        base = c * slots
        rows[base : base + box_count, :surf] = density[c]
        base += box_count
        for e in range(cap):
            rows[pl.ds(base + member * cap + e, 1), :surf] = density[c, pl.ds(send_list[member, e], 1), :]
            for k, piece in pieces.items():
                rows[pl.ds(base + (member ^ k) * cap + e, 1), :surf] = piece[c, e : e + 1]
        base += peers * cap
        for e in range(rim):
            rows[pl.ds(base + (1 - parity) * rim + e, 1), :surf] = from_first[c, e : e + 1]
            rows[pl.ds(base + parity * rim + e, 1), :surf] = from_second[c, e : e + 1]

    value = rows[...]
    high = value.astype(bf16)
    low = (value - high.astype(f32)).astype(bf16)
    both = jnp.concatenate([high, low], axis=0)

    def spectrum(first):
        columns = slice(first, first + CHUNK)
        x = jnp.dot(both, table[:POINTS_PAD, columns], preferred_element_type=f32)
        x = x[:row_count] + x[row_count:]
        x = x + jnp.dot(high, table[POINTS_PAD:, columns], preferred_element_type=f32)
        return x.astype(bf16).astype(f32)

    for n in range(FREQ // CHUNK):
        re, im = spectrum(n * CHUNK), spectrum(FREQ + n * CHUNK)
        for m in range(CHUNK // LANES):
            j = n * (CHUNK // LANES) + m
            for g in range(row_count // 8):
                at = (slice(g * 8, (g + 1) * 8), slice(m * LANES, (m + 1) * LANES))
                c, s = divmod(g * 8, slots)
                pieces = [re[at], im[at]]
                if j < MAIN:
                    pieces.append(pieces[0] + pieces[1])
                for part, piece in enumerate(pieces):
                    row = source_row(comp_count, part * comp_count + c, j)
                    main[pl.ds(s * pitch + row, 8, stride=pitch), :] = piece


def interact_kernel(comp_count, source, offset, hat, main, total, total_tail):
    box_count, list_count = source.shape
    pitch = source_rows(comp_count)
    f32 = jnp.float32
    plus = lax.broadcasted_iota(jnp.int32, (8, LANES), 0) < comp_count
    halves = MAIN // 8

    @pl.loop(0, box_count)
    def _(t):
        def rows_of(first):
            return tuple(
                (source[t, first + u] * pitch, offset[t, first + u] * HAT_ROWS) for u in range(UNROLL)
            )

        def pair(s, o, accs):
            k = [[hat[pl.ds(o + kernel_row(r, 8 * h), 8), :] for h in range(halves)] for r in range(3)]
            accs = list(accs)
            at = 0
            for c in range(comp_count):
                for h in range(halves):
                    s_re, s_im, s_sum = (
                        main[pl.ds(s + source_row(comp_count, r * comp_count + c, 8 * h), 8), :] for r in range(3)
                    )
                    accs[at] = accs[at] + k[0][h] * s_sum
                    accs[at + 1] = accs[at + 1] + k[1][h] * s_im
                    accs[at + 2] = accs[at + 2] + k[2][h] * s_re
                    at += 3
            k_tail = hat[pl.ds(o + kernel_row(0, MAIN), 8), :]
            for j in range(TAIL):
                x = main[pl.ds(s + source_row(comp_count, 0, MAIN + j), 8), :]
                for r in range(2):
                    row = 2 * j + r
                    accs[at + r] = accs[at + r] + jnp.broadcast_to(k_tail[row : row + 1], (8, LANES)) * x
                at += 2
            return tuple(accs)

        count = 3 * comp_count * halves + 2 * TAIL
        zero = jnp.zeros((8, LANES), f32)

        def block(i, carry):
            accs, here = carry
            ahead = rows_of(lax.rem((i + 1) * UNROLL, list_count))
            for s, o in here:
                accs = pair(s, o, accs)
            return accs, ahead

        accs, _ = lax.fori_loop(0, list_count // UNROLL, block, ((zero,) * count, rows_of(0)))
        at = 0
        for c in range(comp_count):
            for h in range(halves):
                for part, value in enumerate((accs[at] - accs[at + 1], accs[at] + accs[at + 2])):
                    row = (part * comp_count + c) * box_count + t
                    total[pl.ds(row * PITCH + 8 * h, 8), :] = value
                at += 3
        for j in range(TAIL):
            own, cross = accs[at], accs[at + 1]
            up = jnp.concatenate([cross[comp_count:], cross[:comp_count]], axis=0)
            down = jnp.concatenate([cross[-comp_count:], cross[:-comp_count]], axis=0)
            total_tail[j, pl.ds(t * TAIL_PITCH, 8), :] = jnp.where(plus, own - up, own + down)
            at += 2


def inverse_kernel(total, total_tail, table, factor, out):
    comp_count, box_count, surf = out.shape
    f32, bf16 = jnp.float32, jnp.bfloat16
    groups = box_count // 8
    count = comp_count * box_count
    nt = (((1,), (1,)), ((), ()))
    result = jnp.zeros((2 * POINTS_PAD, 2 * count), f32)
    for n in range(2 * FREQ // PIECE):
        lanes = []
        for m in range(PIECE // LANES):
            part, j = divmod(n * (PIECE // LANES) + m, TILES)
            pieces = []
            for c in range(comp_count):
                for g in range(groups):
                    if j < MAIN:
                        row = (part * comp_count + c) * box_count + g * 8
                        pieces.append(total[pl.ds(row * PITCH + j, 8, stride=PITCH), :])
                    else:
                        row = g * 8 * TAIL_PITCH + part * comp_count + c
                        pieces.append(total_tail[j - MAIN, pl.ds(row, 8, stride=TAIL_PITCH), :])
            lanes.append(jnp.concatenate(pieces, axis=0))
        columns = slice(n * PIECE, (n + 1) * PIECE)
        x = jnp.concatenate(lanes, axis=1) * factor[:, columns]
        high = x.astype(bf16)
        low = (x - high.astype(f32)).astype(bf16)
        both = jnp.concatenate([high, low], axis=0)
        result += lax.dot_general(table[:, columns], both, nt, preferred_element_type=f32)
    result = result[:POINTS_PAD, :count] + result[:POINTS_PAD, count:] + result[POINTS_PAD:, :count]
    result = result.T
    for c in range(comp_count):
        out[c] = result[c * box_count : (c + 1) * box_count, :surf]


def translate_kernel(send_list, source, offset, density, from_near, relayed, *refs):
    *pieces, table, factor, hat, out, main, rows, total, total_tail = refs
    forward_kernel(send_list, density, from_near, relayed, *pieces, table, main, rows)
    interact_kernel(density.shape[0], source, offset, hat, main, total, total_tail)
    inverse_kernel(total, total_tail, table, factor, out)


def on_device(density, kernel_hat, send_list, halo_list, inter_src, inter_off):
    table, factor = transform_tables()
    box_count, comp_count, surf = density.shape
    _, peers, cap = send_list.shape
    rim = halo_list.shape[2]
    f32 = jnp.float32
    vmem = pl.BlockSpec(memory_space=pltpu.VMEM)
    smem = pl.BlockSpec(memory_space=pltpu.SMEM)
    density = density.transpose(1, 0, 2)

    boxes = jax.ShapeDtypeStruct((comp_count, cap, surf), f32)
    side = jax.ShapeDtypeStruct((comp_count, rim, surf), f32)
    to_near, *to_far, to_first, to_second = pl.pallas_call(
        pack_kernel,
        out_shape=(jax.ShapeDtypeStruct((2, *boxes.shape), f32),) + (boxes,) * (peers - 3) + (side,) * 2,
        in_specs=[vmem, smem, smem],
        out_specs=(vmem,) * peers,
        name="pack",
    )(density, send_list[0], halo_list[0])

    def swap(x, k):
        return lax.ppermute(x, "dev", [(i, i ^ k) for i in range(peers)])

    def swap_groups(x, start):
        pairs = [(i, i + 1) for i in range(start, lax.axis_size("group") - 1, 2)]
        return lax.ppermute(x, "group", pairs + [(j, i) for i, j in pairs])

    from_near = swap(to_near, 1)
    from_far = [swap(x, k) for x, k in zip(to_far, (2, *range(4, peers)))]
    from_first = swap_groups(to_first, 0)
    from_second = swap_groups(to_second, 1)
    by_part, near = lax.optimization_barrier((kernel_hat.transpose(1, 0, 2), from_near))
    relayed = swap(near, 2)

    offsets = kernel_hat.shape[0]
    hat = pl.pallas_call(
        prepare_kernel,
        out_shape=jax.ShapeDtypeStruct((offsets * HAT_ROWS + 8, LANES), f32),
        in_specs=[vmem],
        out_specs=vmem,
        compiler_params=pltpu.CompilerParams(vmem_limit_bytes=16 * 1024 * 1024),
        cost_estimate=pl.CostEstimate(flops=kernel_hat.size, bytes_accessed=6 * kernel_hat.size, transcendentals=0),
        name="prepare",
    )(by_part)

    slots = box_count + peers * cap + 2 * rim
    row_count = comp_count * slots
    arrays = (
        send_list[0], inter_src, inter_off, density, from_near, relayed, *from_far, from_first, from_second,
        jnp.asarray(table), jnp.asarray(factor), hat,
    )
    potential = pl.pallas_call(
        translate_kernel,
        out_shape=jax.ShapeDtypeStruct((comp_count, box_count, surf), f32),
        in_specs=[smem] * 3 + [vmem] * (len(arrays) - 3),
        out_specs=vmem,
        scratch_shapes=[
            pltpu.VMEM((slots * source_rows(comp_count) + 8, LANES), f32),
            pltpu.VMEM((row_count, POINTS_PAD), f32),
            pltpu.VMEM((2 * comp_count * box_count * PITCH, LANES), f32),
            pltpu.VMEM((TAIL, (box_count + 2) * TAIL_PITCH, LANES), f32),
        ],
        compiler_params=pltpu.CompilerParams(vmem_limit_bytes=24 * 1024 * 1024),
        name="translate",
    )(*arrays)
    return potential.transpose(1, 0, 2)


def solution(mesh):
    in_specs = (
        P(("group", "dev"), None, None),
        P(),
        P(("group", "dev"), None, None),
        P(("group", "dev"), None, None),
        P(("group", "dev"), None),
        P(("group", "dev"), None),
    )
    out_specs = P(("group", "dev"), None, None)
    return jax.shard_map(
        on_device, mesh=mesh, in_specs=in_specs, out_specs=out_specs, check_vma=False
    )
```

```python
import functools
import math

import jax
import jax.numpy as jnp
import ml_dtypes
import numpy as np
from jax import lax
from jax.experimental import pallas as pl
from jax.experimental.pallas import tpu as pltpu
from jax.sharding import PartitionSpec as P

ORDER = 6
GRID = 16
LANES = 128
HALF = GRID // 2 + 1
FREQ = GRID * GRID * HALF
TILES = FREQ // LANES
MAIN = 16
TAIL = TILES - MAIN
PITCH = MAIN + 1
TAIL_PITCH = 7
HAT_ROWS = 3 * MAIN + 2 * TAIL + 1
POINTS_PAD = 160
CHUNK = 256
PIECE = 512
UNROLL = 16


def surface_points(edge_count):
    points = [
        (i, j, k)
        for i in range(edge_count)
        for j in range(edge_count)
        for k in range(edge_count)
        if min(i, j, k) == 0 or max(i, j, k) == edge_count - 1
    ]
    return np.array(points, dtype=np.int64)


@functools.lru_cache(maxsize=None)
def transform_tables():
    points = surface_points(ORDER)
    kx, ky, kz = (a.reshape(-1) for a in np.meshgrid(np.arange(GRID), np.arange(GRID), np.arange(HALF), indexing="ij"))
    phase = (points[:, :1] * kx + points[:, 1:2] * ky + points[:, 2:] * kz) % GRID
    angle = phase * (2.0 * math.pi / GRID)
    table = np.zeros((POINTS_PAD, 2 * FREQ), np.float64)
    table[: len(points), :FREQ] = np.cos(angle)
    table[: len(points), FREQ:] = -np.sin(angle)
    table = np.where(np.abs(table) < 1e-9, 0.0, table)
    high = table.astype(ml_dtypes.bfloat16)
    low = (table - high.astype(np.float64)).astype(ml_dtypes.bfloat16)
    edge_plane = (kz == 0) | (kz == GRID // 2)
    factor = np.where(edge_plane, 1.0, 2.0) / GRID**3 * np.where((kx + ky + kz) % 2 == 0, 1.0, -1.0)
    factor = np.concatenate([factor, factor]).astype(np.float32)[None, :]
    return np.concatenate([high, low], axis=0), factor


def source_rows(comp_count):
    return (3 * comp_count * MAIN + TAIL * 8) | 1


def source_row(comp_count, which, tile):
    if tile < MAIN:
        return which * MAIN + tile
    return 3 * comp_count * MAIN + (tile - MAIN) * 8 + which


def kernel_row(which, tile):
    return which * MAIN + tile if tile < MAIN else 3 * MAIN + (tile - MAIN) * 2 + which


def pack_kernel(density, send_list, halo_list, *outs):
    peers, cap = send_list.shape
    rim = halo_list.shape[1]
    member = lax.axis_index("dev")
    parity = lax.rem(lax.axis_index("group"), 2)
    to_near, *to_far, to_first, to_second = outs
    for c in range(density.shape[0]):
        for e in range(cap):
            for part, k in enumerate((1, 3)):
                to_near[part, c, e : e + 1, :] = density[c, pl.ds(send_list[member ^ k, e], 1), :]
            for k, out in zip((2, *range(4, peers)), to_far):
                out[c, e : e + 1, :] = density[c, pl.ds(send_list[member ^ k, e], 1), :]
        for e in range(rim):
            to_first[c, e : e + 1, :] = density[c, pl.ds(halo_list[1 - parity, e], 1), :]
            to_second[c, e : e + 1, :] = density[c, pl.ds(halo_list[parity, e], 1), :]


def prepare_kernel(kernel_hat, hat):
    parts, count, _ = kernel_hat.shape

    def move(first, height):
        for j in range(TILES):
            re, im = (
                kernel_hat[part, pl.ds(first, height), j * LANES : (j + 1) * LANES].astype(jnp.float32)
                for part in range(parts)
            )
            for which, x in enumerate((re, re + im, im - re) if j < MAIN else (re, im)):
                for g in range(0, height, 8):
                    size = min(8, height - g)
                    row = (first + g) * HAT_ROWS + kernel_row(which, j)
                    hat[pl.ds(row, size, stride=HAT_ROWS), :] = x[g : g + size]

    whole = count // 16

    @pl.loop(0, whole)
    def _(i):
        move(pl.multiple_of(i * 16, 16), 16)

    if count % 16:
        move(whole * 16, count % 16)


def forward_kernel(send_list, density, from_near, relayed, *refs):
    *from_far, from_first, from_second, table, main, rows = refs
    comp_count, box_count, surf = density.shape
    peers, cap = send_list.shape
    rim = from_first.shape[1]
    row_count = rows.shape[0]
    slots = row_count // comp_count
    pitch = source_rows(comp_count)
    f32, bf16 = jnp.float32, jnp.bfloat16

    member = lax.axis_index("dev")
    parity = lax.rem(lax.axis_index("group"), 2)
    rows[...] = jnp.zeros_like(rows)
    pieces = {1: from_near.at[0], 2: relayed.at[0], 3: relayed.at[1]}
    pieces.update(zip(range(4, peers), from_far))
    for c in range(comp_count):
        base = c * slots
        rows[base : base + box_count, :surf] = density[c]
        base += box_count
        for e in range(cap):
            rows[pl.ds(base + member * cap + e, 1), :surf] = density[c, pl.ds(send_list[member, e], 1), :]
            for k, piece in pieces.items():
                rows[pl.ds(base + (member ^ k) * cap + e, 1), :surf] = piece[c, e : e + 1]
        base += peers * cap
        for e in range(rim):
            rows[pl.ds(base + (1 - parity) * rim + e, 1), :surf] = from_first[c, e : e + 1]
            rows[pl.ds(base + parity * rim + e, 1), :surf] = from_second[c, e : e + 1]

    value = rows[...]
    high = value.astype(bf16)
    low = (value - high.astype(f32)).astype(bf16)
    both = jnp.concatenate([high, low], axis=0)

    def spectrum(first):
        columns = slice(first, first + CHUNK)
        x = jnp.dot(both, table[:POINTS_PAD, columns], preferred_element_type=f32)
        x = x[:row_count] + x[row_count:]
        x = x + jnp.dot(high, table[POINTS_PAD:, columns], preferred_element_type=f32)
        return x.astype(bf16).astype(f32)

    for n in range(FREQ // CHUNK):
        re, im = spectrum(n * CHUNK), spectrum(FREQ + n * CHUNK)
        for m in range(CHUNK // LANES):
            j = n * (CHUNK // LANES) + m
            for g in range(row_count // 8):
                at = (slice(g * 8, (g + 1) * 8), slice(m * LANES, (m + 1) * LANES))
                c, s = divmod(g * 8, slots)
                pieces = [re[at], im[at]]
                if j < MAIN:
                    pieces.append(pieces[0] + pieces[1])
                for part, piece in enumerate(pieces):
                    row = source_row(comp_count, part * comp_count + c, j)
                    main[pl.ds(s * pitch + row, 8, stride=pitch), :] = piece


def interact_kernel(comp_count, source, offset, hat, main, total, total_tail):
    box_count, list_count = source.shape
    pitch = source_rows(comp_count)
    f32 = jnp.float32
    plus = lax.broadcasted_iota(jnp.int32, (8, LANES), 0) < comp_count
    halves = MAIN // 8

    @pl.loop(0, box_count)
    def _(t):
        def rows_of(first):
            return tuple(
                (source[t, first + u] * pitch, offset[t, first + u] * HAT_ROWS) for u in range(UNROLL)
            )

        def pair(s, o, accs):
            k = [[hat[pl.ds(o + kernel_row(r, 8 * h), 8), :] for h in range(halves)] for r in range(3)]
            accs = list(accs)
            at = 0
            for c in range(comp_count):
                for h in range(halves):
                    s_re, s_im, s_sum = (
                        main[pl.ds(s + source_row(comp_count, r * comp_count + c, 8 * h), 8), :] for r in range(3)
                    )
                    accs[at] = accs[at] + k[0][h] * s_sum
                    accs[at + 1] = accs[at + 1] + k[1][h] * s_im
                    accs[at + 2] = accs[at + 2] + k[2][h] * s_re
                    at += 3
            k_tail = hat[pl.ds(o + kernel_row(0, MAIN), 8), :]
            for j in range(TAIL):
                x = main[pl.ds(s + source_row(comp_count, 0, MAIN + j), 8), :]
                for r in range(2):
                    row = 2 * j + r
                    accs[at + r] = accs[at + r] + jnp.broadcast_to(k_tail[row : row + 1], (8, LANES)) * x
                at += 2
            return tuple(accs)

        count = 3 * comp_count * halves + 2 * TAIL
        zero = jnp.zeros((8, LANES), f32)

        def block(i, carry):
            accs, here = carry
            ahead = rows_of(lax.rem((i + 1) * UNROLL, list_count))
            for s, o in here:
                accs = pair(s, o, accs)
            return accs, ahead

        accs, _ = lax.fori_loop(0, list_count // UNROLL, block, ((zero,) * count, rows_of(0)))
        at = 0
        for c in range(comp_count):
            for h in range(halves):
                for part, value in enumerate((accs[at] - accs[at + 1], accs[at] + accs[at + 2])):
                    row = (part * comp_count + c) * box_count + t
                    total[pl.ds(row * PITCH + 8 * h, 8), :] = value
                at += 3
        for j in range(TAIL):
            own, cross = accs[at], accs[at + 1]
            up = jnp.concatenate([cross[comp_count:], cross[:comp_count]], axis=0)
            down = jnp.concatenate([cross[-comp_count:], cross[:-comp_count]], axis=0)
            total_tail[j, pl.ds(t * TAIL_PITCH, 8), :] = jnp.where(plus, own - up, own + down)
            at += 2


def inverse_kernel(total, total_tail, table, factor, out):
    comp_count, box_count, surf = out.shape
    f32, bf16 = jnp.float32, jnp.bfloat16
    groups = box_count // 8
    count = comp_count * box_count
    nt = (((1,), (1,)), ((), ()))
    result = jnp.zeros((2 * POINTS_PAD, 2 * count), f32)
    for n in range(2 * FREQ // PIECE):
        lanes = []
        for m in range(PIECE // LANES):
            part, j = divmod(n * (PIECE // LANES) + m, TILES)
            pieces = []
            for c in range(comp_count):
                for g in range(groups):
                    if j < MAIN:
                        row = (part * comp_count + c) * box_count + g * 8
                        pieces.append(total[pl.ds(row * PITCH + j, 8, stride=PITCH), :])
                    else:
                        row = g * 8 * TAIL_PITCH + part * comp_count + c
                        pieces.append(total_tail[j - MAIN, pl.ds(row, 8, stride=TAIL_PITCH), :])
            lanes.append(jnp.concatenate(pieces, axis=0))
        columns = slice(n * PIECE, (n + 1) * PIECE)
        x = jnp.concatenate(lanes, axis=1) * factor[:, columns]
        high = x.astype(bf16)
        low = (x - high.astype(f32)).astype(bf16)
        both = jnp.concatenate([high, low], axis=0)
        result += lax.dot_general(table[:, columns], both, nt, preferred_element_type=f32)
    result = result[:POINTS_PAD, :count] + result[:POINTS_PAD, count:] + result[POINTS_PAD:, :count]
    result = result.T
    for c in range(comp_count):
        out[c] = result[c * box_count : (c + 1) * box_count, :surf]


def translate_kernel(send_list, source, offset, density, from_near, relayed, *refs):
    *pieces, table, factor, hat, out, main, rows, total, total_tail = refs
    forward_kernel(send_list, density, from_near, relayed, *pieces, table, main, rows)
    interact_kernel(density.shape[0], source, offset, hat, main, total, total_tail)
    inverse_kernel(total, total_tail, table, factor, out)


def on_device(density, kernel_hat, send_list, halo_list, inter_src, inter_off):
    table, factor = transform_tables()
    box_count, comp_count, surf = density.shape
    _, peers, cap = send_list.shape
    rim = halo_list.shape[2]
    f32 = jnp.float32
    vmem = pl.BlockSpec(memory_space=pltpu.VMEM)
    smem = pl.BlockSpec(memory_space=pltpu.SMEM)
    density = density.transpose(1, 0, 2)

    boxes = jax.ShapeDtypeStruct((comp_count, cap, surf), f32)
    side = jax.ShapeDtypeStruct((comp_count, rim, surf), f32)
    to_near, to_two, *to_far, to_first, to_second = pl.pallas_call(
        pack_kernel,
        out_shape=(jax.ShapeDtypeStruct((2, *boxes.shape), f32),) + (boxes,) * (peers - 3) + (side,) * 2,
        in_specs=[vmem, smem, smem],
        out_specs=(vmem,) * peers,
        name="pack",
    )(density, send_list[0], halo_list[0])

    def swap(x, k):
        return lax.ppermute(x, "dev", [(i, i ^ k) for i in range(peers)])

    def swap_groups(x, start):
        pairs = [(i, i + 1) for i in range(start, lax.axis_size("group") - 1, 2)]
        return lax.ppermute(x, "group", pairs + [(j, i) for i, j in pairs])

    from_near = swap(to_near, 1)
    from_far = [swap(x, k) for x, k in zip(to_far, range(4, peers))]
    from_first = swap_groups(to_first, 0)
    from_second = swap_groups(to_second, 1)
    by_part, near = lax.optimization_barrier((kernel_hat.transpose(1, 0, 2), from_near))
    relayed = swap(jnp.stack([to_two, near[1]]), 2)

    offsets = kernel_hat.shape[0]
    hat = pl.pallas_call(
        prepare_kernel,
        out_shape=jax.ShapeDtypeStruct((offsets * HAT_ROWS + 8, LANES), f32),
        in_specs=[vmem],
        out_specs=vmem,
        compiler_params=pltpu.CompilerParams(vmem_limit_bytes=16 * 1024 * 1024),
        cost_estimate=pl.CostEstimate(flops=kernel_hat.size, bytes_accessed=6 * kernel_hat.size, transcendentals=0),
        name="prepare",
    )(by_part)

    slots = box_count + peers * cap + 2 * rim
    row_count = comp_count * slots
    arrays = (
        send_list[0], inter_src, inter_off, density, from_near, relayed, *from_far, from_first, from_second,
        jnp.asarray(table), jnp.asarray(factor), hat,
    )
    potential = pl.pallas_call(
        translate_kernel,
        out_shape=jax.ShapeDtypeStruct((comp_count, box_count, surf), f32),
        in_specs=[smem] * 3 + [vmem] * (len(arrays) - 3),
        out_specs=vmem,
        scratch_shapes=[
            pltpu.VMEM((slots * source_rows(comp_count) + 8, LANES), f32),
            pltpu.VMEM((row_count, POINTS_PAD), f32),
            pltpu.VMEM((2 * comp_count * box_count * PITCH, LANES), f32),
            pltpu.VMEM((TAIL, (box_count + 2) * TAIL_PITCH, LANES), f32),
        ],
        compiler_params=pltpu.CompilerParams(vmem_limit_bytes=24 * 1024 * 1024),
        name="translate",
    )(*arrays)
    return potential.transpose(1, 0, 2)


def solution(mesh):
    in_specs = (
        P(("group", "dev"), None, None),
        P(),
        P(("group", "dev"), None, None),
        P(("group", "dev"), None, None),
        P(("group", "dev"), None),
        P(("group", "dev"), None),
    )
    out_specs = P(("group", "dev"), None, None)
    return jax.shard_map(
        on_device, mesh=mesh, in_specs=in_specs, out_specs=out_specs, check_vma=False
    )
```

```python
import functools
import math

import jax
import jax.numpy as jnp
import ml_dtypes
import numpy as np
from jax import lax
from jax.experimental import pallas as pl
from jax.experimental.pallas import tpu as pltpu
from jax.sharding import PartitionSpec as P

ORDER = 6
GRID = 16
LANES = 128
HALF = GRID // 2 + 1
FREQ = GRID * GRID * HALF
TILES = FREQ // LANES
MAIN = 16
TAIL = TILES - MAIN
PITCH = MAIN + 1
TAIL_PITCH = 7
HAT_ROWS = 3 * MAIN + 2 * TAIL + 1
POINTS_PAD = 160
CHUNK = 256
PIECE = 512
UNROLL = 4


def surface_points(edge_count):
    points = [
        (i, j, k)
        for i in range(edge_count)
        for j in range(edge_count)
        for k in range(edge_count)
        if min(i, j, k) == 0 or max(i, j, k) == edge_count - 1
    ]
    return np.array(points, dtype=np.int64)


@functools.lru_cache(maxsize=None)
def transform_tables():
    points = surface_points(ORDER)
    kx, ky, kz = (a.reshape(-1) for a in np.meshgrid(np.arange(GRID), np.arange(GRID), np.arange(HALF), indexing="ij"))
    phase = (points[:, :1] * kx + points[:, 1:2] * ky + points[:, 2:] * kz) % GRID
    angle = phase * (2.0 * math.pi / GRID)
    table = np.zeros((POINTS_PAD, 2 * FREQ), np.float64)
    table[: len(points), :FREQ] = np.cos(angle)
    table[: len(points), FREQ:] = -np.sin(angle)
    table = np.where(np.abs(table) < 1e-9, 0.0, table)
    high = table.astype(ml_dtypes.bfloat16)
    low = (table - high.astype(np.float64)).astype(ml_dtypes.bfloat16)
    edge_plane = (kz == 0) | (kz == GRID // 2)
    factor = np.where(edge_plane, 1.0, 2.0) / GRID**3 * np.where((kx + ky + kz) % 2 == 0, 1.0, -1.0)
    factor = np.concatenate([factor, factor]).astype(np.float32)[None, :]
    return np.concatenate([high, low], axis=0), factor


def source_rows(comp_count):
    return (3 * comp_count * MAIN + TAIL * 8) | 1


def source_row(comp_count, which, tile):
    if tile < MAIN:
        return which * MAIN + tile
    return 3 * comp_count * MAIN + (tile - MAIN) * 8 + which


def kernel_row(which, tile):
    return which * MAIN + tile if tile < MAIN else 3 * MAIN + (tile - MAIN) * 2 + which


def pack_kernel(density, send_list, halo_list, *outs):
    peers, cap = send_list.shape
    rim = halo_list.shape[1]
    member = lax.axis_index("dev")
    parity = lax.rem(lax.axis_index("group"), 2)
    to_near, *to_far, to_first, to_second = outs
    for c in range(density.shape[0]):
        for e in range(cap):
            for part, k in enumerate((1, 3)):
                to_near[part, c, e : e + 1, :] = density[c, pl.ds(send_list[member ^ k, e], 1), :]
            for k, out in zip((2, *range(4, peers)), to_far):
                out[c, e : e + 1, :] = density[c, pl.ds(send_list[member ^ k, e], 1), :]
        for e in range(rim):
            to_first[c, e : e + 1, :] = density[c, pl.ds(halo_list[1 - parity, e], 1), :]
            to_second[c, e : e + 1, :] = density[c, pl.ds(halo_list[parity, e], 1), :]


def prepare_kernel(kernel_hat, hat):
    parts, count, _ = kernel_hat.shape

    def move(first, height):
        for j in range(TILES):
            re, im = (
                kernel_hat[part, pl.ds(first, height), j * LANES : (j + 1) * LANES].astype(jnp.float32)
                for part in range(parts)
            )
            for which, x in enumerate((re, re + im, im - re) if j < MAIN else (re, im)):
                for g in range(0, height, 8):
                    size = min(8, height - g)
                    row = (first + g) * HAT_ROWS + kernel_row(which, j)
                    hat[pl.ds(row, size, stride=HAT_ROWS), :] = x[g : g + size]

    whole = count // 16

    @pl.loop(0, whole)
    def _(i):
        move(pl.multiple_of(i * 16, 16), 16)

    if count % 16:
        move(whole * 16, count % 16)


def forward_kernel(send_list, density, from_near, relayed, *refs):
    *from_far, from_first, from_second, table, main, rows = refs
    comp_count, box_count, surf = density.shape
    peers, cap = send_list.shape
    rim = from_first.shape[1]
    row_count = rows.shape[0]
    slots = row_count // comp_count
    pitch = source_rows(comp_count)
    f32, bf16 = jnp.float32, jnp.bfloat16

    member = lax.axis_index("dev")
    parity = lax.rem(lax.axis_index("group"), 2)
    rows[...] = jnp.zeros_like(rows)
    pieces = {1: from_near.at[0], 2: relayed.at[0], 3: relayed.at[1]}
    pieces.update(zip(range(4, peers), from_far))
    for c in range(comp_count):
        base = c * slots
        rows[base : base + box_count, :surf] = density[c]
        base += box_count
        for e in range(cap):
            rows[pl.ds(base + member * cap + e, 1), :surf] = density[c, pl.ds(send_list[member, e], 1), :]
            for k, piece in pieces.items():
                rows[pl.ds(base + (member ^ k) * cap + e, 1), :surf] = piece[c, e : e + 1]
        base += peers * cap
        for e in range(rim):
            rows[pl.ds(base + (1 - parity) * rim + e, 1), :surf] = from_first[c, e : e + 1]
            rows[pl.ds(base + parity * rim + e, 1), :surf] = from_second[c, e : e + 1]

    value = rows[...]
    high = value.astype(bf16)
    low = (value - high.astype(f32)).astype(bf16)
    both = jnp.concatenate([high, low], axis=0)

    def spectrum(first):
        columns = slice(first, first + CHUNK)
        x = jnp.dot(both, table[:POINTS_PAD, columns], preferred_element_type=f32)
        x = x[:row_count] + x[row_count:]
        x = x + jnp.dot(high, table[POINTS_PAD:, columns], preferred_element_type=f32)
        return x.astype(bf16).astype(f32)

    for n in range(FREQ // CHUNK):
        re, im = spectrum(n * CHUNK), spectrum(FREQ + n * CHUNK)
        for m in range(CHUNK // LANES):
            j = n * (CHUNK // LANES) + m
            for g in range(row_count // 8):
                at = (slice(g * 8, (g + 1) * 8), slice(m * LANES, (m + 1) * LANES))
                c, s = divmod(g * 8, slots)
                pieces = [re[at], im[at]]
                if j < MAIN:
                    pieces.append(pieces[0] + pieces[1])
                for part, piece in enumerate(pieces):
                    row = source_row(comp_count, part * comp_count + c, j)
                    main[pl.ds(s * pitch + row, 8, stride=pitch), :] = piece


def interact_kernel(comp_count, source, offset, hat, main, total, total_tail):
    box_count, list_count = source.shape
    pitch = source_rows(comp_count)
    f32 = jnp.float32
    plus = lax.broadcasted_iota(jnp.int32, (8, LANES), 0) < comp_count
    halves = MAIN // 8

    @pl.loop(0, box_count)
    def _(t):
        def rows_of(first):
            return tuple(
                (source[t, first + u] * pitch, offset[t, first + u] * HAT_ROWS) for u in range(UNROLL)
            )

        def pair(s, o, accs):
            k = [[hat[pl.ds(o + kernel_row(r, 8 * h), 8), :] for h in range(halves)] for r in range(3)]
            accs = list(accs)
            at = 0
            for c in range(comp_count):
                for h in range(halves):
                    s_re, s_im, s_sum = (
                        main[pl.ds(s + source_row(comp_count, r * comp_count + c, 8 * h), 8), :] for r in range(3)
                    )
                    accs[at] = accs[at] + k[0][h] * s_sum
                    accs[at + 1] = accs[at + 1] + k[1][h] * s_im
                    accs[at + 2] = accs[at + 2] + k[2][h] * s_re
                    at += 3
            k_tail = hat[pl.ds(o + kernel_row(0, MAIN), 8), :]
            for j in range(TAIL):
                x = main[pl.ds(s + source_row(comp_count, 0, MAIN + j), 8), :]
                for r in range(2):
                    row = 2 * j + r
                    accs[at + r] = accs[at + r] + jnp.broadcast_to(k_tail[row : row + 1], (8, LANES)) * x
                at += 2
            return tuple(accs)

        count = 3 * comp_count * halves + 2 * TAIL
        zero = jnp.zeros((8, LANES), f32)

        def block(i, carry):
            accs, here = carry
            ahead = rows_of(lax.rem((i + 1) * UNROLL, list_count))
            for s, o in here:
                accs = pair(s, o, accs)
            return accs, ahead

        accs, _ = lax.fori_loop(0, list_count // UNROLL, block, ((zero,) * count, rows_of(0)))
        at = 0
        for c in range(comp_count):
            for h in range(halves):
                for part, value in enumerate((accs[at] - accs[at + 1], accs[at] + accs[at + 2])):
                    row = (part * comp_count + c) * box_count + t
                    total[pl.ds(row * PITCH + 8 * h, 8), :] = value
                at += 3
        for j in range(TAIL):
            own, cross = accs[at], accs[at + 1]
            up = jnp.concatenate([cross[comp_count:], cross[:comp_count]], axis=0)
            down = jnp.concatenate([cross[-comp_count:], cross[:-comp_count]], axis=0)
            total_tail[j, pl.ds(t * TAIL_PITCH, 8), :] = jnp.where(plus, own - up, own + down)
            at += 2


def inverse_kernel(total, total_tail, table, factor, out):
    comp_count, box_count, surf = out.shape
    f32, bf16 = jnp.float32, jnp.bfloat16
    groups = box_count // 8
    count = comp_count * box_count
    nt = (((1,), (1,)), ((), ()))
    result = jnp.zeros((2 * POINTS_PAD, 2 * count), f32)
    for n in range(2 * FREQ // PIECE):
        lanes = []
        for m in range(PIECE // LANES):
            part, j = divmod(n * (PIECE // LANES) + m, TILES)
            pieces = []
            for c in range(comp_count):
                for g in range(groups):
                    if j < MAIN:
                        row = (part * comp_count + c) * box_count + g * 8
                        pieces.append(total[pl.ds(row * PITCH + j, 8, stride=PITCH), :])
                    else:
                        row = g * 8 * TAIL_PITCH + part * comp_count + c
                        pieces.append(total_tail[j - MAIN, pl.ds(row, 8, stride=TAIL_PITCH), :])
            lanes.append(jnp.concatenate(pieces, axis=0))
        columns = slice(n * PIECE, (n + 1) * PIECE)
        x = jnp.concatenate(lanes, axis=1) * factor[:, columns]
        high = x.astype(bf16)
        low = (x - high.astype(f32)).astype(bf16)
        both = jnp.concatenate([high, low], axis=0)
        result += lax.dot_general(table[:, columns], both, nt, preferred_element_type=f32)
    result = result[:POINTS_PAD, :count] + result[:POINTS_PAD, count:] + result[POINTS_PAD:, :count]
    result = result.T
    for c in range(comp_count):
        out[c] = result[c * box_count : (c + 1) * box_count, :surf]


def translate_kernel(send_list, source, offset, density, from_near, relayed, *refs):
    *pieces, table, factor, hat, out, main, rows, total, total_tail = refs
    forward_kernel(send_list, density, from_near, relayed, *pieces, table, main, rows)
    interact_kernel(density.shape[0], source, offset, hat, main, total, total_tail)
    inverse_kernel(total, total_tail, table, factor, out)


def on_device(density, kernel_hat, send_list, halo_list, inter_src, inter_off):
    table, factor = transform_tables()
    box_count, comp_count, surf = density.shape
    _, peers, cap = send_list.shape
    rim = halo_list.shape[2]
    f32 = jnp.float32
    vmem = pl.BlockSpec(memory_space=pltpu.VMEM)
    smem = pl.BlockSpec(memory_space=pltpu.SMEM)
    density = density.transpose(1, 0, 2)

    boxes = jax.ShapeDtypeStruct((comp_count, cap, surf), f32)
    side = jax.ShapeDtypeStruct((comp_count, rim, surf), f32)
    to_near, to_two, *to_far, to_first, to_second = pl.pallas_call(
        pack_kernel,
        out_shape=(jax.ShapeDtypeStruct((2, *boxes.shape), f32),) + (boxes,) * (peers - 3) + (side,) * 2,
        in_specs=[vmem, smem, smem],
        out_specs=(vmem,) * peers,
        name="pack",
    )(density, send_list[0], halo_list[0])

    def swap(x, k):
        return lax.ppermute(x, "dev", [(i, i ^ k) for i in range(peers)])

    def swap_groups(x, start):
        pairs = [(i, i + 1) for i in range(start, lax.axis_size("group") - 1, 2)]
        return lax.ppermute(x, "group", pairs + [(j, i) for i, j in pairs])

    from_near = swap(to_near, 1)
    from_far = [swap(x, k) for x, k in zip(to_far, range(4, peers))]
    from_first = swap_groups(to_first, 0)
    from_second = swap_groups(to_second, 1)
    by_part, near = lax.optimization_barrier((kernel_hat.transpose(1, 0, 2), from_near))
    relayed = swap(jnp.stack([to_two, near[1]]), 2)

    offsets = kernel_hat.shape[0]
    hat = pl.pallas_call(
        prepare_kernel,
        out_shape=jax.ShapeDtypeStruct((offsets * HAT_ROWS + 8, LANES), f32),
        in_specs=[vmem],
        out_specs=vmem,
        compiler_params=pltpu.CompilerParams(vmem_limit_bytes=16 * 1024 * 1024),
        cost_estimate=pl.CostEstimate(flops=kernel_hat.size, bytes_accessed=6 * kernel_hat.size, transcendentals=0),
        name="prepare",
    )(by_part)

    slots = box_count + peers * cap + 2 * rim
    row_count = comp_count * slots
    arrays = (
        send_list[0], inter_src, inter_off, density, from_near, relayed, *from_far, from_first, from_second,
        jnp.asarray(table), jnp.asarray(factor), hat,
    )
    potential = pl.pallas_call(
        translate_kernel,
        out_shape=jax.ShapeDtypeStruct((comp_count, box_count, surf), f32),
        in_specs=[smem] * 3 + [vmem] * (len(arrays) - 3),
        out_specs=vmem,
        scratch_shapes=[
            pltpu.VMEM((slots * source_rows(comp_count) + 8, LANES), f32),
            pltpu.VMEM((row_count, POINTS_PAD), f32),
            pltpu.VMEM((2 * comp_count * box_count * PITCH, LANES), f32),
            pltpu.VMEM((TAIL, (box_count + 2) * TAIL_PITCH, LANES), f32),
        ],
        compiler_params=pltpu.CompilerParams(vmem_limit_bytes=24 * 1024 * 1024),
        name="translate",
    )(*arrays)
    return potential.transpose(1, 0, 2)


def solution(mesh):
    in_specs = (
        P(("group", "dev"), None, None),
        P(),
        P(("group", "dev"), None, None),
        P(("group", "dev"), None, None),
        P(("group", "dev"), None),
        P(("group", "dev"), None),
    )
    out_specs = P(("group", "dev"), None, None)
    return jax.shard_map(
        on_device, mesh=mesh, in_specs=in_specs, out_specs=out_specs, check_vma=False
    )
```

```python
import functools
import math

import jax
import jax.numpy as jnp
import ml_dtypes
import numpy as np
from jax import lax
from jax.experimental import pallas as pl
from jax.experimental.pallas import tpu as pltpu
from jax.sharding import PartitionSpec as P

ORDER = 6
GRID = 16
LANES = 128
HALF = GRID // 2 + 1
FREQ = GRID * GRID * HALF
TILES = FREQ // LANES
MAIN = 16
TAIL = TILES - MAIN
PITCH = MAIN + 1
TAIL_PITCH = 7
HAT_ROWS = 3 * MAIN + 2 * TAIL + 1
POINTS_PAD = 160
CHUNK = 256
PIECE = 512
UNROLL = 8


def surface_points(edge_count):
    points = [
        (i, j, k)
        for i in range(edge_count)
        for j in range(edge_count)
        for k in range(edge_count)
        if min(i, j, k) == 0 or max(i, j, k) == edge_count - 1
    ]
    return np.array(points, dtype=np.int64)


@functools.lru_cache(maxsize=None)
def transform_tables():
    points = surface_points(ORDER)
    kx, ky, kz = (a.reshape(-1) for a in np.meshgrid(np.arange(GRID), np.arange(GRID), np.arange(HALF), indexing="ij"))
    phase = (points[:, :1] * kx + points[:, 1:2] * ky + points[:, 2:] * kz) % GRID
    angle = phase * (2.0 * math.pi / GRID)
    table = np.zeros((POINTS_PAD, 2 * FREQ), np.float64)
    table[: len(points), :FREQ] = np.cos(angle)
    table[: len(points), FREQ:] = -np.sin(angle)
    table = np.where(np.abs(table) < 1e-9, 0.0, table)
    high = table.astype(ml_dtypes.bfloat16)
    low = (table - high.astype(np.float64)).astype(ml_dtypes.bfloat16)
    edge_plane = (kz == 0) | (kz == GRID // 2)
    factor = np.where(edge_plane, 1.0, 2.0) / GRID**3 * np.where((kx + ky + kz) % 2 == 0, 1.0, -1.0)
    factor = np.concatenate([factor, factor]).astype(np.float32)[None, :]
    return np.concatenate([high, low], axis=0), factor


def source_rows(comp_count):
    return (3 * comp_count * MAIN + TAIL * 8) | 1


def source_row(comp_count, which, tile):
    if tile < MAIN:
        return which * MAIN + tile
    return 3 * comp_count * MAIN + (tile - MAIN) * 8 + which


def kernel_row(which, tile):
    return which * MAIN + tile if tile < MAIN else 3 * MAIN + (tile - MAIN) * 2 + which


def pack_kernel(density, send_list, halo_list, *outs):
    peers, cap = send_list.shape
    rim = halo_list.shape[1]
    member = lax.axis_index("dev")
    parity = lax.rem(lax.axis_index("group"), 2)
    to_near, *to_far, to_first, to_second = outs
    for c in range(density.shape[0]):
        for e in range(cap):
            for part, k in enumerate((1, 3)):
                to_near[part, c, e : e + 1, :] = density[c, pl.ds(send_list[member ^ k, e], 1), :]
            for k, out in zip((2, *range(4, peers)), to_far):
                out[c, e : e + 1, :] = density[c, pl.ds(send_list[member ^ k, e], 1), :]
        for e in range(rim):
            to_first[c, e : e + 1, :] = density[c, pl.ds(halo_list[1 - parity, e], 1), :]
            to_second[c, e : e + 1, :] = density[c, pl.ds(halo_list[parity, e], 1), :]


def prepare_kernel(kernel_hat, hat):
    parts, count, _ = kernel_hat.shape

    def move(first, height):
        for j in range(TILES):
            re, im = (
                kernel_hat[part, pl.ds(first, height), j * LANES : (j + 1) * LANES].astype(jnp.float32)
                for part in range(parts)
            )
            for which, x in enumerate((re, re + im, im - re) if j < MAIN else (re, im)):
                for g in range(0, height, 8):
                    size = min(8, height - g)
                    row = (first + g) * HAT_ROWS + kernel_row(which, j)
                    hat[pl.ds(row, size, stride=HAT_ROWS), :] = x[g : g + size]

    whole = count // 16

    @pl.loop(0, whole)
    def _(i):
        move(pl.multiple_of(i * 16, 16), 16)

    if count % 16:
        move(whole * 16, count % 16)


def forward_kernel(send_list, density, from_near, relayed, *refs):
    *from_far, from_first, from_second, table, main, rows = refs
    comp_count, box_count, surf = density.shape
    peers, cap = send_list.shape
    rim = from_first.shape[1]
    row_count = rows.shape[0]
    slots = row_count // comp_count
    pitch = source_rows(comp_count)
    f32, bf16 = jnp.float32, jnp.bfloat16

    member = lax.axis_index("dev")
    parity = lax.rem(lax.axis_index("group"), 2)
    rows[...] = jnp.zeros_like(rows)
    pieces = {1: from_near.at[0], 2: relayed.at[0], 3: relayed.at[1]}
    pieces.update(zip(range(4, peers), from_far))
    for c in range(comp_count):
        base = c * slots
        rows[base : base + box_count, :surf] = density[c]
        base += box_count
        for e in range(cap):
            rows[pl.ds(base + member * cap + e, 1), :surf] = density[c, pl.ds(send_list[member, e], 1), :]
            for k, piece in pieces.items():
                rows[pl.ds(base + (member ^ k) * cap + e, 1), :surf] = piece[c, e : e + 1]
        base += peers * cap
        for e in range(rim):
            rows[pl.ds(base + (1 - parity) * rim + e, 1), :surf] = from_first[c, e : e + 1]
            rows[pl.ds(base + parity * rim + e, 1), :surf] = from_second[c, e : e + 1]

    value = rows[...]
    high = value.astype(bf16)
    low = (value - high.astype(f32)).astype(bf16)
    both = jnp.concatenate([high, low], axis=0)

    def spectrum(first):
        columns = slice(first, first + CHUNK)
        x = jnp.dot(both, table[:POINTS_PAD, columns], preferred_element_type=f32)
        x = x[:row_count] + x[row_count:]
        x = x + jnp.dot(high, table[POINTS_PAD:, columns], preferred_element_type=f32)
        return x.astype(bf16).astype(f32)

    for n in range(FREQ // CHUNK):
        re, im = spectrum(n * CHUNK), spectrum(FREQ + n * CHUNK)
        for m in range(CHUNK // LANES):
            j = n * (CHUNK // LANES) + m
            for g in range(row_count // 8):
                at = (slice(g * 8, (g + 1) * 8), slice(m * LANES, (m + 1) * LANES))
                c, s = divmod(g * 8, slots)
                pieces = [re[at], im[at]]
                if j < MAIN:
                    pieces.append(pieces[0] + pieces[1])
                for part, piece in enumerate(pieces):
                    row = source_row(comp_count, part * comp_count + c, j)
                    main[pl.ds(s * pitch + row, 8, stride=pitch), :] = piece


def interact_kernel(comp_count, source, offset, hat, main, total, total_tail):
    box_count, list_count = source.shape
    pitch = source_rows(comp_count)
    f32 = jnp.float32
    plus = lax.broadcasted_iota(jnp.int32, (8, LANES), 0) < comp_count
    halves = MAIN // 8

    @pl.loop(0, box_count)
    def _(t):
        def rows_of(first):
            return tuple(
                (source[t, first + u] * pitch, offset[t, first + u] * HAT_ROWS) for u in range(UNROLL)
            )

        def pair(s, o, accs):
            k = [[hat[pl.ds(o + kernel_row(r, 8 * h), 8), :] for h in range(halves)] for r in range(3)]
            accs = list(accs)
            at = 0
            for c in range(comp_count):
                for h in range(halves):
                    s_re, s_im, s_sum = (
                        main[pl.ds(s + source_row(comp_count, r * comp_count + c, 8 * h), 8), :] for r in range(3)
                    )
                    accs[at] = accs[at] + k[0][h] * s_sum
                    accs[at + 1] = accs[at + 1] + k[1][h] * s_im
                    accs[at + 2] = accs[at + 2] + k[2][h] * s_re
                    at += 3
            k_tail = hat[pl.ds(o + kernel_row(0, MAIN), 8), :]
            for j in range(TAIL):
                x = main[pl.ds(s + source_row(comp_count, 0, MAIN + j), 8), :]
                for r in range(2):
                    row = 2 * j + r
                    accs[at + r] = accs[at + r] + jnp.broadcast_to(k_tail[row : row + 1], (8, LANES)) * x
                at += 2
            return tuple(accs)

        count = 3 * comp_count * halves + 2 * TAIL
        zero = jnp.zeros((8, LANES), f32)

        def block(i, carry):
            accs, here = carry
            ahead = rows_of(lax.rem((i + 1) * UNROLL, list_count))
            for s, o in here:
                accs = pair(s, o, accs)
            return accs, ahead

        accs, _ = lax.fori_loop(0, list_count // UNROLL, block, ((zero,) * count, rows_of(0)))
        at = 0
        for c in range(comp_count):
            for h in range(halves):
                for part, value in enumerate((accs[at] - accs[at + 1], accs[at] + accs[at + 2])):
                    row = (part * comp_count + c) * box_count + t
                    total[pl.ds(row * PITCH + 8 * h, 8), :] = value
                at += 3
        for j in range(TAIL):
            own, cross = accs[at], accs[at + 1]
            up = jnp.concatenate([cross[comp_count:], cross[:comp_count]], axis=0)
            down = jnp.concatenate([cross[-comp_count:], cross[:-comp_count]], axis=0)
            total_tail[j, pl.ds(t * TAIL_PITCH, 8), :] = jnp.where(plus, own - up, own + down)
            at += 2


def inverse_kernel(total, total_tail, table, factor, out):
    comp_count, box_count, surf = out.shape
    f32, bf16 = jnp.float32, jnp.bfloat16
    groups = box_count // 8
    count = comp_count * box_count
    nt = (((1,), (1,)), ((), ()))
    result = jnp.zeros((2 * POINTS_PAD, 2 * count), f32)
    for n in range(2 * FREQ // PIECE):
        lanes = []
        for m in range(PIECE // LANES):
            part, j = divmod(n * (PIECE // LANES) + m, TILES)
            pieces = []
            for c in range(comp_count):
                for g in range(groups):
                    if j < MAIN:
                        row = (part * comp_count + c) * box_count + g * 8
                        pieces.append(total[pl.ds(row * PITCH + j, 8, stride=PITCH), :])
                    else:
                        row = g * 8 * TAIL_PITCH + part * comp_count + c
                        pieces.append(total_tail[j - MAIN, pl.ds(row, 8, stride=TAIL_PITCH), :])
            lanes.append(jnp.concatenate(pieces, axis=0))
        columns = slice(n * PIECE, (n + 1) * PIECE)
        x = jnp.concatenate(lanes, axis=1) * factor[:, columns]
        high = x.astype(bf16)
        low = (x - high.astype(f32)).astype(bf16)
        both = jnp.concatenate([high, low], axis=0)
        result += lax.dot_general(table[:, columns], both, nt, preferred_element_type=f32)
    result = result[:POINTS_PAD, :count] + result[:POINTS_PAD, count:] + result[POINTS_PAD:, :count]
    result = result.T
    for c in range(comp_count):
        out[c] = result[c * box_count : (c + 1) * box_count, :surf]


def translate_kernel(send_list, source, offset, density, from_near, relayed, *refs):
    *pieces, table, factor, hat, out, main, rows, total, total_tail = refs
    forward_kernel(send_list, density, from_near, relayed, *pieces, table, main, rows)
    interact_kernel(density.shape[0], source, offset, hat, main, total, total_tail)
    inverse_kernel(total, total_tail, table, factor, out)


def on_device(density, kernel_hat, send_list, halo_list, inter_src, inter_off):
    table, factor = transform_tables()
    box_count, comp_count, surf = density.shape
    _, peers, cap = send_list.shape
    rim = halo_list.shape[2]
    f32 = jnp.float32
    vmem = pl.BlockSpec(memory_space=pltpu.VMEM)
    smem = pl.BlockSpec(memory_space=pltpu.SMEM)
    density = density.transpose(1, 0, 2)

    boxes = jax.ShapeDtypeStruct((comp_count, cap, surf), f32)
    side = jax.ShapeDtypeStruct((comp_count, rim, surf), f32)
    to_near, to_two, *to_far, to_first, to_second = pl.pallas_call(
        pack_kernel,
        out_shape=(jax.ShapeDtypeStruct((2, *boxes.shape), f32),) + (boxes,) * (peers - 3) + (side,) * 2,
        in_specs=[vmem, smem, smem],
        out_specs=(vmem,) * peers,
        name="pack",
    )(density, send_list[0], halo_list[0])

    def swap(x, k):
        return lax.ppermute(x, "dev", [(i, i ^ k) for i in range(peers)])

    def swap_groups(x, start):
        pairs = [(i, i + 1) for i in range(start, lax.axis_size("group") - 1, 2)]
        return lax.ppermute(x, "group", pairs + [(j, i) for i, j in pairs])

    from_near = swap(to_near, 1)
    from_far = [swap(x, k) for x, k in zip(to_far, range(4, peers))]
    from_first = swap_groups(to_first, 0)
    from_second = swap_groups(to_second, 1)
    by_part, near = lax.optimization_barrier((kernel_hat.transpose(1, 0, 2), from_near))
    relayed = swap(jnp.stack([to_two, near[1]]), 2)

    offsets = kernel_hat.shape[0]
    hat = pl.pallas_call(
        prepare_kernel,
        out_shape=jax.ShapeDtypeStruct((offsets * HAT_ROWS + 8, LANES), f32),
        in_specs=[vmem],
        out_specs=vmem,
        compiler_params=pltpu.CompilerParams(vmem_limit_bytes=16 * 1024 * 1024),
        cost_estimate=pl.CostEstimate(flops=kernel_hat.size, bytes_accessed=6 * kernel_hat.size, transcendentals=0),
        name="prepare",
    )(by_part)

    slots = box_count + peers * cap + 2 * rim
    row_count = comp_count * slots
    arrays = (
        send_list[0], inter_src, inter_off, density, from_near, relayed, *from_far, from_first, from_second,
        jnp.asarray(table), jnp.asarray(factor), hat,
    )
    potential = pl.pallas_call(
        translate_kernel,
        out_shape=jax.ShapeDtypeStruct((comp_count, box_count, surf), f32),
        in_specs=[smem] * 3 + [vmem] * (len(arrays) - 3),
        out_specs=vmem,
        scratch_shapes=[
            pltpu.VMEM((slots * source_rows(comp_count) + 8, LANES), f32),
            pltpu.VMEM((row_count, POINTS_PAD), f32),
            pltpu.VMEM((2 * comp_count * box_count * PITCH, LANES), f32),
            pltpu.VMEM((TAIL, (box_count + 2) * TAIL_PITCH, LANES), f32),
        ],
        compiler_params=pltpu.CompilerParams(vmem_limit_bytes=24 * 1024 * 1024),
        name="translate",
    )(*arrays)
    return potential.transpose(1, 0, 2)


def solution(mesh):
    in_specs = (
        P(("group", "dev"), None, None),
        P(),
        P(("group", "dev"), None, None),
        P(("group", "dev"), None, None),
        P(("group", "dev"), None),
        P(("group", "dev"), None),
    )
    out_specs = P(("group", "dev"), None, None)
    return jax.shard_map(
        on_device, mesh=mesh, in_specs=in_specs, out_specs=out_specs, check_vma=False
    )
```

```python
import functools
import math

import jax
import jax.numpy as jnp
import ml_dtypes
import numpy as np
from jax import lax
from jax.experimental import pallas as pl
from jax.experimental.pallas import tpu as pltpu
from jax.sharding import PartitionSpec as P

ORDER = 6
GRID = 16
LANES = 128
HALF = GRID // 2 + 1
FREQ = GRID * GRID * HALF
TILES = FREQ // LANES
MAIN = 16
TAIL = TILES - MAIN
PITCH = MAIN + 1
TAIL_PITCH = 7
HAT_ROWS = 3 * MAIN + 2 * TAIL + 1
POINTS_PAD = 160
CHUNK = 256
PIECE = 2304
UNROLL = 8


def surface_points(edge_count):
    points = [
        (i, j, k)
        for i in range(edge_count)
        for j in range(edge_count)
        for k in range(edge_count)
        if min(i, j, k) == 0 or max(i, j, k) == edge_count - 1
    ]
    return np.array(points, dtype=np.int64)


@functools.lru_cache(maxsize=None)
def transform_tables():
    points = surface_points(ORDER)
    kx, ky, kz = (a.reshape(-1) for a in np.meshgrid(np.arange(GRID), np.arange(GRID), np.arange(HALF), indexing="ij"))
    phase = (points[:, :1] * kx + points[:, 1:2] * ky + points[:, 2:] * kz) % GRID
    angle = phase * (2.0 * math.pi / GRID)
    table = np.zeros((POINTS_PAD, 2 * FREQ), np.float64)
    table[: len(points), :FREQ] = np.cos(angle)
    table[: len(points), FREQ:] = -np.sin(angle)
    table = np.where(np.abs(table) < 1e-9, 0.0, table)
    high = table.astype(ml_dtypes.bfloat16)
    low = (table - high.astype(np.float64)).astype(ml_dtypes.bfloat16)
    edge_plane = (kz == 0) | (kz == GRID // 2)
    factor = np.where(edge_plane, 1.0, 2.0) / GRID**3 * np.where((kx + ky + kz) % 2 == 0, 1.0, -1.0)
    factor = np.concatenate([factor, factor]).astype(np.float32)[None, :]
    return np.concatenate([high, low], axis=0), factor


def source_rows(comp_count):
    return (3 * comp_count * MAIN + TAIL * 8) | 1


def source_row(comp_count, which, tile):
    if tile < MAIN:
        return which * MAIN + tile
    return 3 * comp_count * MAIN + (tile - MAIN) * 8 + which


def kernel_row(which, tile):
    return which * MAIN + tile if tile < MAIN else 3 * MAIN + (tile - MAIN) * 2 + which


def pack_kernel(density, send_list, halo_list, *outs):
    peers, cap = send_list.shape
    rim = halo_list.shape[1]
    member = lax.axis_index("dev")
    parity = lax.rem(lax.axis_index("group"), 2)
    to_near, *to_far, to_first, to_second = outs
    for c in range(density.shape[0]):
        for e in range(cap):
            for part, k in enumerate((1, 3)):
                to_near[part, c, e : e + 1, :] = density[c, pl.ds(send_list[member ^ k, e], 1), :]
            for k, out in zip((2, *range(4, peers)), to_far):
                out[c, e : e + 1, :] = density[c, pl.ds(send_list[member ^ k, e], 1), :]
        for e in range(rim):
            to_first[c, e : e + 1, :] = density[c, pl.ds(halo_list[1 - parity, e], 1), :]
            to_second[c, e : e + 1, :] = density[c, pl.ds(halo_list[parity, e], 1), :]


def prepare_kernel(kernel_hat, hat):
    parts, count, _ = kernel_hat.shape

    def move(first, height):
        for j in range(TILES):
            re, im = (
                kernel_hat[part, pl.ds(first, height), j * LANES : (j + 1) * LANES].astype(jnp.float32)
                for part in range(parts)
            )
            for which, x in enumerate((re, re + im, im - re) if j < MAIN else (re, im)):
                for g in range(0, height, 8):
                    size = min(8, height - g)
                    row = (first + g) * HAT_ROWS + kernel_row(which, j)
                    hat[pl.ds(row, size, stride=HAT_ROWS), :] = x[g : g + size]

    whole = count // 16

    @pl.loop(0, whole)
    def _(i):
        move(pl.multiple_of(i * 16, 16), 16)

    if count % 16:
        move(whole * 16, count % 16)


def forward_kernel(send_list, density, from_near, relayed, *refs):
    *from_far, from_first, from_second, table, main, rows = refs
    comp_count, box_count, surf = density.shape
    peers, cap = send_list.shape
    rim = from_first.shape[1]
    row_count = rows.shape[0]
    slots = row_count // comp_count
    pitch = source_rows(comp_count)
    f32, bf16 = jnp.float32, jnp.bfloat16

    member = lax.axis_index("dev")
    parity = lax.rem(lax.axis_index("group"), 2)
    rows[...] = jnp.zeros_like(rows)
    pieces = {1: from_near.at[0], 2: relayed.at[0], 3: relayed.at[1]}
    pieces.update(zip(range(4, peers), from_far))
    for c in range(comp_count):
        base = c * slots
        rows[base : base + box_count, :surf] = density[c]
        base += box_count
        for e in range(cap):
            rows[pl.ds(base + member * cap + e, 1), :surf] = density[c, pl.ds(send_list[member, e], 1), :]
            for k, piece in pieces.items():
                rows[pl.ds(base + (member ^ k) * cap + e, 1), :surf] = piece[c, e : e + 1]
        base += peers * cap
        for e in range(rim):
            rows[pl.ds(base + (1 - parity) * rim + e, 1), :surf] = from_first[c, e : e + 1]
            rows[pl.ds(base + parity * rim + e, 1), :surf] = from_second[c, e : e + 1]

    value = rows[...]
    high = value.astype(bf16)
    low = (value - high.astype(f32)).astype(bf16)
    both = jnp.concatenate([high, low], axis=0)

    def spectrum(first):
        columns = slice(first, first + CHUNK)
        x = jnp.dot(both, table[:POINTS_PAD, columns], preferred_element_type=f32)
        x = x[:row_count] + x[row_count:]
        x = x + jnp.dot(high, table[POINTS_PAD:, columns], preferred_element_type=f32)
        return x.astype(bf16).astype(f32)

    for n in range(FREQ // CHUNK):
        re, im = spectrum(n * CHUNK), spectrum(FREQ + n * CHUNK)
        for m in range(CHUNK // LANES):
            j = n * (CHUNK // LANES) + m
            for g in range(row_count // 8):
                at = (slice(g * 8, (g + 1) * 8), slice(m * LANES, (m + 1) * LANES))
                c, s = divmod(g * 8, slots)
                pieces = [re[at], im[at]]
                if j < MAIN:
                    pieces.append(pieces[0] + pieces[1])
                for part, piece in enumerate(pieces):
                    row = source_row(comp_count, part * comp_count + c, j)
                    main[pl.ds(s * pitch + row, 8, stride=pitch), :] = piece


def interact_kernel(comp_count, source, offset, hat, main, total, total_tail):
    box_count, list_count = source.shape
    pitch = source_rows(comp_count)
    f32 = jnp.float32
    plus = lax.broadcasted_iota(jnp.int32, (8, LANES), 0) < comp_count
    halves = MAIN // 8

    @pl.loop(0, box_count)
    def _(t):
        def rows_of(first):
            return tuple(
                (source[t, first + u] * pitch, offset[t, first + u] * HAT_ROWS) for u in range(UNROLL)
            )

        def pair(s, o, accs):
            k = [[hat[pl.ds(o + kernel_row(r, 8 * h), 8), :] for h in range(halves)] for r in range(3)]
            accs = list(accs)
            at = 0
            for c in range(comp_count):
                for h in range(halves):
                    s_re, s_im, s_sum = (
                        main[pl.ds(s + source_row(comp_count, r * comp_count + c, 8 * h), 8), :] for r in range(3)
                    )
                    accs[at] = accs[at] + k[0][h] * s_sum
                    accs[at + 1] = accs[at + 1] + k[1][h] * s_im
                    accs[at + 2] = accs[at + 2] + k[2][h] * s_re
                    at += 3
            k_tail = hat[pl.ds(o + kernel_row(0, MAIN), 8), :]
            for j in range(TAIL):
                x = main[pl.ds(s + source_row(comp_count, 0, MAIN + j), 8), :]
                for r in range(2):
                    row = 2 * j + r
                    accs[at + r] = accs[at + r] + jnp.broadcast_to(k_tail[row : row + 1], (8, LANES)) * x
                at += 2
            return tuple(accs)

        count = 3 * comp_count * halves + 2 * TAIL
        zero = jnp.zeros((8, LANES), f32)

        def block(i, carry):
            accs, here = carry
            ahead = rows_of(lax.rem((i + 1) * UNROLL, list_count))
            for s, o in here:
                accs = pair(s, o, accs)
            return accs, ahead

        accs, _ = lax.fori_loop(0, list_count // UNROLL, block, ((zero,) * count, rows_of(0)))
        at = 0
        for c in range(comp_count):
            for h in range(halves):
                for part, value in enumerate((accs[at] - accs[at + 1], accs[at] + accs[at + 2])):
                    row = (part * comp_count + c) * box_count + t
                    total[pl.ds(row * PITCH + 8 * h, 8), :] = value
                at += 3
        for j in range(TAIL):
            own, cross = accs[at], accs[at + 1]
            up = jnp.concatenate([cross[comp_count:], cross[:comp_count]], axis=0)
            down = jnp.concatenate([cross[-comp_count:], cross[:-comp_count]], axis=0)
            total_tail[j, pl.ds(t * TAIL_PITCH, 8), :] = jnp.where(plus, own - up, own + down)
            at += 2


def inverse_kernel(total, total_tail, table, factor, out):
    comp_count, box_count, surf = out.shape
    f32, bf16 = jnp.float32, jnp.bfloat16
    groups = box_count // 8
    count = comp_count * box_count
    nt = (((1,), (1,)), ((), ()))
    result = jnp.zeros((2 * POINTS_PAD, 2 * count), f32)
    for n in range(2 * FREQ // PIECE):
        lanes = []
        for m in range(PIECE // LANES):
            part, j = divmod(n * (PIECE // LANES) + m, TILES)
            pieces = []
            for c in range(comp_count):
                for g in range(groups):
                    if j < MAIN:
                        row = (part * comp_count + c) * box_count + g * 8
                        pieces.append(total[pl.ds(row * PITCH + j, 8, stride=PITCH), :])
                    else:
                        row = g * 8 * TAIL_PITCH + part * comp_count + c
                        pieces.append(total_tail[j - MAIN, pl.ds(row, 8, stride=TAIL_PITCH), :])
            lanes.append(jnp.concatenate(pieces, axis=0))
        columns = slice(n * PIECE, (n + 1) * PIECE)
        x = jnp.concatenate(lanes, axis=1) * factor[:, columns]
        high = x.astype(bf16)
        low = (x - high.astype(f32)).astype(bf16)
        both = jnp.concatenate([high, low], axis=0)
        result += lax.dot_general(table[:, columns], both, nt, preferred_element_type=f32)
    result = result[:POINTS_PAD, :count] + result[:POINTS_PAD, count:] + result[POINTS_PAD:, :count]
    result = result.T
    for c in range(comp_count):
        out[c] = result[c * box_count : (c + 1) * box_count, :surf]


def translate_kernel(send_list, source, offset, density, from_near, relayed, *refs):
    *pieces, table, factor, hat, out, main, rows, total, total_tail = refs
    forward_kernel(send_list, density, from_near, relayed, *pieces, table, main, rows)
    interact_kernel(density.shape[0], source, offset, hat, main, total, total_tail)
    inverse_kernel(total, total_tail, table, factor, out)


def on_device(density, kernel_hat, send_list, halo_list, inter_src, inter_off):
    table, factor = transform_tables()
    box_count, comp_count, surf = density.shape
    _, peers, cap = send_list.shape
    rim = halo_list.shape[2]
    f32 = jnp.float32
    vmem = pl.BlockSpec(memory_space=pltpu.VMEM)
    smem = pl.BlockSpec(memory_space=pltpu.SMEM)
    density = density.transpose(1, 0, 2)

    boxes = jax.ShapeDtypeStruct((comp_count, cap, surf), f32)
    side = jax.ShapeDtypeStruct((comp_count, rim, surf), f32)
    to_near, to_two, *to_far, to_first, to_second = pl.pallas_call(
        pack_kernel,
        out_shape=(jax.ShapeDtypeStruct((2, *boxes.shape), f32),) + (boxes,) * (peers - 3) + (side,) * 2,
        in_specs=[vmem, smem, smem],
        out_specs=(vmem,) * peers,
        name="pack",
    )(density, send_list[0], halo_list[0])

    def swap(x, k):
        return lax.ppermute(x, "dev", [(i, i ^ k) for i in range(peers)])

    def swap_groups(x, start):
        pairs = [(i, i + 1) for i in range(start, lax.axis_size("group") - 1, 2)]
        return lax.ppermute(x, "group", pairs + [(j, i) for i, j in pairs])

    from_near = swap(to_near, 1)
    from_far = [swap(x, k) for x, k in zip(to_far, range(4, peers))]
    from_first = swap_groups(to_first, 0)
    from_second = swap_groups(to_second, 1)
    by_part, near = lax.optimization_barrier((kernel_hat.transpose(1, 0, 2), from_near))
    relayed = swap(jnp.stack([to_two, near[1]]), 2)

    offsets = kernel_hat.shape[0]
    hat = pl.pallas_call(
        prepare_kernel,
        out_shape=jax.ShapeDtypeStruct((offsets * HAT_ROWS + 8, LANES), f32),
        in_specs=[vmem],
        out_specs=vmem,
        compiler_params=pltpu.CompilerParams(vmem_limit_bytes=16 * 1024 * 1024),
        cost_estimate=pl.CostEstimate(flops=kernel_hat.size, bytes_accessed=6 * kernel_hat.size, transcendentals=0),
        name="prepare",
    )(by_part)

    slots = box_count + peers * cap + 2 * rim
    row_count = comp_count * slots
    arrays = (
        send_list[0], inter_src, inter_off, density, from_near, relayed, *from_far, from_first, from_second,
        jnp.asarray(table), jnp.asarray(factor), hat,
    )
    potential = pl.pallas_call(
        translate_kernel,
        out_shape=jax.ShapeDtypeStruct((comp_count, box_count, surf), f32),
        in_specs=[smem] * 3 + [vmem] * (len(arrays) - 3),
        out_specs=vmem,
        scratch_shapes=[
            pltpu.VMEM((slots * source_rows(comp_count) + 8, LANES), f32),
            pltpu.VMEM((row_count, POINTS_PAD), f32),
            pltpu.VMEM((2 * comp_count * box_count * PITCH, LANES), f32),
            pltpu.VMEM((TAIL, (box_count + 2) * TAIL_PITCH, LANES), f32),
        ],
        compiler_params=pltpu.CompilerParams(vmem_limit_bytes=24 * 1024 * 1024),
        name="translate",
    )(*arrays)
    return potential.transpose(1, 0, 2)


def solution(mesh):
    in_specs = (
        P(("group", "dev"), None, None),
        P(),
        P(("group", "dev"), None, None),
        P(("group", "dev"), None, None),
        P(("group", "dev"), None),
        P(("group", "dev"), None),
    )
    out_specs = P(("group", "dev"), None, None)
    return jax.shard_map(
        on_device, mesh=mesh, in_specs=in_specs, out_specs=out_specs, check_vma=False
    )
```

```python
import functools
import math

import jax
import jax.numpy as jnp
import ml_dtypes
import numpy as np
from jax import lax
from jax.experimental import pallas as pl
from jax.experimental.pallas import tpu as pltpu
from jax.sharding import PartitionSpec as P

ORDER = 6
GRID = 16
LANES = 128
HALF = GRID // 2 + 1
FREQ = GRID * GRID * HALF
TILES = FREQ // LANES
MAIN = 16
TAIL = TILES - MAIN
PITCH = MAIN + 1
TAIL_PITCH = 7
HAT_ROWS = 3 * MAIN + 2 * TAIL + 1
POINTS_PAD = 160
CHUNK = 256
PIECE = 512
UNROLL = 8


def surface_points(edge_count):
    points = [
        (i, j, k)
        for i in range(edge_count)
        for j in range(edge_count)
        for k in range(edge_count)
        if min(i, j, k) == 0 or max(i, j, k) == edge_count - 1
    ]
    return np.array(points, dtype=np.int64)


@functools.lru_cache(maxsize=None)
def transform_tables():
    points = surface_points(ORDER)
    kx, ky, kz = (a.reshape(-1) for a in np.meshgrid(np.arange(GRID), np.arange(GRID), np.arange(HALF), indexing="ij"))
    phase = (points[:, :1] * kx + points[:, 1:2] * ky + points[:, 2:] * kz) % GRID
    angle = phase * (2.0 * math.pi / GRID)
    table = np.zeros((POINTS_PAD, 2 * FREQ), np.float64)
    table[: len(points), :FREQ] = np.cos(angle)
    table[: len(points), FREQ:] = -np.sin(angle)
    table = np.where(np.abs(table) < 1e-9, 0.0, table)
    high = table.astype(ml_dtypes.bfloat16)
    low = (table - high.astype(np.float64)).astype(ml_dtypes.bfloat16)
    edge_plane = (kz == 0) | (kz == GRID // 2)
    factor = np.where(edge_plane, 1.0, 2.0) / GRID**3 * np.where((kx + ky + kz) % 2 == 0, 1.0, -1.0)
    factor = np.concatenate([factor, factor]).astype(np.float32)[None, :]
    return np.concatenate([high, low], axis=0), factor


def source_rows(comp_count):
    return (3 * comp_count * MAIN + TAIL * 8) | 1


def source_row(comp_count, which, tile):
    if tile < MAIN:
        return which * MAIN + tile
    return 3 * comp_count * MAIN + (tile - MAIN) * 8 + which


def kernel_row(which, tile):
    return which * MAIN + tile if tile < MAIN else 3 * MAIN + (tile - MAIN) * 2 + which


def pack_kernel(density, send_list, halo_list, *outs):
    peers, cap = send_list.shape
    rim = halo_list.shape[1]
    member = lax.axis_index("dev")
    parity = lax.rem(lax.axis_index("group"), 2)
    to_near, *to_far, to_first, to_second = outs
    for c in range(density.shape[0]):
        for e in range(cap):
            for part, k in enumerate((1, 3)):
                to_near[part, c, e : e + 1, :] = density[c, pl.ds(send_list[member ^ k, e], 1), :]
            for k, out in zip((2, *range(4, peers)), to_far):
                out[c, e : e + 1, :] = density[c, pl.ds(send_list[member ^ k, e], 1), :]
        for e in range(rim):
            to_first[c, e : e + 1, :] = density[c, pl.ds(halo_list[1 - parity, e], 1), :]
            to_second[c, e : e + 1, :] = density[c, pl.ds(halo_list[parity, e], 1), :]


def prepare_kernel(kernel_hat, hat):
    parts, count, _ = kernel_hat.shape

    def move(first, height):
        for j in range(TILES):
            re, im = (
                kernel_hat[part, pl.ds(first, height), j * LANES : (j + 1) * LANES].astype(jnp.float32)
                for part in range(parts)
            )
            for which, x in enumerate((re, re + im, im - re) if j < MAIN else (re, im)):
                for g in range(0, height, 8):
                    size = min(8, height - g)
                    row = (first + g) * HAT_ROWS + kernel_row(which, j)
                    hat[pl.ds(row, size, stride=HAT_ROWS), :] = x[g : g + size]

    whole = count // 16

    @pl.loop(0, whole)
    def _(i):
        move(pl.multiple_of(i * 16, 16), 16)

    if count % 16:
        move(whole * 16, count % 16)


def forward_kernel(send_list, density, from_near, relayed, *refs):
    *from_far, from_first, from_second, table, main, rows = refs
    comp_count, box_count, surf = density.shape
    peers, cap = send_list.shape
    rim = from_first.shape[1]
    row_count = rows.shape[0]
    slots = row_count // comp_count
    pitch = source_rows(comp_count)
    f32, bf16 = jnp.float32, jnp.bfloat16

    member = lax.axis_index("dev")
    parity = lax.rem(lax.axis_index("group"), 2)
    rows[...] = jnp.zeros_like(rows)
    pieces = {1: from_near.at[0], 2: relayed.at[0], 3: relayed.at[1]}
    pieces.update(zip(range(4, peers), from_far))
    for c in range(comp_count):
        base = c * slots
        rows[base : base + box_count, :surf] = density[c]
        base += box_count
        for e in range(cap):
            rows[pl.ds(base + member * cap + e, 1), :surf] = density[c, pl.ds(send_list[member, e], 1), :]
            for k, piece in pieces.items():
                rows[pl.ds(base + (member ^ k) * cap + e, 1), :surf] = piece[c, e : e + 1]
        base += peers * cap
        for e in range(rim):
            rows[pl.ds(base + (1 - parity) * rim + e, 1), :surf] = from_first[c, e : e + 1]
            rows[pl.ds(base + parity * rim + e, 1), :surf] = from_second[c, e : e + 1]

    value = rows[...]
    high = value.astype(bf16)
    low = (value - high.astype(f32)).astype(bf16)
    both = jnp.concatenate([high, low], axis=0)

    def spectrum(first):
        columns = slice(first, first + CHUNK)
        x = jnp.dot(both, table[:POINTS_PAD, columns], preferred_element_type=f32)
        x = x[:row_count] + x[row_count:]
        x = x + jnp.dot(high, table[POINTS_PAD:, columns], preferred_element_type=f32)
        return x.astype(bf16).astype(f32)

    for n in range(FREQ // CHUNK):
        re, im = spectrum(n * CHUNK), spectrum(FREQ + n * CHUNK)
        for m in range(CHUNK // LANES):
            j = n * (CHUNK // LANES) + m
            for g in range(row_count // 8):
                at = (slice(g * 8, (g + 1) * 8), slice(m * LANES, (m + 1) * LANES))
                c, s = divmod(g * 8, slots)
                pieces = [re[at], im[at]]
                if j < MAIN:
                    pieces.append(pieces[0] + pieces[1])
                for part, piece in enumerate(pieces):
                    row = source_row(comp_count, part * comp_count + c, j)
                    main[pl.ds(s * pitch + row, 8, stride=pitch), :] = piece


def interact_kernel(comp_count, source, offset, hat, main, total, total_tail):
    box_count, list_count = source.shape
    pitch = source_rows(comp_count)
    f32 = jnp.float32
    plus = lax.broadcasted_iota(jnp.int32, (8, LANES), 0) < comp_count
    halves = MAIN // 8

    @pl.loop(0, box_count)
    def _(t):
        def rows_of(first):
            return tuple(
                (source[t, first + u] * pitch, offset[t, first + u] * HAT_ROWS) for u in range(UNROLL)
            )

        def pair(s, o, accs):
            k = [[hat[pl.ds(o + kernel_row(r, 8 * h), 8), :] for h in range(halves)] for r in range(3)]
            accs = list(accs)
            at = 0
            for c in range(comp_count):
                for h in range(halves):
                    s_re, s_im, s_sum = (
                        main[pl.ds(s + source_row(comp_count, r * comp_count + c, 8 * h), 8), :] for r in range(3)
                    )
                    accs[at] = accs[at] + k[0][h] * s_sum
                    accs[at + 1] = accs[at + 1] + k[1][h] * s_im
                    accs[at + 2] = accs[at + 2] + k[2][h] * s_re
                    at += 3
            k_tail = hat[pl.ds(o + kernel_row(0, MAIN), 8), :]
            for j in range(TAIL):
                x = main[pl.ds(s + source_row(comp_count, 0, MAIN + j), 8), :]
                for r in range(2):
                    row = 2 * j + r
                    accs[at + r] = accs[at + r] + jnp.broadcast_to(k_tail[row : row + 1], (8, LANES)) * x
                at += 2
            return tuple(accs)

        count = 3 * comp_count * halves + 2 * TAIL
        zero = jnp.zeros((8, LANES), f32)

        def block(i, carry):
            accs, here = carry
            ahead = rows_of(lax.rem((i + 1) * UNROLL, list_count))
            for s, o in here:
                accs = pair(s, o, accs)
            return accs, ahead

        accs, _ = lax.fori_loop(0, list_count // UNROLL, block, ((zero,) * count, rows_of(0)))
        at = 0
        for c in range(comp_count):
            for h in range(halves):
                for part, value in enumerate((accs[at] - accs[at + 1], accs[at] + accs[at + 2])):
                    row = (part * comp_count + c) * box_count + t
                    total[pl.ds(row * PITCH + 8 * h, 8), :] = value
                at += 3
        for j in range(TAIL):
            own, cross = accs[at], accs[at + 1]
            up = jnp.concatenate([cross[comp_count:], cross[:comp_count]], axis=0)
            down = jnp.concatenate([cross[-comp_count:], cross[:-comp_count]], axis=0)
            total_tail[j, pl.ds(t * TAIL_PITCH, 8), :] = jnp.where(plus, own - up, own + down)
            at += 2


def inverse_kernel(total, total_tail, table, factor, out):
    comp_count, box_count, surf = out.shape
    f32, bf16 = jnp.float32, jnp.bfloat16
    groups = box_count // 8
    count = comp_count * box_count
    nt = (((1,), (1,)), ((), ()))
    result = jnp.zeros((2 * POINTS_PAD, 2 * count), f32)
    for n in range(2 * FREQ // PIECE):
        lanes = []
        for m in range(PIECE // LANES):
            part, j = divmod(n * (PIECE // LANES) + m, TILES)
            pieces = []
            for c in range(comp_count):
                for g in range(groups):
                    if j < MAIN:
                        row = (part * comp_count + c) * box_count + g * 8
                        pieces.append(total[pl.ds(row * PITCH + j, 8, stride=PITCH), :])
                    else:
                        row = g * 8 * TAIL_PITCH + part * comp_count + c
                        pieces.append(total_tail[j - MAIN, pl.ds(row, 8, stride=TAIL_PITCH), :])
            lanes.append(jnp.concatenate(pieces, axis=0))
        columns = slice(n * PIECE, (n + 1) * PIECE)
        x = jnp.concatenate(lanes, axis=1) * factor[:, columns]
        high = x.astype(bf16)
        low = (x - high.astype(f32)).astype(bf16)
        both = jnp.concatenate([high, low], axis=0)
        result += lax.dot_general(table[:, columns], both, nt, preferred_element_type=f32)
    result = result[:POINTS_PAD, :count] + result[:POINTS_PAD, count:] + result[POINTS_PAD:, :count]
    result = result.T
    for c in range(comp_count):
        out[c] = result[c * box_count : (c + 1) * box_count, :surf]


def translate_kernel(send_list, source, offset, density, from_near, relayed, *refs):
    *pieces, table, factor, hat, out, main, rows, total, total_tail = refs
    forward_kernel(send_list, density, from_near, relayed, *pieces, table, main, rows)
    interact_kernel(density.shape[0], source, offset, hat, main, total, total_tail)
    inverse_kernel(total, total_tail, table, factor, out)


def on_device(density, kernel_hat, send_list, halo_list, inter_src, inter_off):
    table, factor = transform_tables()
    box_count, comp_count, surf = density.shape
    _, peers, cap = send_list.shape
    rim = halo_list.shape[2]
    f32 = jnp.float32
    vmem = pl.BlockSpec(memory_space=pltpu.VMEM)
    smem = pl.BlockSpec(memory_space=pltpu.SMEM)
    density = density.transpose(1, 0, 2)

    boxes = jax.ShapeDtypeStruct((comp_count, cap, surf), f32)
    side = jax.ShapeDtypeStruct((comp_count, rim, surf), f32)
    to_near, to_two, *to_far, to_first, to_second = pl.pallas_call(
        pack_kernel,
        out_shape=(jax.ShapeDtypeStruct((2, *boxes.shape), f32),) + (boxes,) * (peers - 3) + (side,) * 2,
        in_specs=[vmem, smem, smem],
        out_specs=(vmem,) * peers,
        name="pack",
    )(density, send_list[0], halo_list[0])

    def swap(x, k):
        return lax.ppermute(x, "dev", [(i, i ^ k) for i in range(peers)])

    def swap_groups(x, start):
        pairs = [(i, i + 1) for i in range(start, lax.axis_size("group") - 1, 2)]
        return lax.ppermute(x, "group", pairs + [(j, i) for i, j in pairs])

    from_near = swap(to_near, 1)
    from_far = [swap(x, k) for x, k in zip(to_far, range(4, peers))]
    from_first = swap_groups(to_first, 0)
    from_second = swap_groups(to_second, 1)
    kernels, near = lax.optimization_barrier((kernel_hat, from_near))
    relayed = swap(jnp.stack([to_two, near[1]]), 2)

    offsets = kernel_hat.shape[0]
    hat = pl.pallas_call(
        prepare_kernel,
        out_shape=jax.ShapeDtypeStruct((offsets * HAT_ROWS + 8, LANES), f32),
        in_specs=[vmem],
        out_specs=vmem,
        compiler_params=pltpu.CompilerParams(vmem_limit_bytes=16 * 1024 * 1024),
        cost_estimate=pl.CostEstimate(flops=kernel_hat.size, bytes_accessed=6 * kernel_hat.size, transcendentals=0),
        name="prepare",
    )(kernels.transpose(1, 0, 2))

    slots = box_count + peers * cap + 2 * rim
    row_count = comp_count * slots
    arrays = (
        send_list[0], inter_src, inter_off, density, from_near, relayed, *from_far, from_first, from_second,
        jnp.asarray(table), jnp.asarray(factor), hat,
    )
    potential = pl.pallas_call(
        translate_kernel,
        out_shape=jax.ShapeDtypeStruct((comp_count, box_count, surf), f32),
        in_specs=[smem] * 3 + [vmem] * (len(arrays) - 3),
        out_specs=vmem,
        scratch_shapes=[
            pltpu.VMEM((slots * source_rows(comp_count) + 8, LANES), f32),
            pltpu.VMEM((row_count, POINTS_PAD), f32),
            pltpu.VMEM((2 * comp_count * box_count * PITCH, LANES), f32),
            pltpu.VMEM((TAIL, (box_count + 2) * TAIL_PITCH, LANES), f32),
        ],
        compiler_params=pltpu.CompilerParams(vmem_limit_bytes=24 * 1024 * 1024),
        name="translate",
    )(*arrays)
    return potential.transpose(1, 0, 2)


def solution(mesh):
    in_specs = (
        P(("group", "dev"), None, None),
        P(),
        P(("group", "dev"), None, None),
        P(("group", "dev"), None, None),
        P(("group", "dev"), None),
        P(("group", "dev"), None),
    )
    out_specs = P(("group", "dev"), None, None)
    return jax.shard_map(
        on_device, mesh=mesh, in_specs=in_specs, out_specs=out_specs, check_vma=False
    )
```

```python
import functools
import math

import jax
import jax.numpy as jnp
import ml_dtypes
import numpy as np
from jax import lax
from jax.experimental import pallas as pl
from jax.experimental.pallas import tpu as pltpu
from jax.sharding import PartitionSpec as P

ORDER = 6
GRID = 16
LANES = 128
HALF = GRID // 2 + 1
FREQ = GRID * GRID * HALF
TILES = FREQ // LANES
MAIN = 16
TAIL = TILES - MAIN
PITCH = MAIN + 1
TAIL_PITCH = 7
HAT_ROWS = 3 * MAIN + 2 * TAIL + 1
POINTS_PAD = 160
CHUNK = 256
PIECE = 512
UNROLL = 8


def surface_points(edge_count):
    points = [
        (i, j, k)
        for i in range(edge_count)
        for j in range(edge_count)
        for k in range(edge_count)
        if min(i, j, k) == 0 or max(i, j, k) == edge_count - 1
    ]
    return np.array(points, dtype=np.int64)


@functools.lru_cache(maxsize=None)
def transform_tables():
    points = surface_points(ORDER)
    kx, ky, kz = (a.reshape(-1) for a in np.meshgrid(np.arange(GRID), np.arange(GRID), np.arange(HALF), indexing="ij"))
    phase = (points[:, :1] * kx + points[:, 1:2] * ky + points[:, 2:] * kz) % GRID
    angle = phase * (2.0 * math.pi / GRID)
    table = np.zeros((POINTS_PAD, 2 * FREQ), np.float64)
    table[: len(points), :FREQ] = np.cos(angle)
    table[: len(points), FREQ:] = -np.sin(angle)
    table = np.where(np.abs(table) < 1e-9, 0.0, table)
    high = table.astype(ml_dtypes.bfloat16)
    low = (table - high.astype(np.float64)).astype(ml_dtypes.bfloat16)
    edge_plane = (kz == 0) | (kz == GRID // 2)
    factor = np.where(edge_plane, 1.0, 2.0) / GRID**3 * np.where((kx + ky + kz) % 2 == 0, 1.0, -1.0)
    factor = np.concatenate([factor, factor]).astype(np.float32)[None, :]
    return np.concatenate([high, low], axis=0), factor


def source_rows(comp_count):
    return (3 * comp_count * MAIN + TAIL * 8) | 1


def source_row(comp_count, which, tile):
    if tile < MAIN:
        return which * MAIN + tile
    return 3 * comp_count * MAIN + (tile - MAIN) * 8 + which


def kernel_row(which, tile):
    return which * MAIN + tile if tile < MAIN else 3 * MAIN + (tile - MAIN) * 2 + which


def pack_kernel(density, send_list, halo_list, *outs):
    peers, cap = send_list.shape
    rim = halo_list.shape[1]
    member = lax.axis_index("dev")
    parity = lax.rem(lax.axis_index("group"), 2)
    to_near, *to_far, to_first, to_second = outs
    for c in range(density.shape[0]):
        for e in range(cap):
            for part, k in enumerate((1, 3)):
                to_near[part, c, e : e + 1, :] = density[c, pl.ds(send_list[member ^ k, e], 1), :]
            for k, out in zip((2, *range(4, peers)), to_far):
                out[c, e : e + 1, :] = density[c, pl.ds(send_list[member ^ k, e], 1), :]
        for e in range(rim):
            to_first[c, e : e + 1, :] = density[c, pl.ds(halo_list[1 - parity, e], 1), :]
            to_second[c, e : e + 1, :] = density[c, pl.ds(halo_list[parity, e], 1), :]


def prepare_kernel(kernel_hat, hat):
    parts, count, _ = kernel_hat.shape

    def move(first, height):
        for j in range(TILES):
            re, im = (
                kernel_hat[part, pl.ds(first, height), j * LANES : (j + 1) * LANES].astype(jnp.float32)
                for part in range(parts)
            )
            for which, x in enumerate((re, re + im, im - re) if j < MAIN else (re, im)):
                for g in range(0, height, 8):
                    size = min(8, height - g)
                    row = (first + g) * HAT_ROWS + kernel_row(which, j)
                    hat[pl.ds(row, size, stride=HAT_ROWS), :] = x[g : g + size]

    whole = count // 16

    @pl.loop(0, whole)
    def _(i):
        move(pl.multiple_of(i * 16, 16), 16)

    if count % 16:
        move(whole * 16, count % 16)


def forward_kernel(send_list, density, from_near, relayed, *refs):
    *from_far, from_first, from_second, table, main, rows = refs
    comp_count, box_count, surf = density.shape
    peers, cap = send_list.shape
    rim = from_first.shape[1]
    row_count = rows.shape[0]
    slots = row_count // comp_count
    pitch = source_rows(comp_count)
    f32, bf16 = jnp.float32, jnp.bfloat16

    member = lax.axis_index("dev")
    parity = lax.rem(lax.axis_index("group"), 2)
    rows[...] = jnp.zeros_like(rows)
    pieces = {1: from_near.at[0], 2: relayed.at[0], 3: relayed.at[1]}
    pieces.update(zip(range(4, peers), from_far))
    for c in range(comp_count):
        base = c * slots
        rows[base : base + box_count, :surf] = density[c]
        base += box_count
        for e in range(cap):
            rows[pl.ds(base + member * cap + e, 1), :surf] = density[c, pl.ds(send_list[member, e], 1), :]
            for k, piece in pieces.items():
                rows[pl.ds(base + (member ^ k) * cap + e, 1), :surf] = piece[c, e : e + 1]
        base += peers * cap
        for e in range(rim):
            rows[pl.ds(base + (1 - parity) * rim + e, 1), :surf] = from_first[c, e : e + 1]
            rows[pl.ds(base + parity * rim + e, 1), :surf] = from_second[c, e : e + 1]

    value = rows[...]
    high = value.astype(bf16)
    low = (value - high.astype(f32)).astype(bf16)
    both = jnp.concatenate([high, low], axis=0)

    def spectrum(first):
        columns = slice(first, first + CHUNK)
        x = jnp.dot(both, table[:POINTS_PAD, columns], preferred_element_type=f32)
        x = x[:row_count] + x[row_count:]
        x = x + jnp.dot(high, table[POINTS_PAD:, columns], preferred_element_type=f32)
        return x.astype(bf16).astype(f32)

    for n in range(FREQ // CHUNK):
        re, im = spectrum(n * CHUNK), spectrum(FREQ + n * CHUNK)
        for m in range(CHUNK // LANES):
            j = n * (CHUNK // LANES) + m
            for g in range(row_count // 8):
                at = (slice(g * 8, (g + 1) * 8), slice(m * LANES, (m + 1) * LANES))
                c, s = divmod(g * 8, slots)
                pieces = [re[at], im[at]]
                if j < MAIN:
                    pieces.append(pieces[0] + pieces[1])
                for part, piece in enumerate(pieces):
                    row = source_row(comp_count, part * comp_count + c, j)
                    main[pl.ds(s * pitch + row, 8, stride=pitch), :] = piece


def interact_kernel(comp_count, source, offset, hat, main, total, total_tail):
    box_count, list_count = source.shape
    pitch = source_rows(comp_count)
    f32 = jnp.float32
    plus = lax.broadcasted_iota(jnp.int32, (8, LANES), 0) < comp_count
    halves = MAIN // 8

    @pl.loop(0, box_count)
    def _(t):
        def rows_of(first):
            return tuple(
                (source[t, first + u] * pitch, offset[t, first + u] * HAT_ROWS) for u in range(UNROLL)
            )

        def pair(s, o, accs):
            k = [[hat[pl.ds(o + kernel_row(r, 8 * h), 8), :] for h in range(halves)] for r in range(3)]
            accs = list(accs)
            at = 0
            for c in range(comp_count):
                for h in range(halves):
                    s_re, s_im, s_sum = (
                        main[pl.ds(s + source_row(comp_count, r * comp_count + c, 8 * h), 8), :] for r in range(3)
                    )
                    accs[at] = accs[at] + k[0][h] * s_sum
                    accs[at + 1] = accs[at + 1] + k[1][h] * s_im
                    accs[at + 2] = accs[at + 2] + k[2][h] * s_re
                    at += 3
            k_tail = hat[pl.ds(o + kernel_row(0, MAIN), 8), :]
            for j in range(TAIL):
                x = main[pl.ds(s + source_row(comp_count, 0, MAIN + j), 8), :]
                for r in range(2):
                    row = 2 * j + r
                    accs[at + r] = accs[at + r] + jnp.broadcast_to(k_tail[row : row + 1], (8, LANES)) * x
                at += 2
            return tuple(accs)

        count = 3 * comp_count * halves + 2 * TAIL
        zero = jnp.zeros((8, LANES), f32)

        def block(i, carry):
            accs, here = carry
            ahead = rows_of(lax.rem((i + 1) * UNROLL, list_count))
            for s, o in here:
                accs = pair(s, o, accs)
            return accs, ahead

        accs, _ = lax.fori_loop(0, list_count // UNROLL, block, ((zero,) * count, rows_of(0)))
        at = 0
        for c in range(comp_count):
            for h in range(halves):
                for part, value in enumerate((accs[at] - accs[at + 1], accs[at] + accs[at + 2])):
                    row = (part * comp_count + c) * box_count + t
                    total[pl.ds(row * PITCH + 8 * h, 8), :] = value
                at += 3
        for j in range(TAIL):
            own, cross = accs[at], accs[at + 1]
            up = jnp.concatenate([cross[comp_count:], cross[:comp_count]], axis=0)
            down = jnp.concatenate([cross[-comp_count:], cross[:-comp_count]], axis=0)
            total_tail[j, pl.ds(t * TAIL_PITCH, 8), :] = jnp.where(plus, own - up, own + down)
            at += 2


def inverse_kernel(total, total_tail, table, factor, out):
    comp_count, box_count, surf = out.shape
    f32, bf16 = jnp.float32, jnp.bfloat16
    groups = box_count // 8
    count = comp_count * box_count
    nt = (((1,), (1,)), ((), ()))
    result = jnp.zeros((2 * POINTS_PAD, 2 * count), f32)
    for n in range(2 * FREQ // PIECE):
        lanes = []
        for m in range(PIECE // LANES):
            part, j = divmod(n * (PIECE // LANES) + m, TILES)
            pieces = []
            for c in range(comp_count):
                for g in range(groups):
                    if j < MAIN:
                        row = (part * comp_count + c) * box_count + g * 8
                        pieces.append(total[pl.ds(row * PITCH + j, 8, stride=PITCH), :])
                    else:
                        row = g * 8 * TAIL_PITCH + part * comp_count + c
                        pieces.append(total_tail[j - MAIN, pl.ds(row, 8, stride=TAIL_PITCH), :])
            lanes.append(jnp.concatenate(pieces, axis=0))
        columns = slice(n * PIECE, (n + 1) * PIECE)
        x = jnp.concatenate(lanes, axis=1) * factor[:, columns]
        high = x.astype(bf16)
        low = (x - high.astype(f32)).astype(bf16)
        both = jnp.concatenate([high, low], axis=0)
        result += lax.dot_general(table[:, columns], both, nt, preferred_element_type=f32)
    result = result[:POINTS_PAD, :count] + result[:POINTS_PAD, count:] + result[POINTS_PAD:, :count]
    result = result.T
    for c in range(comp_count):
        out[c] = result[c * box_count : (c + 1) * box_count, :surf]


def translate_kernel(send_list, source, offset, density, from_near, relayed, *refs):
    *pieces, table, factor, hat, out, main, rows, total, total_tail = refs
    forward_kernel(send_list, density, from_near, relayed, *pieces, table, main, rows)
    interact_kernel(density.shape[0], source, offset, hat, main, total, total_tail)
    inverse_kernel(total, total_tail, table, factor, out)


def on_device(density, kernel_hat, send_list, halo_list, inter_src, inter_off):
    table, factor = transform_tables()
    box_count, comp_count, surf = density.shape
    _, peers, cap = send_list.shape
    rim = halo_list.shape[2]
    f32 = jnp.float32
    vmem = pl.BlockSpec(memory_space=pltpu.VMEM)
    smem = pl.BlockSpec(memory_space=pltpu.SMEM)
    density = density.transpose(1, 0, 2)

    boxes = jax.ShapeDtypeStruct((comp_count, cap, surf), f32)
    side = jax.ShapeDtypeStruct((comp_count, rim, surf), f32)
    to_near, to_two, *to_far, to_first, to_second = pl.pallas_call(
        pack_kernel,
        out_shape=(jax.ShapeDtypeStruct((2, *boxes.shape), f32),) + (boxes,) * (peers - 3) + (side,) * 2,
        in_specs=[vmem, smem, smem],
        out_specs=(vmem,) * peers,
        name="pack",
    )(density, send_list[0], halo_list[0])

    def swap(x, k):
        return lax.ppermute(x, "dev", [(i, i ^ k) for i in range(peers)])

    def swap_groups(x, start):
        pairs = [(i, i + 1) for i in range(start, lax.axis_size("group") - 1, 2)]
        return lax.ppermute(x, "group", pairs + [(j, i) for i, j in pairs])

    from_near = swap(to_near, 1)
    from_far = [swap(x, k) for x, k in zip(to_far, range(4, peers))]
    from_second = swap_groups(to_second, 1)
    from_first = swap_groups(to_first, 0)
    by_part, near = lax.optimization_barrier((kernel_hat.transpose(1, 0, 2), from_near))
    relayed = swap(jnp.stack([to_two, near[1]]), 2)

    offsets = kernel_hat.shape[0]
    hat = pl.pallas_call(
        prepare_kernel,
        out_shape=jax.ShapeDtypeStruct((offsets * HAT_ROWS + 8, LANES), f32),
        in_specs=[vmem],
        out_specs=vmem,
        compiler_params=pltpu.CompilerParams(vmem_limit_bytes=16 * 1024 * 1024),
        cost_estimate=pl.CostEstimate(flops=kernel_hat.size, bytes_accessed=6 * kernel_hat.size, transcendentals=0),
        name="prepare",
    )(by_part)

    slots = box_count + peers * cap + 2 * rim
    row_count = comp_count * slots
    arrays = (
        send_list[0], inter_src, inter_off, density, from_near, relayed, *from_far, from_first, from_second,
        jnp.asarray(table), jnp.asarray(factor), hat,
    )
    potential = pl.pallas_call(
        translate_kernel,
        out_shape=jax.ShapeDtypeStruct((comp_count, box_count, surf), f32),
        in_specs=[smem] * 3 + [vmem] * (len(arrays) - 3),
        out_specs=vmem,
        scratch_shapes=[
            pltpu.VMEM((slots * source_rows(comp_count) + 8, LANES), f32),
            pltpu.VMEM((row_count, POINTS_PAD), f32),
            pltpu.VMEM((2 * comp_count * box_count * PITCH, LANES), f32),
            pltpu.VMEM((TAIL, (box_count + 2) * TAIL_PITCH, LANES), f32),
        ],
        compiler_params=pltpu.CompilerParams(vmem_limit_bytes=24 * 1024 * 1024),
        name="translate",
    )(*arrays)
    return potential.transpose(1, 0, 2)


def solution(mesh):
    in_specs = (
        P(("group", "dev"), None, None),
        P(),
        P(("group", "dev"), None, None),
        P(("group", "dev"), None, None),
        P(("group", "dev"), None),
        P(("group", "dev"), None),
    )
    out_specs = P(("group", "dev"), None, None)
    return jax.shard_map(
        on_device, mesh=mesh, in_specs=in_specs, out_specs=out_specs, check_vma=False
    )
```

```python
import functools
import math

import jax
import jax.numpy as jnp
import ml_dtypes
import numpy as np
from jax import lax
from jax.experimental import pallas as pl
from jax.experimental.pallas import tpu as pltpu
from jax.sharding import PartitionSpec as P

ORDER = 6
GRID = 16
LANES = 128
HALF = GRID // 2 + 1
FREQ = GRID * GRID * HALF
TILES = FREQ // LANES
MAIN = 16
TAIL = TILES - MAIN
PITCH = MAIN + 1
TAIL_PITCH = 7
HAT_ROWS = 3 * MAIN + 2 * TAIL + 1
POINTS_PAD = 160
CHUNK = 256
PIECE = 256
UNROLL = 8


def surface_points(edge_count):
    points = [
        (i, j, k)
        for i in range(edge_count)
        for j in range(edge_count)
        for k in range(edge_count)
        if min(i, j, k) == 0 or max(i, j, k) == edge_count - 1
    ]
    return np.array(points, dtype=np.int64)


@functools.lru_cache(maxsize=None)
def transform_tables():
    points = surface_points(ORDER)
    kx, ky, kz = (a.reshape(-1) for a in np.meshgrid(np.arange(GRID), np.arange(GRID), np.arange(HALF), indexing="ij"))
    phase = (points[:, :1] * kx + points[:, 1:2] * ky + points[:, 2:] * kz) % GRID
    angle = phase * (2.0 * math.pi / GRID)
    table = np.zeros((POINTS_PAD, 2 * FREQ), np.float64)
    table[: len(points), :FREQ] = np.cos(angle)
    table[: len(points), FREQ:] = -np.sin(angle)
    table = np.where(np.abs(table) < 1e-9, 0.0, table)
    high = table.astype(ml_dtypes.bfloat16)
    low = (table - high.astype(np.float64)).astype(ml_dtypes.bfloat16)
    edge_plane = (kz == 0) | (kz == GRID // 2)
    factor = np.where(edge_plane, 1.0, 2.0) / GRID**3 * np.where((kx + ky + kz) % 2 == 0, 1.0, -1.0)
    factor = np.concatenate([factor, factor]).astype(np.float32)[None, :]
    return np.concatenate([high, low], axis=0), factor


def source_rows(comp_count):
    return (3 * comp_count * MAIN + TAIL * 8) | 1


def source_row(comp_count, which, tile):
    if tile < MAIN:
        return which * MAIN + tile
    return 3 * comp_count * MAIN + (tile - MAIN) * 8 + which


def kernel_row(which, tile):
    return which * MAIN + tile if tile < MAIN else 3 * MAIN + (tile - MAIN) * 2 + which


def pack_kernel(density, send_list, halo_list, *outs):
    peers, cap = send_list.shape
    rim = halo_list.shape[1]
    member = lax.axis_index("dev")
    parity = lax.rem(lax.axis_index("group"), 2)
    to_near, *to_far, to_first, to_second = outs
    for c in range(density.shape[0]):
        for e in range(cap):
            for part, k in enumerate((1, 3)):
                to_near[part, c, e : e + 1, :] = density[c, pl.ds(send_list[member ^ k, e], 1), :]
            for k, out in zip((2, *range(4, peers)), to_far):
                out[c, e : e + 1, :] = density[c, pl.ds(send_list[member ^ k, e], 1), :]
        for e in range(rim):
            to_first[c, e : e + 1, :] = density[c, pl.ds(halo_list[1 - parity, e], 1), :]
            to_second[c, e : e + 1, :] = density[c, pl.ds(halo_list[parity, e], 1), :]


def prepare_kernel(kernel_hat, hat):
    parts, count, _ = kernel_hat.shape

    def move(first, height):
        for j in range(TILES):
            re, im = (
                kernel_hat[part, pl.ds(first, height), j * LANES : (j + 1) * LANES].astype(jnp.float32)
                for part in range(parts)
            )
            for which, x in enumerate((re, re + im, im - re) if j < MAIN else (re, im)):
                for g in range(0, height, 8):
                    size = min(8, height - g)
                    row = (first + g) * HAT_ROWS + kernel_row(which, j)
                    hat[pl.ds(row, size, stride=HAT_ROWS), :] = x[g : g + size]

    whole = count // 16

    @pl.loop(0, whole)
    def _(i):
        move(pl.multiple_of(i * 16, 16), 16)

    if count % 16:
        move(whole * 16, count % 16)


def forward_kernel(send_list, density, from_near, relayed, *refs):
    *from_far, from_first, from_second, table, main, rows = refs
    comp_count, box_count, surf = density.shape
    peers, cap = send_list.shape
    rim = from_first.shape[1]
    row_count = rows.shape[0]
    slots = row_count // comp_count
    pitch = source_rows(comp_count)
    f32, bf16 = jnp.float32, jnp.bfloat16

    member = lax.axis_index("dev")
    parity = lax.rem(lax.axis_index("group"), 2)
    rows[...] = jnp.zeros_like(rows)
    pieces = {1: from_near.at[0], 2: relayed.at[0], 3: relayed.at[1]}
    pieces.update(zip(range(4, peers), from_far))
    for c in range(comp_count):
        base = c * slots
        rows[base : base + box_count, :surf] = density[c]
        base += box_count
        for e in range(cap):
            rows[pl.ds(base + member * cap + e, 1), :surf] = density[c, pl.ds(send_list[member, e], 1), :]
            for k, piece in pieces.items():
                rows[pl.ds(base + (member ^ k) * cap + e, 1), :surf] = piece[c, e : e + 1]
        base += peers * cap
        for e in range(rim):
            rows[pl.ds(base + (1 - parity) * rim + e, 1), :surf] = from_first[c, e : e + 1]
            rows[pl.ds(base + parity * rim + e, 1), :surf] = from_second[c, e : e + 1]

    value = rows[...]
    high = value.astype(bf16)
    low = (value - high.astype(f32)).astype(bf16)
    both = jnp.concatenate([high, low], axis=0)

    def spectrum(first):
        columns = slice(first, first + CHUNK)
        x = jnp.dot(both, table[:POINTS_PAD, columns], preferred_element_type=f32)
        x = x[:row_count] + x[row_count:]
        x = x + jnp.dot(high, table[POINTS_PAD:, columns], preferred_element_type=f32)
        return x.astype(bf16).astype(f32)

    for n in range(FREQ // CHUNK):
        re, im = spectrum(n * CHUNK), spectrum(FREQ + n * CHUNK)
        for m in range(CHUNK // LANES):
            j = n * (CHUNK // LANES) + m
            for g in range(row_count // 8):
                at = (slice(g * 8, (g + 1) * 8), slice(m * LANES, (m + 1) * LANES))
                c, s = divmod(g * 8, slots)
                pieces = [re[at], im[at]]
                if j < MAIN:
                    pieces.append(pieces[0] + pieces[1])
                for part, piece in enumerate(pieces):
                    row = source_row(comp_count, part * comp_count + c, j)
                    main[pl.ds(s * pitch + row, 8, stride=pitch), :] = piece


def interact_kernel(comp_count, source, offset, hat, main, total, total_tail):
    box_count, list_count = source.shape
    pitch = source_rows(comp_count)
    f32 = jnp.float32
    plus = lax.broadcasted_iota(jnp.int32, (8, LANES), 0) < comp_count
    halves = MAIN // 8

    @pl.loop(0, box_count)
    def _(t):
        def rows_of(first):
            return tuple(
                (source[t, first + u] * pitch, offset[t, first + u] * HAT_ROWS) for u in range(UNROLL)
            )

        def pair(s, o, accs):
            k = [[hat[pl.ds(o + kernel_row(r, 8 * h), 8), :] for h in range(halves)] for r in range(3)]
            accs = list(accs)
            at = 0
            for c in range(comp_count):
                for h in range(halves):
                    s_re, s_im, s_sum = (
                        main[pl.ds(s + source_row(comp_count, r * comp_count + c, 8 * h), 8), :] for r in range(3)
                    )
                    accs[at] = accs[at] + k[0][h] * s_sum
                    accs[at + 1] = accs[at + 1] + k[1][h] * s_im
                    accs[at + 2] = accs[at + 2] + k[2][h] * s_re
                    at += 3
            k_tail = hat[pl.ds(o + kernel_row(0, MAIN), 8), :]
            for j in range(TAIL):
                x = main[pl.ds(s + source_row(comp_count, 0, MAIN + j), 8), :]
                for r in range(2):
                    row = 2 * j + r
                    accs[at + r] = accs[at + r] + jnp.broadcast_to(k_tail[row : row + 1], (8, LANES)) * x
                at += 2
            return tuple(accs)

        count = 3 * comp_count * halves + 2 * TAIL
        zero = jnp.zeros((8, LANES), f32)

        def block(i, carry):
            accs, here = carry
            ahead = rows_of(lax.rem((i + 1) * UNROLL, list_count))
            for s, o in here:
                accs = pair(s, o, accs)
            return accs, ahead

        accs, _ = lax.fori_loop(0, list_count // UNROLL, block, ((zero,) * count, rows_of(0)))
        at = 0
        for c in range(comp_count):
            for h in range(halves):
                for part, value in enumerate((accs[at] - accs[at + 1], accs[at] + accs[at + 2])):
                    row = (part * comp_count + c) * box_count + t
                    total[pl.ds(row * PITCH + 8 * h, 8), :] = value
                at += 3
        for j in range(TAIL):
            own, cross = accs[at], accs[at + 1]
            up = jnp.concatenate([cross[comp_count:], cross[:comp_count]], axis=0)
            down = jnp.concatenate([cross[-comp_count:], cross[:-comp_count]], axis=0)
            total_tail[j, pl.ds(t * TAIL_PITCH, 8), :] = jnp.where(plus, own - up, own + down)
            at += 2


def inverse_kernel(total, total_tail, table, factor, out):
    comp_count, box_count, surf = out.shape
    f32, bf16 = jnp.float32, jnp.bfloat16
    groups = box_count // 8
    count = comp_count * box_count
    nt = (((1,), (1,)), ((), ()))
    result = jnp.zeros((2 * POINTS_PAD, 2 * count), f32)
    for n in range(2 * FREQ // PIECE):
        lanes = []
        for m in range(PIECE // LANES):
            part, j = divmod(n * (PIECE // LANES) + m, TILES)
            pieces = []
            for c in range(comp_count):
                for g in range(groups):
                    if j < MAIN:
                        row = (part * comp_count + c) * box_count + g * 8
                        pieces.append(total[pl.ds(row * PITCH + j, 8, stride=PITCH), :])
                    else:
                        row = g * 8 * TAIL_PITCH + part * comp_count + c
                        pieces.append(total_tail[j - MAIN, pl.ds(row, 8, stride=TAIL_PITCH), :])
            lanes.append(jnp.concatenate(pieces, axis=0))
        columns = slice(n * PIECE, (n + 1) * PIECE)
        x = jnp.concatenate(lanes, axis=1) * factor[:, columns]
        high = x.astype(bf16)
        low = (x - high.astype(f32)).astype(bf16)
        both = jnp.concatenate([high, low], axis=0)
        result += lax.dot_general(table[:, columns], both, nt, preferred_element_type=f32)
    result = result[:POINTS_PAD, :count] + result[:POINTS_PAD, count:] + result[POINTS_PAD:, :count]
    result = result.T
    for c in range(comp_count):
        out[c] = result[c * box_count : (c + 1) * box_count, :surf]


def translate_kernel(send_list, source, offset, density, from_near, relayed, *refs):
    *pieces, table, factor, hat, out, main, rows, total, total_tail = refs
    forward_kernel(send_list, density, from_near, relayed, *pieces, table, main, rows)
    interact_kernel(density.shape[0], source, offset, hat, main, total, total_tail)
    inverse_kernel(total, total_tail, table, factor, out)


def on_device(density, kernel_hat, send_list, halo_list, inter_src, inter_off):
    table, factor = transform_tables()
    box_count, comp_count, surf = density.shape
    _, peers, cap = send_list.shape
    rim = halo_list.shape[2]
    f32 = jnp.float32
    vmem = pl.BlockSpec(memory_space=pltpu.VMEM)
    smem = pl.BlockSpec(memory_space=pltpu.SMEM)
    density = density.transpose(1, 0, 2)

    boxes = jax.ShapeDtypeStruct((comp_count, cap, surf), f32)
    side = jax.ShapeDtypeStruct((comp_count, rim, surf), f32)
    to_near, to_two, *to_far, to_first, to_second = pl.pallas_call(
        pack_kernel,
        out_shape=(jax.ShapeDtypeStruct((2, *boxes.shape), f32),) + (boxes,) * (peers - 3) + (side,) * 2,
        in_specs=[vmem, smem, smem],
        out_specs=(vmem,) * peers,
        name="pack",
    )(density, send_list[0], halo_list[0])

    def swap(x, k):
        return lax.ppermute(x, "dev", [(i, i ^ k) for i in range(peers)])

    def swap_groups(x, start):
        pairs = [(i, i + 1) for i in range(start, lax.axis_size("group") - 1, 2)]
        return lax.ppermute(x, "group", pairs + [(j, i) for i, j in pairs])

    from_near = swap(to_near, 1)
    from_far = [swap(x, k) for x, k in zip(to_far, range(4, peers))]
    from_first = swap_groups(to_first, 0)
    from_second = swap_groups(to_second, 1)
    by_part, near = lax.optimization_barrier((kernel_hat.transpose(1, 0, 2), from_near))
    relayed = swap(jnp.stack([to_two, near[1]]), 2)

    offsets = kernel_hat.shape[0]
    hat = pl.pallas_call(
        prepare_kernel,
        out_shape=jax.ShapeDtypeStruct((offsets * HAT_ROWS + 8, LANES), f32),
        in_specs=[vmem],
        out_specs=vmem,
        compiler_params=pltpu.CompilerParams(vmem_limit_bytes=16 * 1024 * 1024),
        cost_estimate=pl.CostEstimate(flops=kernel_hat.size, bytes_accessed=6 * kernel_hat.size, transcendentals=0),
        name="prepare",
    )(by_part)

    slots = box_count + peers * cap + 2 * rim
    row_count = comp_count * slots
    arrays = (
        send_list[0], inter_src, inter_off, density, from_near, relayed, *from_far, from_first, from_second,
        jnp.asarray(table), jnp.asarray(factor), hat,
    )
    potential = pl.pallas_call(
        translate_kernel,
        out_shape=jax.ShapeDtypeStruct((comp_count, box_count, surf), f32),
        in_specs=[smem] * 3 + [vmem] * (len(arrays) - 3),
        out_specs=vmem,
        scratch_shapes=[
            pltpu.VMEM((slots * source_rows(comp_count) + 8, LANES), f32),
            pltpu.VMEM((row_count, POINTS_PAD), f32),
            pltpu.VMEM((2 * comp_count * box_count * PITCH, LANES), f32),
            pltpu.VMEM((TAIL, (box_count + 2) * TAIL_PITCH, LANES), f32),
        ],
        compiler_params=pltpu.CompilerParams(vmem_limit_bytes=24 * 1024 * 1024),
        name="translate",
    )(*arrays)
    return potential.transpose(1, 0, 2)


def solution(mesh):
    in_specs = (
        P(("group", "dev"), None, None),
        P(),
        P(("group", "dev"), None, None),
        P(("group", "dev"), None, None),
        P(("group", "dev"), None),
        P(("group", "dev"), None),
    )
    out_specs = P(("group", "dev"), None, None)
    return jax.shard_map(
        on_device, mesh=mesh, in_specs=in_specs, out_specs=out_specs, check_vma=False
    )
```

```python
import functools
import math

import jax
import jax.numpy as jnp
import ml_dtypes
import numpy as np
from jax import lax
from jax.experimental import pallas as pl
from jax.experimental.pallas import tpu as pltpu
from jax.sharding import PartitionSpec as P

ORDER = 6
GRID = 16
LANES = 128
HALF = GRID // 2 + 1
FREQ = GRID * GRID * HALF
TILES = FREQ // LANES
MAIN = 16
TAIL = TILES - MAIN
PITCH = MAIN + 1
TAIL_PITCH = 7
HAT_ROWS = 3 * MAIN + 2 * TAIL + 1
POINTS_PAD = 160
CHUNK = 256
PIECE = 512
UNROLL = 8


def surface_points(edge_count):
    points = [
        (i, j, k)
        for i in range(edge_count)
        for j in range(edge_count)
        for k in range(edge_count)
        if min(i, j, k) == 0 or max(i, j, k) == edge_count - 1
    ]
    return np.array(points, dtype=np.int64)


@functools.lru_cache(maxsize=None)
def transform_tables():
    points = surface_points(ORDER)
    kx, ky, kz = (a.reshape(-1) for a in np.meshgrid(np.arange(GRID), np.arange(GRID), np.arange(HALF), indexing="ij"))
    phase = (points[:, :1] * kx + points[:, 1:2] * ky + points[:, 2:] * kz) % GRID
    angle = phase * (2.0 * math.pi / GRID)
    table = np.zeros((POINTS_PAD, 2 * FREQ), np.float64)
    table[: len(points), :FREQ] = np.cos(angle)
    table[: len(points), FREQ:] = -np.sin(angle)
    table = np.where(np.abs(table) < 1e-9, 0.0, table)
    high = table.astype(ml_dtypes.bfloat16)
    low = (table - high.astype(np.float64)).astype(ml_dtypes.bfloat16)
    edge_plane = (kz == 0) | (kz == GRID // 2)
    factor = np.where(edge_plane, 1.0, 2.0) / GRID**3 * np.where((kx + ky + kz) % 2 == 0, 1.0, -1.0)
    factor = np.concatenate([factor, factor]).astype(np.float32)[None, :]
    return np.concatenate([high, low], axis=0), factor


def source_rows(comp_count):
    return (3 * comp_count * MAIN + TAIL * 8) | 1


def source_row(comp_count, which, tile):
    if tile < MAIN:
        return which * MAIN + tile
    return 3 * comp_count * MAIN + (tile - MAIN) * 8 + which


def kernel_row(which, tile):
    return which * MAIN + tile if tile < MAIN else 3 * MAIN + (tile - MAIN) * 2 + which


def pack_kernel(density, send_list, halo_list, *outs):
    peers, cap = send_list.shape
    rim = halo_list.shape[1]
    member = lax.axis_index("dev")
    parity = lax.rem(lax.axis_index("group"), 2)
    to_near, *to_far, to_first, to_second = outs
    for c in range(density.shape[0]):
        for e in range(cap):
            for part, k in enumerate((1, 3)):
                to_near[part, c, e : e + 1, :] = density[c, pl.ds(send_list[member ^ k, e], 1), :]
            for k, out in zip((2, *range(4, peers)), to_far):
                out[c, e : e + 1, :] = density[c, pl.ds(send_list[member ^ k, e], 1), :]
        for e in range(rim):
            to_first[c, e : e + 1, :] = density[c, pl.ds(halo_list[1 - parity, e], 1), :]
            to_second[c, e : e + 1, :] = density[c, pl.ds(halo_list[parity, e], 1), :]


def prepare_kernel(kernel_hat, hat):
    parts, count, _ = kernel_hat.shape

    def move(first, height):
        for j in range(TILES):
            re, im = (
                kernel_hat[part, pl.ds(first, height), j * LANES : (j + 1) * LANES].astype(jnp.float32)
                for part in range(parts)
            )
            for which, x in enumerate((re, re + im, im - re) if j < MAIN else (re, im)):
                for g in range(0, height, 8):
                    size = min(8, height - g)
                    row = (first + g) * HAT_ROWS + kernel_row(which, j)
                    hat[pl.ds(row, size, stride=HAT_ROWS), :] = x[g : g + size]

    whole = count // 16

    @pl.loop(0, whole)
    def _(i):
        move(pl.multiple_of(i * 16, 16), 16)

    if count % 16:
        move(whole * 16, count % 16)


def forward_kernel(send_list, density, from_near, relayed, *refs):
    *from_far, from_first, from_second, table, main, rows = refs
    comp_count, box_count, surf = density.shape
    peers, cap = send_list.shape
    rim = from_first.shape[1]
    row_count = rows.shape[0]
    slots = row_count // comp_count
    pitch = source_rows(comp_count)
    f32, bf16 = jnp.float32, jnp.bfloat16

    member = lax.axis_index("dev")
    parity = lax.rem(lax.axis_index("group"), 2)
    rows[...] = jnp.zeros_like(rows)
    pieces = {1: from_near.at[0], 2: relayed.at[0], 3: relayed.at[1]}
    pieces.update(zip(range(4, peers), from_far))
    for c in range(comp_count):
        base = c * slots
        rows[base : base + box_count, :surf] = density[c]
        base += box_count
        for e in range(cap):
            rows[pl.ds(base + member * cap + e, 1), :surf] = density[c, pl.ds(send_list[member, e], 1), :]
            for k, piece in pieces.items():
                rows[pl.ds(base + (member ^ k) * cap + e, 1), :surf] = piece[c, e : e + 1]
        base += peers * cap
        for e in range(rim):
            rows[pl.ds(base + (1 - parity) * rim + e, 1), :surf] = from_first[c, e : e + 1]
            rows[pl.ds(base + parity * rim + e, 1), :surf] = from_second[c, e : e + 1]

    value = rows[...]
    high = value.astype(bf16)
    low = (value - high.astype(f32)).astype(bf16)
    both = jnp.concatenate([high, low], axis=0)

    def spectrum(first):
        columns = slice(first, first + CHUNK)
        x = jnp.dot(both, table[:POINTS_PAD, columns], preferred_element_type=f32)
        x = x[:row_count] + x[row_count:]
        x = x + jnp.dot(high, table[POINTS_PAD:, columns], preferred_element_type=f32)
        return x.astype(bf16).astype(f32)

    for n in range(FREQ // CHUNK):
        re, im = spectrum(n * CHUNK), spectrum(FREQ + n * CHUNK)
        for m in range(CHUNK // LANES):
            j = n * (CHUNK // LANES) + m
            for g in range(row_count // 8):
                at = (slice(g * 8, (g + 1) * 8), slice(m * LANES, (m + 1) * LANES))
                c, s = divmod(g * 8, slots)
                pieces = [re[at], im[at]]
                if j < MAIN:
                    pieces.append(pieces[0] + pieces[1])
                for part, piece in enumerate(pieces):
                    row = source_row(comp_count, part * comp_count + c, j)
                    main[pl.ds(s * pitch + row, 8, stride=pitch), :] = piece


def interact_kernel(comp_count, source, offset, hat, main, total, total_tail):
    box_count, list_count = source.shape
    pitch = source_rows(comp_count)
    f32 = jnp.float32
    plus = lax.broadcasted_iota(jnp.int32, (8, LANES), 0) < comp_count
    halves = MAIN // 8

    @pl.loop(0, box_count)
    def _(t):
        def rows_of(first):
            return tuple(
                (source[t, first + u] * pitch, offset[t, first + u] * HAT_ROWS) for u in range(UNROLL)
            )

        def pair(s, o, accs):
            k = [[hat[pl.ds(o + kernel_row(r, 8 * h), 8), :] for h in range(halves)] for r in range(3)]
            accs = list(accs)
            at = 0
            for c in range(comp_count):
                for h in range(halves):
                    s_re, s_im, s_sum = (
                        main[pl.ds(s + source_row(comp_count, r * comp_count + c, 8 * h), 8), :] for r in range(3)
                    )
                    accs[at] = accs[at] + k[0][h] * s_sum
                    accs[at + 1] = accs[at + 1] + k[1][h] * s_im
                    accs[at + 2] = accs[at + 2] + k[2][h] * s_re
                    at += 3
            k_tail = hat[pl.ds(o + kernel_row(0, MAIN), 8), :]
            for j in range(TAIL):
                x = main[pl.ds(s + source_row(comp_count, 0, MAIN + j), 8), :]
                for r in range(2):
                    row = 2 * j + r
                    accs[at + r] = accs[at + r] + jnp.broadcast_to(k_tail[row : row + 1], (8, LANES)) * x
                at += 2
            return tuple(accs)

        count = 3 * comp_count * halves + 2 * TAIL
        zero = jnp.zeros((8, LANES), f32)

        def block(i, carry):
            accs, here = carry
            ahead = rows_of(lax.rem((i + 1) * UNROLL, list_count))
            for s, o in here:
                accs = pair(s, o, accs)
            return accs, ahead

        accs, _ = lax.fori_loop(0, list_count // UNROLL, block, ((zero,) * count, rows_of(0)))
        at = 0
        for c in range(comp_count):
            for h in range(halves):
                for part, value in enumerate((accs[at] - accs[at + 1], accs[at] + accs[at + 2])):
                    row = (part * comp_count + c) * box_count + t
                    total[pl.ds(row * PITCH + 8 * h, 8), :] = value
                at += 3
        for j in range(TAIL):
            own, cross = accs[at], accs[at + 1]
            up = jnp.concatenate([cross[comp_count:], cross[:comp_count]], axis=0)
            down = jnp.concatenate([cross[-comp_count:], cross[:-comp_count]], axis=0)
            total_tail[j, pl.ds(t * TAIL_PITCH, 8), :] = jnp.where(plus, own - up, own + down)
            at += 2


def inverse_kernel(total, total_tail, table, factor, out):
    comp_count, box_count, surf = out.shape
    f32, bf16 = jnp.float32, jnp.bfloat16
    groups = box_count // 8
    count = comp_count * box_count
    nt = (((1,), (1,)), ((), ()))
    result = jnp.zeros((2 * POINTS_PAD, 2 * count), f32)
    for n in range(2 * FREQ // PIECE):
        lanes = []
        for m in range(PIECE // LANES):
            part, j = divmod(n * (PIECE // LANES) + m, TILES)
            pieces = []
            for c in range(comp_count):
                for g in range(groups):
                    if j < MAIN:
                        row = (part * comp_count + c) * box_count + g * 8
                        pieces.append(total[pl.ds(row * PITCH + j, 8, stride=PITCH), :])
                    else:
                        row = g * 8 * TAIL_PITCH + part * comp_count + c
                        pieces.append(total_tail[j - MAIN, pl.ds(row, 8, stride=TAIL_PITCH), :])
            lanes.append(jnp.concatenate(pieces, axis=0))
        columns = slice(n * PIECE, (n + 1) * PIECE)
        x = jnp.concatenate(lanes, axis=1) * factor[:, columns]
        high = x.astype(bf16)
        low = (x - high.astype(f32)).astype(bf16)
        both = jnp.concatenate([high, low], axis=0)
        result += lax.dot_general(table[:, columns], both, nt, preferred_element_type=f32)
    result = result[:POINTS_PAD, :count] + result[:POINTS_PAD, count:] + result[POINTS_PAD:, :count]
    result = result.T
    for c in range(comp_count):
        out[c] = result[c * box_count : (c + 1) * box_count, :surf]


def translate_kernel(send_list, source, offset, density, from_near, relayed, *refs):
    *pieces, table, factor, hat, out, main, rows, total, total_tail = refs
    forward_kernel(send_list, density, from_near, relayed, *pieces, table, main, rows)
    interact_kernel(density.shape[0], source, offset, hat, main, total, total_tail)
    inverse_kernel(total, total_tail, table, factor, out)


def on_device(density, kernel_hat, send_list, halo_list, inter_src, inter_off):
    table, factor = transform_tables()
    box_count, comp_count, surf = density.shape
    _, peers, cap = send_list.shape
    rim = halo_list.shape[2]
    f32 = jnp.float32
    vmem = pl.BlockSpec(memory_space=pltpu.VMEM)
    smem = pl.BlockSpec(memory_space=pltpu.SMEM)
    density = density.transpose(1, 0, 2)

    boxes = jax.ShapeDtypeStruct((comp_count, cap, surf), f32)
    side = jax.ShapeDtypeStruct((comp_count, rim, surf), f32)
    to_near, to_two, *to_far, to_first, to_second = pl.pallas_call(
        pack_kernel,
        out_shape=(jax.ShapeDtypeStruct((2, *boxes.shape), f32),) + (boxes,) * (peers - 3) + (side,) * 2,
        in_specs=[vmem, smem, smem],
        out_specs=(vmem,) * peers,
        name="pack",
    )(density, send_list[0], halo_list[0])

    def swap(x, k):
        return lax.ppermute(x, "dev", [(i, i ^ k) for i in range(peers)])

    def swap_groups(x, start):
        pairs = [(i, i + 1) for i in range(start, lax.axis_size("group") - 1, 2)]
        return lax.ppermute(x, "group", pairs + [(j, i) for i, j in pairs])

    from_near = swap(to_near, 1)
    from_far = [swap(x, k) for x, k in zip(to_far, range(4, peers))]
    from_first = swap_groups(to_first, 0)
    from_second = swap_groups(to_second, 1)
    by_part, near = lax.optimization_barrier((kernel_hat.transpose(1, 0, 2), from_near))
    relayed = swap(jnp.stack([to_two, near[1]]), 2)

    offsets = kernel_hat.shape[0]
    hat = pl.pallas_call(
        prepare_kernel,
        out_shape=jax.ShapeDtypeStruct((offsets * HAT_ROWS + 8, LANES), f32),
        in_specs=[vmem],
        out_specs=vmem,
        compiler_params=pltpu.CompilerParams(vmem_limit_bytes=13 * 1024 * 1024),
        cost_estimate=pl.CostEstimate(flops=kernel_hat.size, bytes_accessed=6 * kernel_hat.size, transcendentals=0),
        name="prepare",
    )(by_part)

    slots = box_count + peers * cap + 2 * rim
    row_count = comp_count * slots
    arrays = (
        send_list[0], inter_src, inter_off, density, from_near, relayed, *from_far, from_first, from_second,
        jnp.asarray(table), jnp.asarray(factor), hat,
    )
    potential = pl.pallas_call(
        translate_kernel,
        out_shape=jax.ShapeDtypeStruct((comp_count, box_count, surf), f32),
        in_specs=[smem] * 3 + [vmem] * (len(arrays) - 3),
        out_specs=vmem,
        scratch_shapes=[
            pltpu.VMEM((slots * source_rows(comp_count) + 8, LANES), f32),
            pltpu.VMEM((row_count, POINTS_PAD), f32),
            pltpu.VMEM((2 * comp_count * box_count * PITCH, LANES), f32),
            pltpu.VMEM((TAIL, (box_count + 2) * TAIL_PITCH, LANES), f32),
        ],
        compiler_params=pltpu.CompilerParams(vmem_limit_bytes=14 * 1024 * 1024),
        name="translate",
    )(*arrays)
    return potential.transpose(1, 0, 2)


def solution(mesh):
    in_specs = (
        P(("group", "dev"), None, None),
        P(),
        P(("group", "dev"), None, None),
        P(("group", "dev"), None, None),
        P(("group", "dev"), None),
        P(("group", "dev"), None),
    )
    out_specs = P(("group", "dev"), None, None)
    return jax.shard_map(
        on_device, mesh=mesh, in_specs=in_specs, out_specs=out_specs, check_vma=False
    )
```

```python
import functools
import math

import jax
import jax.numpy as jnp
import ml_dtypes
import numpy as np
from jax import lax
from jax.experimental import pallas as pl
from jax.experimental.pallas import tpu as pltpu
from jax.sharding import PartitionSpec as P

ORDER = 6
GRID = 16
LANES = 128
HALF = GRID // 2 + 1
FREQ = GRID * GRID * HALF
TILES = FREQ // LANES
MAIN = 16
TAIL = TILES - MAIN
PITCH = MAIN + 1
TAIL_PITCH = 7
HAT_ROWS = 3 * MAIN + 2 * TAIL + 1
POINTS_PAD = 160
CHUNK = 128
PIECE = 512
UNROLL = 8


def surface_points(edge_count):
    points = [
        (i, j, k)
        for i in range(edge_count)
        for j in range(edge_count)
        for k in range(edge_count)
        if min(i, j, k) == 0 or max(i, j, k) == edge_count - 1
    ]
    return np.array(points, dtype=np.int64)


@functools.lru_cache(maxsize=None)
def transform_tables():
    points = surface_points(ORDER)
    kx, ky, kz = (a.reshape(-1) for a in np.meshgrid(np.arange(GRID), np.arange(GRID), np.arange(HALF), indexing="ij"))
    phase = (points[:, :1] * kx + points[:, 1:2] * ky + points[:, 2:] * kz) % GRID
    angle = phase * (2.0 * math.pi / GRID)
    table = np.zeros((POINTS_PAD, 2 * FREQ), np.float64)
    table[: len(points), :FREQ] = np.cos(angle)
    table[: len(points), FREQ:] = -np.sin(angle)
    table = np.where(np.abs(table) < 1e-9, 0.0, table)
    high = table.astype(ml_dtypes.bfloat16)
    low = (table - high.astype(np.float64)).astype(ml_dtypes.bfloat16)
    edge_plane = (kz == 0) | (kz == GRID // 2)
    factor = np.where(edge_plane, 1.0, 2.0) / GRID**3 * np.where((kx + ky + kz) % 2 == 0, 1.0, -1.0)
    factor = np.concatenate([factor, factor]).astype(np.float32)[None, :]
    return np.concatenate([high, low], axis=0), factor


def source_rows(comp_count):
    return (3 * comp_count * MAIN + TAIL * 8) | 1


def source_row(comp_count, which, tile):
    if tile < MAIN:
        return which * MAIN + tile
    return 3 * comp_count * MAIN + (tile - MAIN) * 8 + which


def kernel_row(which, tile):
    return which * MAIN + tile if tile < MAIN else 3 * MAIN + (tile - MAIN) * 2 + which


def pack_kernel(density, send_list, halo_list, *outs):
    peers, cap = send_list.shape
    rim = halo_list.shape[1]
    member = lax.axis_index("dev")
    parity = lax.rem(lax.axis_index("group"), 2)
    to_near, *to_far, to_first, to_second = outs
    for c in range(density.shape[0]):
        for e in range(cap):
            for part, k in enumerate((1, 3)):
                to_near[part, c, e : e + 1, :] = density[c, pl.ds(send_list[member ^ k, e], 1), :]
            for k, out in zip((2, *range(4, peers)), to_far):
                out[c, e : e + 1, :] = density[c, pl.ds(send_list[member ^ k, e], 1), :]
        for e in range(rim):
            to_first[c, e : e + 1, :] = density[c, pl.ds(halo_list[1 - parity, e], 1), :]
            to_second[c, e : e + 1, :] = density[c, pl.ds(halo_list[parity, e], 1), :]


def prepare_kernel(kernel_hat, hat):
    parts, count, _ = kernel_hat.shape

    def move(first, height):
        for j in range(TILES):
            re, im = (
                kernel_hat[part, pl.ds(first, height), j * LANES : (j + 1) * LANES].astype(jnp.float32)
                for part in range(parts)
            )
            for which, x in enumerate((re, re + im, im - re) if j < MAIN else (re, im)):
                for g in range(0, height, 8):
                    size = min(8, height - g)
                    row = (first + g) * HAT_ROWS + kernel_row(which, j)
                    hat[pl.ds(row, size, stride=HAT_ROWS), :] = x[g : g + size]

    whole = count // 16

    @pl.loop(0, whole)
    def _(i):
        move(pl.multiple_of(i * 16, 16), 16)

    if count % 16:
        move(whole * 16, count % 16)


def forward_kernel(send_list, density, from_near, relayed, *refs):
    *from_far, from_first, from_second, table, main, rows = refs
    comp_count, box_count, surf = density.shape
    peers, cap = send_list.shape
    rim = from_first.shape[1]
    row_count = rows.shape[0]
    slots = row_count // comp_count
    pitch = source_rows(comp_count)
    f32, bf16 = jnp.float32, jnp.bfloat16

    member = lax.axis_index("dev")
    parity = lax.rem(lax.axis_index("group"), 2)
    rows[...] = jnp.zeros_like(rows)
    pieces = {1: from_near.at[0], 2: relayed.at[0], 3: relayed.at[1]}
    pieces.update(zip(range(4, peers), from_far))
    for c in range(comp_count):
        base = c * slots
        rows[base : base + box_count, :surf] = density[c]
        base += box_count
        for e in range(cap):
            rows[pl.ds(base + member * cap + e, 1), :surf] = density[c, pl.ds(send_list[member, e], 1), :]
            for k, piece in pieces.items():
                rows[pl.ds(base + (member ^ k) * cap + e, 1), :surf] = piece[c, e : e + 1]
        base += peers * cap
        for e in range(rim):
            rows[pl.ds(base + (1 - parity) * rim + e, 1), :surf] = from_first[c, e : e + 1]
            rows[pl.ds(base + parity * rim + e, 1), :surf] = from_second[c, e : e + 1]

    value = rows[...]
    high = value.astype(bf16)
    low = (value - high.astype(f32)).astype(bf16)
    both = jnp.concatenate([high, low], axis=0)

    def spectrum(first):
        columns = slice(first, first + CHUNK)
        x = jnp.dot(both, table[:POINTS_PAD, columns], preferred_element_type=f32)
        x = x[:row_count] + x[row_count:]
        x = x + jnp.dot(high, table[POINTS_PAD:, columns], preferred_element_type=f32)
        return x.astype(bf16).astype(f32)

    for n in range(FREQ // CHUNK):
        re, im = spectrum(n * CHUNK), spectrum(FREQ + n * CHUNK)
        for m in range(CHUNK // LANES):
            j = n * (CHUNK // LANES) + m
            for g in range(row_count // 8):
                at = (slice(g * 8, (g + 1) * 8), slice(m * LANES, (m + 1) * LANES))
                c, s = divmod(g * 8, slots)
                pieces = [re[at], im[at]]
                if j < MAIN:
                    pieces.append(pieces[0] + pieces[1])
                for part, piece in enumerate(pieces):
                    row = source_row(comp_count, part * comp_count + c, j)
                    main[pl.ds(s * pitch + row, 8, stride=pitch), :] = piece


def interact_kernel(comp_count, source, offset, hat, main, total, total_tail):
    box_count, list_count = source.shape
    pitch = source_rows(comp_count)
    f32 = jnp.float32
    plus = lax.broadcasted_iota(jnp.int32, (8, LANES), 0) < comp_count
    halves = MAIN // 8

    @pl.loop(0, box_count)
    def _(t):
        def rows_of(first):
            return tuple(
                (source[t, first + u] * pitch, offset[t, first + u] * HAT_ROWS) for u in range(UNROLL)
            )

        def pair(s, o, accs):
            k = [[hat[pl.ds(o + kernel_row(r, 8 * h), 8), :] for h in range(halves)] for r in range(3)]
            accs = list(accs)
            at = 0
            for c in range(comp_count):
                for h in range(halves):
                    s_re, s_im, s_sum = (
                        main[pl.ds(s + source_row(comp_count, r * comp_count + c, 8 * h), 8), :] for r in range(3)
                    )
                    accs[at] = accs[at] + k[0][h] * s_sum
                    accs[at + 1] = accs[at + 1] + k[1][h] * s_im
                    accs[at + 2] = accs[at + 2] + k[2][h] * s_re
                    at += 3
            k_tail = hat[pl.ds(o + kernel_row(0, MAIN), 8), :]
            for j in range(TAIL):
                x = main[pl.ds(s + source_row(comp_count, 0, MAIN + j), 8), :]
                for r in range(2):
                    row = 2 * j + r
                    accs[at + r] = accs[at + r] + jnp.broadcast_to(k_tail[row : row + 1], (8, LANES)) * x
                at += 2
            return tuple(accs)

        count = 3 * comp_count * halves + 2 * TAIL
        zero = jnp.zeros((8, LANES), f32)

        def block(i, carry):
            accs, here = carry
            ahead = rows_of(lax.rem((i + 1) * UNROLL, list_count))
            for s, o in here:
                accs = pair(s, o, accs)
            return accs, ahead

        accs, _ = lax.fori_loop(0, list_count // UNROLL, block, ((zero,) * count, rows_of(0)))
        at = 0
        for c in range(comp_count):
            for h in range(halves):
                for part, value in enumerate((accs[at] - accs[at + 1], accs[at] + accs[at + 2])):
                    row = (part * comp_count + c) * box_count + t
                    total[pl.ds(row * PITCH + 8 * h, 8), :] = value
                at += 3
        for j in range(TAIL):
            own, cross = accs[at], accs[at + 1]
            up = jnp.concatenate([cross[comp_count:], cross[:comp_count]], axis=0)
            down = jnp.concatenate([cross[-comp_count:], cross[:-comp_count]], axis=0)
            total_tail[j, pl.ds(t * TAIL_PITCH, 8), :] = jnp.where(plus, own - up, own + down)
            at += 2


def inverse_kernel(total, total_tail, table, factor, out):
    comp_count, box_count, surf = out.shape
    f32, bf16 = jnp.float32, jnp.bfloat16
    groups = box_count // 8
    count = comp_count * box_count
    nt = (((1,), (1,)), ((), ()))
    result = jnp.zeros((2 * POINTS_PAD, 2 * count), f32)
    for n in range(2 * FREQ // PIECE):
        lanes = []
        for m in range(PIECE // LANES):
            part, j = divmod(n * (PIECE // LANES) + m, TILES)
            pieces = []
            for c in range(comp_count):
                for g in range(groups):
                    if j < MAIN:
                        row = (part * comp_count + c) * box_count + g * 8
                        pieces.append(total[pl.ds(row * PITCH + j, 8, stride=PITCH), :])
                    else:
                        row = g * 8 * TAIL_PITCH + part * comp_count + c
                        pieces.append(total_tail[j - MAIN, pl.ds(row, 8, stride=TAIL_PITCH), :])
            lanes.append(jnp.concatenate(pieces, axis=0))
        columns = slice(n * PIECE, (n + 1) * PIECE)
        x = jnp.concatenate(lanes, axis=1) * factor[:, columns]
        high = x.astype(bf16)
        low = (x - high.astype(f32)).astype(bf16)
        both = jnp.concatenate([high, low], axis=0)
        result += lax.dot_general(table[:, columns], both, nt, preferred_element_type=f32)
    result = result[:POINTS_PAD, :count] + result[:POINTS_PAD, count:] + result[POINTS_PAD:, :count]
    result = result.T
    for c in range(comp_count):
        out[c] = result[c * box_count : (c + 1) * box_count, :surf]


def translate_kernel(send_list, source, offset, density, from_near, relayed, *refs):
    *pieces, table, factor, hat, out, main, rows, total, total_tail = refs
    forward_kernel(send_list, density, from_near, relayed, *pieces, table, main, rows)
    interact_kernel(density.shape[0], source, offset, hat, main, total, total_tail)
    inverse_kernel(total, total_tail, table, factor, out)


def on_device(density, kernel_hat, send_list, halo_list, inter_src, inter_off):
    table, factor = transform_tables()
    box_count, comp_count, surf = density.shape
    _, peers, cap = send_list.shape
    rim = halo_list.shape[2]
    f32 = jnp.float32
    vmem = pl.BlockSpec(memory_space=pltpu.VMEM)
    smem = pl.BlockSpec(memory_space=pltpu.SMEM)
    density = density.transpose(1, 0, 2)

    boxes = jax.ShapeDtypeStruct((comp_count, cap, surf), f32)
    side = jax.ShapeDtypeStruct((comp_count, rim, surf), f32)
    to_near, to_two, *to_far, to_first, to_second = pl.pallas_call(
        pack_kernel,
        out_shape=(jax.ShapeDtypeStruct((2, *boxes.shape), f32),) + (boxes,) * (peers - 3) + (side,) * 2,
        in_specs=[vmem, smem, smem],
        out_specs=(vmem,) * peers,
        name="pack",
    )(density, send_list[0], halo_list[0])

    def swap(x, k):
        return lax.ppermute(x, "dev", [(i, i ^ k) for i in range(peers)])

    def swap_groups(x, start):
        pairs = [(i, i + 1) for i in range(start, lax.axis_size("group") - 1, 2)]
        return lax.ppermute(x, "group", pairs + [(j, i) for i, j in pairs])

    from_near = swap(to_near, 1)
    from_far = [swap(x, k) for x, k in zip(to_far, range(4, peers))]
    from_first = swap_groups(to_first, 0)
    from_second = swap_groups(to_second, 1)
    by_part, near = lax.optimization_barrier((kernel_hat.transpose(1, 0, 2), from_near))
    relayed = swap(jnp.stack([to_two, near[1]]), 2)

    offsets = kernel_hat.shape[0]
    hat = pl.pallas_call(
        prepare_kernel,
        out_shape=jax.ShapeDtypeStruct((offsets * HAT_ROWS + 8, LANES), f32),
        in_specs=[vmem],
        out_specs=vmem,
        compiler_params=pltpu.CompilerParams(vmem_limit_bytes=16 * 1024 * 1024),
        cost_estimate=pl.CostEstimate(flops=kernel_hat.size, bytes_accessed=6 * kernel_hat.size, transcendentals=0),
        name="prepare",
    )(by_part)

    slots = box_count + peers * cap + 2 * rim
    row_count = comp_count * slots
    arrays = (
        send_list[0], inter_src, inter_off, density, from_near, relayed, *from_far, from_first, from_second,
        jnp.asarray(table), jnp.asarray(factor), hat,
    )
    potential = pl.pallas_call(
        translate_kernel,
        out_shape=jax.ShapeDtypeStruct((comp_count, box_count, surf), f32),
        in_specs=[smem] * 3 + [vmem] * (len(arrays) - 3),
        out_specs=vmem,
        scratch_shapes=[
            pltpu.VMEM((slots * source_rows(comp_count) + 8, LANES), f32),
            pltpu.VMEM((row_count, POINTS_PAD), f32),
            pltpu.VMEM((2 * comp_count * box_count * PITCH, LANES), f32),
            pltpu.VMEM((TAIL, (box_count + 2) * TAIL_PITCH, LANES), f32),
        ],
        compiler_params=pltpu.CompilerParams(vmem_limit_bytes=24 * 1024 * 1024),
        name="translate",
    )(*arrays)
    return potential.transpose(1, 0, 2)


def solution(mesh):
    in_specs = (
        P(("group", "dev"), None, None),
        P(),
        P(("group", "dev"), None, None),
        P(("group", "dev"), None, None),
        P(("group", "dev"), None),
        P(("group", "dev"), None),
    )
    out_specs = P(("group", "dev"), None, None)
    return jax.shard_map(
        on_device, mesh=mesh, in_specs=in_specs, out_specs=out_specs, check_vma=False
    )
```
